128 devices in a mesh: dp: 8 (over y, core), tensor: 16 (over z, x).
Axes of the slice: x: 4, y: 4, z: 4, core: 2. Of those that a mesh axis runs over, the one named last changes fastest.
Arguments:
- x_rows: bfloat16 [16384, 8192], P(('dp', 'tensor')), may hold values from -30 to 30
- d_attn: bfloat16 [16384, 4096], P('dp', 'tensor'), may hold values from -36 to 36
- q_saved: bfloat16 [16384, 4096], P('dp', 'tensor'), may hold values from -60 to 60
- k_saved: bfloat16 [16384, 2048], P('dp', 'tensor'), may hold values from -5 to 5, as said below
- v_saved: bfloat16 [16384, 2048], P('dp', 'tensor'), may hold values from -5 to 5, as said below
- w_query: bfloat16 [8192, 4096], P(None, 'tensor'), may hold values from -0.0625 to 0.0625
- w_key: bfloat16 [8192, 2048], P(None, 'tensor'), may hold values from -0.055242717 to 0.055242717, as said below
- w_value: bfloat16 [8192, 2048], P(None, 'tensor'), may hold values from -0.055242717 to 0.055242717, as said below
- down_all: bfloat16 [4, 48, 8192], replicated, may hold values from -0.0625 to 0.0625
- up_query: bfloat16 [4, 16, 4096], P(None, None, 'tensor'), may hold values from -0.09375 to 0.09375
- up_kv: bfloat16 [4, 32, 2048], P(None, None, 'tensor'), may hold values from -0.15625 to 0.15625, as said below
- tenant: int32 [16], P('dp'), may hold values from 0 to 3
- doc_starts: int32 [16, 4], P('dp'), may hold values from 0 to 1023, as said below
Outputs:
- d_rows: bfloat16 [16384, 8192], P(('dp', 'tensor'))
- upd_down: float32 [4, 48, 8192], P(None, None, 'tensor')
- upd_query: float32 [4, 16, 4096], P(None, None, 'tensor')
- upd_kv: float32 [4, 32, 2048], P(None, None, 'tensor')
The draws below stay inside these ranges and needn't reach their ends.
Inputs may be any that keep to these rules, and one draw needn't show every extreme that they name: `k_saved`: column block b of 128 holds key head floor(b / 2); the 2 blocks of a head are equal. `v_saved`: column block b of 128 holds value head floor(b / 2); the 2 blocks of a head are equal. `w_key`: column block b of 128 belongs to key head floor(b / 2); the 2 blocks of a head are equal. `w_value`: column block b of 128 belongs to value head floor(b / 2); the 2 blocks of a head are equal. `up_kv`: column block b of 128 belongs to head floor(b / 2); the 2 blocks of a head are equal. `doc_starts`: each row lists the first positions of exactly 4 documents of its sequence: it begins with 0 and rises strictly. In the first sequence the last document is its last token alone.
All inputs are finite; a program needn't handle non-finite values.
Results may differ from the reference program's by a relative error of at most 0.02.
Values may be sent and summed in bfloat16 or wider, within the bound.
A program may use at most 384 MiB of HBM per device.

```python
import math
import jax
import jax.numpy as jnp
from jax import lax

D = 8192
HQ = 32
KVH = 8
HD = 128
ADAPTER_RANK = 16
TEN = 4
SEQ = 1024
DOCS = 4
SEQS = 16
TOKENS = 16384
KV_REP = 2
KVCOLS = 2048
N_TENSOR = 16


def feature_scales(key, count, spread):
    rough = jax.random.uniform(key, (count,), jnp.float32)
    ramp = jnp.sqrt(1.0 + 2.0 * jnp.arange(count, dtype=jnp.float32) / max(count - 1, 1))
    return jnp.exp(rough * math.log(spread)) * ramp


def truncated(key, shape):
    return jax.random.truncated_normal(key, -5.0, 5.0, shape, jnp.float32)


def draw_x_rows(key, part):
    key = jax.random.fold_in(key, 11)
    scales = feature_scales(jax.random.fold_in(key, 1), D, 10.0) * 0.25
    return (truncated(jax.random.fold_in(key, 2), (TOKENS, D)) * scales[None, :]).astype(jnp.bfloat16)


def draw_d_attn(key, part):
    key = jax.random.fold_in(key, 13)
    scales = feature_scales(jax.random.fold_in(key, 1), HQ * HD, 10.0) * 0.3
    return (truncated(jax.random.fold_in(key, 2), (TOKENS, HQ * HD)) * scales[None, :]).astype(jnp.bfloat16)


def draw_k_saved(key, part):
    key = jax.random.fold_in(key, 31)
    keys = truncated(jax.random.fold_in(key, 1), (TOKENS, KVH, HD))
    return jnp.repeat(keys, KV_REP, axis=1).reshape(TOKENS, KVCOLS).astype(jnp.bfloat16)


def draw_q_saved(key, part):
    key = jax.random.fold_in(key, 23)
    query = truncated(jax.random.fold_in(key, 5), (TOKENS, HQ, HD))
    return query.reshape(TOKENS, HQ * HD).astype(jnp.bfloat16)


def draw_v_saved(key, part):
    key = jax.random.fold_in(key, 37)
    values = truncated(key, (TOKENS, KVH, HD))
    return jnp.repeat(values, KV_REP, axis=1).reshape(TOKENS, KVCOLS).astype(jnp.bfloat16)


def draw_w_key(key, part):
    key = jax.random.fold_in(key, 17)
    weights = truncated(key, (D, KVH, HD)) * D ** (-0.5)
    return jnp.repeat(weights, KV_REP, axis=1).reshape(D, KVCOLS).astype(jnp.bfloat16)


def draw_w_value(key, part):
    key = jax.random.fold_in(key, 19)
    weights = truncated(key, (D, KVH, HD)) * D ** (-0.5)
    return jnp.repeat(weights, KV_REP, axis=1).reshape(D, KVCOLS).astype(jnp.bfloat16)


def draw_up_kv(key, part):
    key = jax.random.fold_in(key, 29)
    weights = truncated(key, (TEN, 2 * ADAPTER_RANK, KVH, HD)) * (KVH * HD) ** (-0.5)
    return jnp.repeat(weights, KV_REP, axis=2).reshape(TEN, 2 * ADAPTER_RANK, KVCOLS).astype(jnp.bfloat16)


def draw_doc_starts(key, part):
    key = jax.random.fold_in(key, 41)
    keys = jax.random.split(key, SEQS)

    def one_row(row_key):
        cuts = jax.random.permutation(row_key, SEQ - 2)[:DOCS - 1].astype(jnp.int32) + 1
        return jnp.concatenate([jnp.zeros((1,), jnp.int32), jnp.sort(cuts)])
    table = jax.vmap(one_row)(keys)
    row_ids = jnp.arange(SEQS, dtype=jnp.int32)[:, None]
    col_ids = jnp.arange(DOCS, dtype=jnp.int32)[None, :]
    last_one = (row_ids == 0) & (col_ids == DOCS - 1)
    return jnp.where(last_one, jnp.full_like(table, SEQ - 1), table)


def set_ends(drawn, own_key, least, top_value):
    extent = drawn.shape
    spot = [jax.random.randint(jax.random.fold_in(own_key, axis), (), 0, extent[axis]) for axis in range(len(extent))]
    drawn = drawn.at[tuple(spot)].set(least)
    longest = extent.index(max(extent))
    spot[longest] = (spot[longest] + 1) % extent[longest]
    return drawn.at[tuple(spot)].set(top_value)


def steps_of(own_key, dims, cuts, smallest, top_value):
    level = 1.0
    for position, shards_of in cuts:
        heights = jax.random.uniform(jax.random.fold_in(jax.random.fold_in(own_key, 6), position), (shards_of,), jnp.float32, smallest / len(cuts), top_value / len(cuts))
        level = level * jnp.repeat(jnp.exp(heights), dims[position] // shards_of).reshape((-1,) + (1,) * (len(dims) - 1 - position))
    return level


def centred(key, shape, scale, most, pieces=(), held_as=jnp.bfloat16):
    result = jax.random.normal(key, shape, jnp.float32) * scale
    if len(pieces) > 0:
        result = steps_of(key, shape, pieces, -0.22, 0.18) * result
    return jnp.clip(result, min=-most, max=most).astype(held_as)


def setup_inputs(seed: int = 0) -> dict:
    key_list = jax.random.split(jax.random.key(seed), 14)
    return {
        "x_rows": draw_x_rows(jax.random.fold_in(key_list[13], 71), 0),
        "d_attn": draw_d_attn(jax.random.fold_in(key_list[13], 71), 0),
        "q_saved": draw_q_saved(jax.random.fold_in(key_list[13], 71), 0),
        "k_saved": draw_k_saved(jax.random.fold_in(key_list[13], 71), 0),
        "v_saved": draw_v_saved(jax.random.fold_in(key_list[13], 71), 0),
        "w_query": centred(key_list[5], (D, HQ * HD), D ** -0.5, 0.0625, ((1, 16),)),
        "w_key": draw_w_key(jax.random.fold_in(key_list[13], 71), 0),
        "w_value": draw_w_value(jax.random.fold_in(key_list[13], 71), 0),
        "down_all": centred(key_list[8], (TEN, 3 * ADAPTER_RANK, D), D ** -0.5, 0.0625),
        "up_query": centred(key_list[9], (TEN, ADAPTER_RANK, HQ * HD), (HQ * HD) ** -0.5, 0.09375, ((2, 16),)),
        "up_kv": draw_up_kv(jax.random.fold_in(key_list[13], 71), 0),
        "tenant": set_ends(jax.random.randint(key_list[11], (SEQS,), 0, TEN), jax.random.fold_in(key_list[11], 1), 0, TEN - 1).astype(jnp.int32),
        "doc_starts": draw_doc_starts(jax.random.fold_in(key_list[13], 71), 0),
    }


ADAPTER_SCALING = 2.0
ROPE_BASE = 500000.0
NORM_EPS = 1e-06
MASKED = -1e+30

def doc_layout(starts):
    where_pos = jnp.arange(SEQ, dtype=jnp.int32)
    inside = starts[None, :] <= where_pos[:, None]
    doc_index = lax.optimization_barrier(jnp.sum(inside.astype(jnp.int32), axis=1))
    begin = lax.optimization_barrier(jnp.max(jnp.where(inside, starts[None, :], jnp.zeros_like(starts)[None, :]), axis=1))
    offset = (where_pos - begin).astype(jnp.float32)
    allowed = (doc_index[:, None] == doc_index[None, :]) & (where_pos[None, :] <= where_pos[:, None])
    return (offset, allowed)

def rotary_tables(offset, width):
    half = width // 2
    freq = ROPE_BASE ** (-(2.0 * jnp.arange(half, dtype=jnp.float32)) / width)
    angle = offset[..., None] * freq
    return (jnp.cos(angle), jnp.sin(angle))

def unrotate(grad, cosine, sine):
    half = grad.shape[-1] // 2
    first = grad[..., :half]
    second = grad[..., half:]
    return jnp.concatenate([first * cosine + second * sine, second * cosine - first * sine], axis=-1)

def attention_back(query, key_rows, value_rows, grad_out, allowed, cosine, sine):
    qf = query.astype(jnp.float32)
    kf = key_rows.astype(jnp.float32)
    vf = value_rows.astype(jnp.float32)
    gf = grad_out.astype(jnp.float32)
    scale = HD ** (-0.5)
    scores = jnp.einsum('pghd,kgd->ghpk', qf, kf) * scale
    scores = jnp.where(allowed, scores, MASKED)
    top = lax.optimization_barrier(jnp.max(scores, axis=-1, keepdims=True))
    expd = jnp.exp(scores - top)
    probs = expd / lax.optimization_barrier(jnp.sum(expd, axis=-1, keepdims=True))
    probs_low = lax.optimization_barrier(probs.astype(jnp.bfloat16)).astype(jnp.float32)
    output = jnp.einsum('ghpk,kgd->pghd', probs_low, vf)
    delta = lax.optimization_barrier(jnp.sum(gf * output, axis=-1))
    dprob = jnp.einsum('pghd,kgd->ghpk', gf, vf)
    dscore = probs * (dprob - jnp.transpose(delta, (1, 2, 0))[..., None])
    dscore_low = lax.optimization_barrier(dscore.astype(jnp.bfloat16)).astype(jnp.float32)
    dquery = jnp.einsum('ghpk,kgd->pghd', dscore_low, kf) * scale
    dkey = jnp.einsum('ghpk,pghd->kgd', dscore_low, qf) * scale
    dvalue = jnp.einsum('ghpk,pghd->kgd', probs_low, gf)
    dquery = unrotate(dquery, cosine[:, None, None, :], sine[:, None, None, :])
    dkey = unrotate(dkey, cosine[:, None, :], sine[:, None, :])
    return (dquery.astype(jnp.bfloat16), dkey.astype(jnp.bfloat16), dvalue.astype(jnp.bfloat16))

def normalized(grad, blocks):
    shaped = grad.reshape(TEN, blocks, -1)
    mean = lax.optimization_barrier(jnp.mean(shaped * shaped, axis=2, keepdims=True))
    return (shaped / jnp.sqrt(mean + NORM_EPS)).reshape(grad.shape)

def reference(x_rows, d_attn, q_saved, k_saved, v_saved, w_query, w_key, w_value, down_all, up_query, up_kv, tenant, doc_starts):
    groups = N_TENSOR
    per_group = HQ // N_TENSOR
    wq_wide = w_query.astype(jnp.float32).reshape(D, groups, per_group * HD)
    wk_wide = w_key.astype(jnp.float32).reshape(D, groups, HD)
    wv_wide = w_value.astype(jnp.float32).reshape(D, groups, HD)
    highest = lax.Precision.HIGHEST

    def one_seq(carry, item):
        grad_down, grad_query, grad_kv = carry
        x_seq, g_seq, q_seq, k_seq, v_seq, tenant_id, starts = item
        offset, allowed = doc_layout(starts)
        cosine, sine = rotary_tables(offset, HD)
        dq_low, dk_low, dv_low = attention_back(q_seq.reshape(SEQ, groups, per_group, HD), k_seq.reshape(SEQ, groups, HD), v_seq.reshape(SEQ, groups, HD), g_seq.reshape(SEQ, groups, per_group, HD), allowed, cosine, sine)
        query_gradient_flat = dq_low.reshape(SEQ, groups * per_group * HD)
        key_gradient_flat = dk_low.reshape(SEQ, groups * HD)
        value_gradient_flat = dv_low.reshape(SEQ, groups * HD)
        part = jnp.einsum('pgc,dgc->gpd', dq_low.reshape(SEQ, groups, per_group * HD).astype(jnp.float32), wq_wide)
        part = part + jnp.einsum('pgc,dgc->gpd', dk_low.astype(jnp.float32), wk_wide)
        part = part + jnp.einsum('pgc,dgc->gpd', dv_low.astype(jnp.float32), wv_wide)
        frozen = lax.optimization_barrier(jnp.sum(lax.optimization_barrier(part.astype(jnp.bfloat16)).astype(jnp.float32), axis=0))
        down_t = down_all[tenant_id]
        lowrank_activation = jnp.dot(x_seq, down_t.T, preferred_element_type=jnp.float32).astype(jnp.bfloat16)
        query_up_transposed = up_query[tenant_id]
        keyvalue_up_transposed = up_kv[tenant_id]
        lowrank_gradient = ADAPTER_SCALING * jnp.concatenate([jnp.dot(query_gradient_flat, query_up_transposed.T, preferred_element_type=jnp.float32), jnp.dot(key_gradient_flat, keyvalue_up_transposed[:ADAPTER_RANK].T, preferred_element_type=jnp.float32), jnp.dot(value_gradient_flat, keyvalue_up_transposed[ADAPTER_RANK:].T, preferred_element_type=jnp.float32)], axis=1)
        d_seq = (frozen + jnp.dot(lowrank_gradient, down_t.astype(jnp.float32), precision=highest)).astype(jnp.bfloat16)
        ddown = jnp.dot(lowrank_gradient.T, x_seq.astype(jnp.float32), precision=highest)
        query_up_gradient = ADAPTER_SCALING * jnp.dot(lowrank_activation[:, :ADAPTER_RANK].T, query_gradient_flat, preferred_element_type=jnp.float32)
        key_up_gradient = ADAPTER_SCALING * jnp.dot(lowrank_activation[:, ADAPTER_RANK:2 * ADAPTER_RANK].T, key_gradient_flat, preferred_element_type=jnp.float32)
        value_up_gradient = ADAPTER_SCALING * jnp.dot(lowrank_activation[:, 2 * ADAPTER_RANK:].T, value_gradient_flat, preferred_element_type=jnp.float32)
        dup_kv = jnp.concatenate([key_up_gradient, value_up_gradient], axis=0).reshape(2 * ADAPTER_RANK, KVH, KV_REP, HD)
        dup_kv = jnp.broadcast_to(lax.optimization_barrier(jnp.sum(dup_kv, axis=2, keepdims=True)), dup_kv.shape).reshape(2 * ADAPTER_RANK, KVCOLS)
        hot = (jnp.arange(TEN, dtype=jnp.int32) == tenant_id).astype(jnp.float32)
        carry = (grad_down + hot[:, None, None] * ddown[None], grad_query + hot[:, None, None] * query_up_gradient[None], grad_kv + hot[:, None, None] * dup_kv[None])
        return (carry, d_seq)
    start = (jnp.zeros((TEN, 3 * ADAPTER_RANK, D), jnp.float32), jnp.zeros((TEN, ADAPTER_RANK, HQ * HD), jnp.float32), jnp.zeros((TEN, 2 * ADAPTER_RANK, KVCOLS), jnp.float32))
    items = (x_rows.reshape(SEQS, SEQ, D), d_attn.reshape(SEQS, SEQ, HQ * HD), q_saved.reshape(SEQS, SEQ, HQ * HD), k_saved.reshape(SEQS, SEQ, KVCOLS), v_saved.reshape(SEQS, SEQ, KVCOLS), tenant, doc_starts)
    (grad_down, grad_query, grad_kv), d_rows = lax.scan(one_seq, start, items)
    return (d_rows.reshape(TOKENS, D), normalized(grad_down, 3), normalized(grad_query, 1), normalized(grad_kv, 2))
```

```python
import functools
import math
import numpy as np
import jax
import jax.numpy as jnp
from jax import lax
from jax.experimental import pallas as pl
from jax.experimental.pallas import tpu as pltpu
from jax.sharding import PartitionSpec as P

HD = 128
RANK = 16
TEN = 4
SEQ = 1024
ROPE_BASE = 500000.0
NORM_EPS = 1e-06
MASKED = -1e30
NT = (((1,), (1,)), ((), ()))
TN = (((0,), (0,)), ((), ()))
F32 = jnp.float32
BF16 = jnp.bfloat16
ROWS = 256


def rope_constants():
    half = HD // 2
    freq = ROPE_BASE ** (-(2.0 * np.arange(half)) / HD)
    angle = np.arange(SEQ)[:, None] * freq[None, :]
    cosine = np.concatenate([np.cos(angle), np.cos(angle)], axis=1)
    sine = np.concatenate([np.sin(angle), -np.sin(angle)], axis=1)
    return cosine.astype(np.float32), sine.astype(np.float32)


def attention_kernel(
    ints, q_ref, k_ref, v_ref, g_ref, x_ref, down_ref, upq_ref, upkv_ref, cos_ref, sin_ref,
    grad_ref, dlow_ref, low_ref,
    kt_ref, vt_ref, dk_ref, dv_ref, c_ref, s_ref,
):
    scale = HD ** (-0.5)
    scale2 = scale * math.log2(math.e)
    low_ref[...] = lax.dot_general(
        down_ref[0], x_ref[...], NT, preferred_element_type=F32
    ).astype(BF16)

    def sequence(s, carry):
        base = pl.multiple_of(s * SEQ, SEQ)
        starts = [ints[2 + 4 * s + j] for j in range(4)]
        pos = lax.broadcasted_iota(jnp.int32, (SEQ, HD), 0)
        cb = jnp.broadcast_to(cos_ref[pl.ds(starts[0], 1), :], (SEQ, HD))
        sb = jnp.broadcast_to(sin_ref[pl.ds(starts[0], 1), :], (SEQ, HD))
        for j in range(1, 4):
            inside = pos >= starts[j]
            cb = jnp.where(inside, cos_ref[pl.ds(starts[j], 1), :], cb)
            sb = jnp.where(inside, sin_ref[pl.ds(starts[j], 1), :], sb)
        cp = cos_ref[...]
        sp = sin_ref[...]
        c_ref[...] = cp * cb + sp * sb
        s_ref[...] = sp * cb - cp * sb
        kt_ref[...] = k_ref[pl.ds(base, SEQ), :].T
        vt_ref[...] = v_ref[pl.ds(base, SEQ), :].T
        dk_ref[...] = jnp.zeros_like(dk_ref)
        dv_ref[...] = jnp.zeros_like(dv_ref)
        for h in range(2):
            cols = slice(h * HD, (h + 1) * HD)
            for i in range(SEQ // ROWS):
                width = (i + 1) * ROWS
                rows = pl.ds(base + i * ROWS, ROWS)
                keys = pl.ds(base, width)
                q = q_ref[rows, cols]
                g = g_ref[rows, cols]
                p_row = lax.broadcasted_iota(jnp.int32, (1, ROWS), 1) + i * ROWS
                begin = jnp.zeros((1, ROWS), jnp.int32)
                for j in range(1, 4):
                    begin = jnp.where(p_row >= starts[j], starts[j], begin)
                k_idx = lax.broadcasted_iota(jnp.int32, (width, ROWS), 0)
                allowed = (k_idx >= begin) & (k_idx <= p_row)
                st = lax.dot_general(k_ref[keys, :], q, NT, preferred_element_type=F32)
                st = jnp.where(allowed, st * scale2, MASKED)
                top = jnp.max(st, axis=0, keepdims=True)
                e = jnp.exp2(st - top)
                inv = 1.0 / jnp.sum(e, axis=0, keepdims=True)
                p = e * inv
                p_low = p.astype(BF16)
                ot = jnp.dot(vt_ref[:, :width], p_low, preferred_element_type=F32)
                delta = jnp.sum(g.astype(F32).T * ot, axis=0, keepdims=True)
                dpt = lax.dot_general(v_ref[keys, :], g, NT, preferred_element_type=F32)
                ds_low = (p * (dpt - delta)).astype(BF16)
                dqt = jnp.dot(kt_ref[:, :width], ds_low, preferred_element_type=F32)
                dk_ref[:width, :] += jnp.dot(ds_low, q, preferred_element_type=F32)
                dv_ref[:width, :] += jnp.dot(p_low, g, preferred_element_type=F32)
                dq = dqt.T * scale
                dq = dq * c_ref[i * ROWS : (i + 1) * ROWS, :] + pltpu.roll(
                    dq, HD // 2, 1
                ) * s_ref[i * ROWS : (i + 1) * ROWS, :]
                grad_ref[rows, cols] = dq.astype(BF16)
        dk = dk_ref[...] * scale
        dk = dk * c_ref[...] + pltpu.roll(dk, HD // 2, 1) * s_ref[...]
        grad_ref[pl.ds(base, SEQ), 2 * HD : 3 * HD] = dk.astype(BF16)
        grad_ref[pl.ds(base, SEQ), 3 * HD : 4 * HD] = dv_ref[...].astype(BF16)
        t = ints[s]
        seq_rows = pl.ds(base, SEQ)
        parts = [
            (upq_ref[t], slice(0, 2 * HD)),
            (upkv_ref[t, :RANK, :], slice(2 * HD, 3 * HD)),
            (upkv_ref[t, RANK:, :], slice(3 * HD, 4 * HD)),
        ]
        for n, (up, c) in enumerate(parts):
            back = 2.0 * lax.dot_general(
                up, grad_ref[seq_rows, c], NT, preferred_element_type=F32
            )
            for b in range(8):
                dlow_ref[s * 8 + b, n * RANK : (n + 1) * RANK, :] = back[:, b * 128 : (b + 1) * 128]
        return carry

    lax.fori_loop(0, 2, sequence, 0)


def attention_call(ints, q, k, v, g, x, down, upq, upkv):
    cosine, sine = rope_constants()
    tokens = q.shape[0]
    width = x.shape[1]

    def whole(shape):
        return pl.BlockSpec(shape, lambda i, n: (0,) * len(shape))

    return pl.pallas_call(
        attention_kernel,
        grid_spec=pltpu.PrefetchScalarGridSpec(
            num_scalar_prefetch=1,
            grid=(1,),
            in_specs=[
                whole(q.shape), whole(k.shape), whole(v.shape), whole(g.shape), whole(x.shape),
                pl.BlockSpec((1, 3 * RANK, width), lambda i, n: (n[10], 0, 0)),
                whole(upq.shape), whole(upkv.shape), whole(cosine.shape), whole(sine.shape),
            ],
            out_specs=[whole((tokens, 4 * HD)), whole((16, 48, 128)), whole((48, 128))],
            scratch_shapes=[
                pltpu.VMEM((HD, SEQ), BF16), pltpu.VMEM((HD, SEQ), BF16),
                pltpu.VMEM((SEQ, HD), F32), pltpu.VMEM((SEQ, HD), F32),
                pltpu.VMEM((SEQ, HD), F32), pltpu.VMEM((SEQ, HD), F32),
            ],
        ),
        out_shape=[
            jax.ShapeDtypeStruct((tokens, 4 * HD), BF16),
            jax.ShapeDtypeStruct((16, 48, 128), F32),
            jax.ShapeDtypeStruct((48, 128), BF16),
        ],
        compiler_params=pltpu.CompilerParams(vmem_limit_bytes=56 * 1024 * 1024),
        cost_estimate=pl.CostEstimate(
            flops=6_400_000_000, bytes_accessed=10_000_000, transcendentals=4_000_000
        ),
        name="attention_back",
    )(ints, q, k, v, g, x, down, upq, upkv, cosine, sine)


def from_partner(value, axis, apart):
    mask = 2**apart
    pairs = [(source, source ^ mask) for source in range(lax.axis_size(axis))]
    return lax.ppermute(value, axis, pairs)


def per_device(
    x_rows,
    d_attn,
    q_saved,
    k_saved,
    v_saved,
    w_query,
    w_key,
    w_value,
    down_all,
    up_query,
    up_kv,
    tenant,
    doc_starts,
):
    rows = x_rows.shape[0]
    width = x_rows.shape[1]
    group_tokens = q_saved.shape[0]
    local_heads = q_saved.shape[1] // HD
    sequences = group_tokens // SEQ
    tensor_size = lax.axis_size("tensor")
    here = lax.axis_index("tensor")
    contract = (((1,), (1,)), ((), ()))
    tenant_ids = jnp.arange(TEN, dtype=jnp.int32)
    seq_hot = (tenant[:, None] == tenant_ids[None, :]).astype(jnp.float32)
    token_tenant_onehot = jnp.repeat(seq_hot, SEQ, axis=0)
    row_hot = lax.dynamic_slice_in_dim(token_tenant_onehot, here * rows, rows, 0)
    down_flat = down_all.reshape(TEN * 3 * RANK, width)
    ints = jnp.concatenate(
        [tenant, doc_starts.reshape(-1), lax.dynamic_slice_in_dim(tenant, here // 8, 1)]
    )
    grads, dlow_part, low_own = attention_call(
        ints, q_saved, k_saved, v_saved, d_attn, x_rows, down_all, up_query, up_kv
    )
    low_rows = lax.all_gather(low_own, "tensor", axis=1, tiled=True)
    query_gradient_flat = grads[:, :256]
    key_gradient_flat = grads[:, 256:384]
    value_gradient_flat = grads[:, 384:]
    low_grad = lax.psum_scatter(
        dlow_part.astype(jnp.bfloat16), "tensor", scatter_dimension=0, tiled=True
    )[0].astype(jnp.float32)
    masked_low = low_rows[None, :, :] * token_tenant_onehot.T[:, None, :].astype(jnp.bfloat16)
    query_gradient = 2.0 * jnp.dot(
        masked_low[:, :RANK].reshape(TEN * RANK, group_tokens),
        query_gradient_flat,
        preferred_element_type=jnp.float32,
    ).reshape(TEN, RANK, -1)
    key_gradient = 2.0 * jnp.dot(
        masked_low[:, RANK : 2 * RANK].reshape(TEN * RANK, group_tokens),
        key_gradient_flat,
        preferred_element_type=jnp.float32,
    ).reshape(TEN, RANK, HD)
    value_gradient = 2.0 * jnp.dot(
        masked_low[:, 2 * RANK :].reshape(TEN * RANK, group_tokens),
        value_gradient_flat,
        preferred_element_type=jnp.float32,
    ).reshape(TEN, RANK, HD)
    grad_kv = jnp.concatenate([key_gradient, value_gradient], axis=1)
    grad_kv = grad_kv + from_partner(grad_kv.astype(jnp.bfloat16), "tensor", 0).astype(
        grad_kv.dtype
    )
    total = lax.dot_general(
        query_gradient_flat, w_query, contract, preferred_element_type=jnp.float32
    )
    total = total + lax.dot_general(
        key_gradient_flat, w_key, contract, preferred_element_type=jnp.float32
    )
    frozen = lax.psum_scatter(
        (
            total
            + lax.dot_general(
                value_gradient_flat, w_value, contract, preferred_element_type=jnp.float32
            )
        ).astype(jnp.bfloat16),
        "tensor",
        scatter_dimension=0,
        tiled=True,
    ).astype(jnp.float32)
    spread = (row_hot[:, :, None] * low_grad.T[:, None, :]).reshape(rows, TEN * 3 * RANK)
    down_wide = down_flat.astype(jnp.float32)
    lowrank_dx = jnp.dot(spread, down_wide, precision=lax.Precision.HIGHEST)
    d_rows = (frozen + lowrank_dx).astype(jnp.bfloat16)
    weighted = (row_hot.T[:, None, :] * low_grad[None, :, :]).reshape(TEN * 3 * RANK, rows)
    down_part = jnp.dot(
        weighted, x_rows.astype(jnp.float32), precision=lax.Precision.HIGHEST
    ).reshape(TEN, 3 * RANK, width)
    local_width = width // tensor_size
    down_grad = lax.psum(
        lax.psum_scatter(
            down_part.astype(jnp.bfloat16), "tensor", scatter_dimension=2, tiled=True
        ).astype(jnp.float32),
        "dp",
    )
    query_gradient, grad_kv = (
        lax.psum(query_gradient.astype(jnp.bfloat16), "dp").astype(jnp.float32),
        lax.psum(grad_kv.astype(jnp.bfloat16), "dp").astype(jnp.float32),
    )
    square_down = jnp.sum((down_grad * down_grad).reshape(TEN, 3, -1), axis=2)
    square_q = jnp.sum((query_gradient * query_gradient).reshape(TEN, -1), axis=1)
    square_kv = jnp.sum((grad_kv * grad_kv).reshape(TEN, 2, -1), axis=2)
    total_down, total_q, total_kv = lax.psum((square_down, square_q, square_kv), "tensor")
    count_down = RANK * width
    count_q = RANK * query_gradient.shape[2] * tensor_size
    count_kv = RANK * HD * tensor_size
    upd_down = (
        down_grad.reshape(TEN, 3, RANK, -1)
        / jnp.sqrt(total_down / count_down + NORM_EPS)[:, :, None, None]
    ).reshape(down_grad.shape)
    upd_query = query_gradient / jnp.sqrt(total_q / count_q + NORM_EPS)[:, None, None]
    upd_kv = (
        grad_kv.reshape(TEN, 2, RANK, -1)
        / jnp.sqrt(total_kv / count_kv + NORM_EPS)[:, :, None, None]
    ).reshape(grad_kv.shape)
    return (d_rows, upd_down, upd_query, upd_kv)


def solution(mesh):
    in_specs = (
        P(("dp", "tensor"), None),
        P("dp", "tensor"),
        P("dp", "tensor"),
        P("dp", "tensor"),
        P("dp", "tensor"),
        P(None, "tensor"),
        P(None, "tensor"),
        P(None, "tensor"),
        P(),
        P(None, None, "tensor"),
        P(None, None, "tensor"),
        P("dp"),
        P("dp", None),
    )
    out_specs = (
        P(("dp", "tensor"), None),
        P(None, None, "tensor"),
        P(None, None, "tensor"),
        P(None, None, "tensor"),
    )
    return jax.shard_map(
        per_device, mesh=mesh, in_specs=in_specs, out_specs=out_specs, check_vma=False
    )
```

```python
import functools
import math
import numpy as np
import jax
import jax.numpy as jnp
from jax import lax
from jax.experimental import pallas as pl
from jax.experimental.pallas import tpu as pltpu
from jax.sharding import PartitionSpec as P

HD = 128
RANK = 16
TEN = 4
SEQ = 1024
ROPE_BASE = 500000.0
NORM_EPS = 1e-06
MASKED = -1e30
NT = (((1,), (1,)), ((), ()))
TN = (((0,), (0,)), ((), ()))
F32 = jnp.float32
BF16 = jnp.bfloat16
ROWS = 256


def rope_constants():
    half = HD // 2
    freq = ROPE_BASE ** (-(2.0 * np.arange(half)) / HD)
    angle = np.arange(SEQ)[:, None] * freq[None, :]
    cosine = np.concatenate([np.cos(angle), np.cos(angle)], axis=1)
    sine = np.concatenate([np.sin(angle), -np.sin(angle)], axis=1)
    return cosine.astype(np.float32), sine.astype(np.float32)


def attention_kernel(
    tenant_ref, doc_ref, q_ref, k_ref, v_ref, g_ref, x_ref, down_ref, upq_ref, upkv_ref,
    cos_ref, sin_ref,
    grad_ref, dlow_ref, low_ref, hot_ref, dsel_ref,
    kt_ref, vt_ref, dk_ref, dv_ref, c_ref, s_ref, down_sem,
):
    own = tenant_ref[lax.axis_index("tensor") // 8]
    fetch = pltpu.make_async_copy(down_ref.at[own], dsel_ref, down_sem)
    fetch.start()
    for s in range(2):
        for t in range(TEN):
            hot_ref[4 * s + t : 4 * s + t + 1, :] = jnp.where(
                jnp.full((1, 128), tenant_ref[s]) == t, 1.0, 0.0
            )
    scale = HD ** (-0.5)
    scale2 = scale * math.log2(math.e)

    def sequence(s, carry):
        base = pl.multiple_of(s * SEQ, SEQ)
        starts = [doc_ref[s, j] for j in range(4)]
        pos = lax.broadcasted_iota(jnp.int32, (SEQ, HD), 0)
        cb = jnp.broadcast_to(cos_ref[pl.ds(starts[0], 1), :], (SEQ, HD))
        sb = jnp.broadcast_to(sin_ref[pl.ds(starts[0], 1), :], (SEQ, HD))
        for j in range(1, 4):
            inside = pos >= starts[j]
            cb = jnp.where(inside, cos_ref[pl.ds(starts[j], 1), :], cb)
            sb = jnp.where(inside, sin_ref[pl.ds(starts[j], 1), :], sb)
        cp = cos_ref[...]
        sp = sin_ref[...]
        c_ref[...] = cp * cb + sp * sb
        s_ref[...] = sp * cb - cp * sb
        kt_ref[...] = k_ref[pl.ds(base, SEQ), :].T
        vt_ref[...] = v_ref[pl.ds(base, SEQ), :].T
        dk_ref[...] = jnp.zeros_like(dk_ref)
        dv_ref[...] = jnp.zeros_like(dv_ref)
        for h in range(2):
            cols = slice(h * HD, (h + 1) * HD)
            for i in range(SEQ // ROWS):
                width = (i + 1) * ROWS
                rows = pl.ds(base + i * ROWS, ROWS)
                keys = pl.ds(base, width)
                q = q_ref[rows, cols]
                g = g_ref[rows, cols]
                p_row = lax.broadcasted_iota(jnp.int32, (1, ROWS), 1) + i * ROWS
                begin = jnp.zeros((1, ROWS), jnp.int32)
                for j in range(1, 4):
                    begin = jnp.where(p_row >= starts[j], starts[j], begin)
                k_idx = lax.broadcasted_iota(jnp.int32, (width, ROWS), 0)
                allowed = (k_idx >= begin) & (k_idx <= p_row)
                st = lax.dot_general(k_ref[keys, :], q, NT, preferred_element_type=F32)
                st = jnp.where(allowed, st * scale2, MASKED)
                top = jnp.max(st, axis=0, keepdims=True)
                e = jnp.exp2(st - top)
                inv = 1.0 / jnp.sum(e, axis=0, keepdims=True)
                p = e * inv
                p_low = p.astype(BF16)
                ot = jnp.dot(vt_ref[:, :width], p_low, preferred_element_type=F32)
                delta = jnp.sum(g.astype(F32).T * ot, axis=0, keepdims=True)
                dpt = lax.dot_general(v_ref[keys, :], g, NT, preferred_element_type=F32)
                ds_low = (p * (dpt - delta)).astype(BF16)
                dqt = jnp.dot(kt_ref[:, :width], ds_low, preferred_element_type=F32)
                dk_ref[:width, :] += jnp.dot(ds_low, q, preferred_element_type=F32)
                dv_ref[:width, :] += jnp.dot(p_low, g, preferred_element_type=F32)
                dq = dqt.T * scale
                dq = dq * c_ref[i * ROWS : (i + 1) * ROWS, :] + pltpu.roll(
                    dq, HD // 2, 1
                ) * s_ref[i * ROWS : (i + 1) * ROWS, :]
                grad_ref[rows, cols] = dq.astype(BF16)
        dk = dk_ref[...] * scale
        dk = dk * c_ref[...] + pltpu.roll(dk, HD // 2, 1) * s_ref[...]
        grad_ref[pl.ds(base, SEQ), 2 * HD : 3 * HD] = dk.astype(BF16)
        grad_ref[pl.ds(base, SEQ), 3 * HD : 4 * HD] = dv_ref[...].astype(BF16)
        t = tenant_ref[s]
        seq_rows = pl.ds(base, SEQ)
        parts = [
            (upq_ref[t], slice(0, 2 * HD)),
            (upkv_ref[t, :RANK, :], slice(2 * HD, 3 * HD)),
            (upkv_ref[t, RANK:, :], slice(3 * HD, 4 * HD)),
        ]
        for n, (up, c) in enumerate(parts):
            back = 2.0 * lax.dot_general(
                up, grad_ref[seq_rows, c], NT, preferred_element_type=F32
            )
            for b in range(8):
                dlow_ref[s * 8 + b, n * RANK : (n + 1) * RANK, :] = back[:, b * 128 : (b + 1) * 128]
        return carry

    lax.fori_loop(0, 2, sequence, 0)
    fetch.wait()
    low_ref[...] = lax.dot_general(
        dsel_ref[...], x_ref[...], NT, preferred_element_type=F32
    ).astype(BF16)


def attention_call(tenant, docs, q, k, v, g, x, down, upq, upkv):
    cosine, sine = rope_constants()
    tokens = q.shape[0]
    vmem = pl.BlockSpec(memory_space=pltpu.VMEM)
    smem = pl.BlockSpec(memory_space=pltpu.SMEM)
    return pl.pallas_call(
        attention_kernel,
        in_specs=[smem] * 2 + [vmem] * 5 + [pl.BlockSpec(memory_space=pl.ANY)] + [vmem] * 4,
        out_specs=[vmem] * 5,
        scratch_shapes=[
            pltpu.VMEM((HD, SEQ), BF16), pltpu.VMEM((HD, SEQ), BF16),
            pltpu.VMEM((SEQ, HD), F32), pltpu.VMEM((SEQ, HD), F32),
            pltpu.VMEM((SEQ, HD), F32), pltpu.VMEM((SEQ, HD), F32),
            pltpu.SemaphoreType.DMA,
        ],
        out_shape=[
            jax.ShapeDtypeStruct((tokens, 4 * HD), BF16),
            jax.ShapeDtypeStruct((16, 48, 128), F32),
            jax.ShapeDtypeStruct((48, 128), BF16),
            jax.ShapeDtypeStruct((8, 128), F32),
            jax.ShapeDtypeStruct((48, x.shape[1]), BF16),
        ],
        compiler_params=pltpu.CompilerParams(vmem_limit_bytes=56 * 1024 * 1024),
        cost_estimate=pl.CostEstimate(
            flops=6_400_000_000, bytes_accessed=10_000_000, transcendentals=4_000_000
        ),
        name="attention_back",
    )(tenant, docs, q, k, v, g, x, down, upq, upkv, cosine, sine)


MESH_ID = pl.DeviceIdType.MESH
CHUNK = 256
QUARTER = 512
BLOCK_D = 2048
ORDER = ((2, 0), (2, 1), (1, 0), (3, 1), (1, 1), (3, 0), (0, 1), (0, 0))


def exchange_kernel(
    grad_ref, dlow_ref, low_ref, hot_ref, x_ref, dsel_ref,
    wq_ref, wk_ref, wv_ref, p1_ref, p2_ref, p3_ref, c1_ref, c2_ref, c3_ref,
    out_ref, ud_ref, uq_ref, ukv_ref,
    gall, a_ref, wx, part, zbuf, fbuf, fin,
    dlall, lowall, lowcat, dlw_ref, kvown, kvpeer, qown, gdown, gdall, dsum,
    rsbuf, rsall, agbuf, sqall,
    wsem, gsend, grecv, dlsend, dlrecv, lowsend, lowrecv, kvsem, dnsend, dnrecv,
    rssend, rsrecv, agsend, agrecv, sqsend, sqrecv, zsend, zrecv, fsend, frecv,
):
    me_dp = lax.axis_index("dp")
    me_t = lax.axis_index("tensor")
    z = me_t // 4
    x = me_t % 4
    core = me_dp % 2
    xr, xl, xo = (x + 1) % 4, (x + 3) % 4, (x + 2) % 4
    pair = x + 1 - 2 * (x % 2)
    mirror = 3 - x
    z_right = ((z + 1) % 4) * 4 + x
    z_left = ((z + 3) % 4) * 4 + x

    def remote(src, dst, ssem, rsem, dp, t):
        return pltpu.make_async_remote_copy(
            src_ref=src, dst_ref=dst, send_sem=ssem, recv_sem=rsem,
            device_id=(dp, t), device_id_type=MESH_ID,
        )

    barrier = pltpu.get_barrier_semaphore()

    def greet_tensor(o, c):
        pl.semaphore_signal(
            barrier, inc=1, device_id=(me_dp, (me_t + o) % 16), device_id_type=MESH_ID
        )
        return c

    def greet_dp(o, c):
        pl.semaphore_signal(
            barrier, inc=1, device_id=((me_dp + o) % 8, me_t), device_id_type=MESH_ID
        )
        return c

    lax.fori_loop(1, 16, greet_tensor, 0)
    lax.fori_loop(1, 8, greet_dp, 0)

    mine = pl.multiple_of(core * 1024, 1024)
    other = pl.multiple_of((1 - core) * 1024, 1024)
    d0 = pl.multiple_of(x * BLOCK_D, BLOCK_D)
    kv_here = 4 + x // 2
    kv_there = 5 - x // 2

    def piece(i, src, dst):
        return pltpu.make_async_copy(src, dst, wsem.at[i])

    w_copies = [
        piece(0, wq_ref.at[pl.ds(d0, BLOCK_D), :], wx.at[x]),
        piece(1, wk_ref.at[pl.ds(d0, BLOCK_D), :], wx.at[kv_here, :, pl.ds(0, 128)]),
        piece(2, wv_ref.at[pl.ds(d0, BLOCK_D), :], wx.at[kv_here, :, pl.ds(128, 128)]),
    ]
    for n, (row, refs) in enumerate(((mine, (p1_ref, p2_ref, p3_ref)), (other, (c1_ref, c2_ref, c3_ref)))):
        i = 3 + 5 * n
        w_copies += [
            piece(i, refs[0], wx.at[pair, pl.ds(row, 1024), :]),
            piece(i + 1, refs[1].at[pl.ds(0, 1024), :], wx.at[xo, pl.ds(row, 1024), :]),
            piece(i + 2, refs[1].at[pl.ds(1024, 512), :], wx.at[kv_there, pl.ds(row, 512), :]),
            piece(i + 3, refs[2].at[pl.ds(0, 1024), :], wx.at[mirror, pl.ds(row, 1024), :]),
            piece(
                i + 4, refs[2].at[pl.ds(1024, 512), :],
                wx.at[kv_there, pl.ds(pl.multiple_of(row + 512, 512), 512), :],
            ),
        ]
    for copy in w_copies:
        copy.start()

    pl.semaphore_wait(barrier, 22)

    def first_row(c):
        off, half = ORDER[c]
        return pl.multiple_of(((z + off) % 4) * QUARTER + half * CHUNK, CHUNK)

    def gather_out(c):
        rows = pl.ds(first_row(c), CHUNK)
        src = grad_ref.at[rows, :]
        dst = gall.at[x, rows, :]
        return (
            remote(src, dst, gsend.at[0, c], grecv.at[0, c], me_dp, z * 4 + xr),
            remote(src, dst, gsend.at[1, c], grecv.at[1, c], me_dp, z * 4 + xl),
        )

    def gather_in(c):
        rows = pl.ds(first_row(c), CHUNK)
        from_l = gall.at[xl, rows, :]
        from_r = gall.at[xr, rows, :]
        return (
            remote(from_l, from_l, gsend.at[0, c], grecv.at[0, c], me_dp, z * 4 + xr),
            remote(from_r, from_r, gsend.at[1, c], grecv.at[1, c], me_dp, z * 4 + xl),
        )

    def forward_out(c):
        r0 = first_row(c)
        to_r = gall.at[xl, pl.ds(r0, CHUNK // 2), :]
        to_l = gall.at[xr, pl.ds(pl.multiple_of(r0 + CHUNK // 2, CHUNK // 2), CHUNK // 2), :]
        return (
            remote(to_r, to_r, gsend.at[2, c], grecv.at[2, c], me_dp, z * 4 + xr),
            remote(to_l, to_l, gsend.at[3, c], grecv.at[3, c], me_dp, z * 4 + xl),
        )

    def forward_in(c):
        r0 = first_row(c)
        from_l = gall.at[xo, pl.ds(r0, CHUNK // 2), :]
        from_r = gall.at[xo, pl.ds(pl.multiple_of(r0 + CHUNK // 2, CHUNK // 2), CHUNK // 2), :]
        return (
            remote(from_l, from_l, gsend.at[2, c], grecv.at[2, c], me_dp, z * 4 + xr),
            remote(from_r, from_r, gsend.at[3, c], grecv.at[3, c], me_dp, z * 4 + xl),
        )

    def start(copies):
        for copy in copies:
            copy.start()

    def arrive(c):
        for copy in gather_in(c):
            copy.wait_recv()
        start(forward_out(c))

    def to_tensor(src, buf, ssem, rsem, picked):
        def descriptor(t):
            return remote(
                src.at[t] if picked else src, buf.at[me_t], ssem.at[t], rsem.at[me_t], me_dp, t
            )

        def begin(o, c):
            descriptor((me_t + o) % 16).start()
            return c

        def receive(o, c):
            t = (me_t + o) % 16
            remote(buf.at[t], buf.at[t], ssem.at[t], rsem.at[t], me_dp, t).wait_recv()
            return c

        def sent(o, c):
            descriptor((me_t + o) % 16).wait_send()
            return c

        return (
            lambda: lax.fori_loop(1, 16, begin, 0),
            lambda: lax.fori_loop(1, 16, receive, 0),
            lambda: lax.fori_loop(1, 16, sent, 0),
        )

    def to_dp(src_at, buf, ssem, rsem):
        def descriptor(d):
            return remote(src_at(d), buf.at[me_dp], ssem.at[d], rsem.at[me_dp], d, me_t)

        def begin(o, c):
            descriptor((me_dp + o) % 8).start()
            return c

        def receive(o, c):
            d = (me_dp + o) % 8
            remote(buf.at[d], buf.at[d], ssem.at[d], rsem.at[d], d, me_t).wait_recv()
            return c

        def sent(o, c):
            descriptor((me_dp + o) % 8).wait_send()
            return c

        return (
            lambda: lax.fori_loop(1, 8, begin, 0),
            lambda: lax.fori_loop(1, 8, receive, 0),
            lambda: lax.fori_loop(1, 8, sent, 0),
        )

    dl_start, dl_recv, dl_sent = to_tensor(dlow_ref, dlall, dlsend, dlrecv, True)
    low_start, low_recv, low_sent = to_tensor(low_ref, lowall, lowsend, lowrecv, False)
    dn_start, dn_recv, dn_sent = to_tensor(gdown, gdall, dnsend, dnrecv, True)
    sq_start, sq_recv, sq_sent = to_tensor(sqall.at[me_t], sqall, sqsend, sqrecv, False)
    rs_start, rs_recv, rs_sent = to_dp(lambda d: rsbuf.at[d], rsall, rssend, rsrecv)
    ag_start, ag_recv, ag_sent = to_dp(lambda d: agbuf.at[me_dp], agbuf, agsend, agrecv)
    kv_copy = remote(kvown, kvpeer, kvsem.at[0], kvsem.at[1], me_dp, z * 4 + pair)

    start(gather_out(0))
    dl_start()
    low_start()
    start(gather_out(1))
    start(gather_out(2))
    dlall[me_t] = dlow_ref[me_t]
    lowall[me_t] = low_ref[...]
    gall[x] = grad_ref[...]

    def step_low():
        low_recv()
        for b in range(16):
            lowcat[:, b * 128 : (b + 1) * 128] = lowall[b]
        for s in range(2):
            rows = slice(s * SEQ, (s + 1) * SEQ)
            qown[s] = 2.0 * jnp.dot(
                lowcat[:RANK, rows], grad_ref[rows, 0:256], preferred_element_type=F32
            )
            kvown[s, :RANK, :] = 2.0 * jnp.dot(
                lowcat[RANK : 2 * RANK, rows], grad_ref[rows, 256:384], preferred_element_type=F32
            )
            kvown[s, RANK:, :] = 2.0 * jnp.dot(
                lowcat[2 * RANK :, rows], grad_ref[rows, 384:512], preferred_element_type=F32
            )
        kv_copy.start()

    def step_dlow():
        dl_recv()
        total = dlall[0]
        for b in range(1, 16):
            total = total + dlall[b]
        dlw_ref[...] = total.astype(BF16)

        def column(t, c):
            gdown[t] = jnp.dot(
                dlw_ref[...], x_ref[:, pl.ds(pl.multiple_of(t * 512, 512), 512)],
                preferred_element_type=F32,
            ).astype(BF16)
            return c

        lax.fori_loop(0, 16, column, 0)
        dn_start()
        gdall[me_t] = gdown[me_t]

    def step_down():
        dn_recv()
        kv_copy.wait_recv()
        for s in range(2):
            total = gdall[8 * s].astype(F32)
            for b in range(1, 8):
                total = total + gdall[8 * s + b].astype(F32)
            dsum[s] = total
            kvown_sum = kvown[s] + kvpeer[s]
            kvpeer[s] = kvown_sum
        for j in range(8):
            cb = j % 4
            for i in range(2):
                t = 2 * (j // 4) + i
                rsbuf[j, 48 * i : 48 * (i + 1), :] = (
                    dsum[0, :, cb * 128 : (cb + 1) * 128] * hot_ref[t : t + 1, :]
                    + dsum[1, :, cb * 128 : (cb + 1) * 128] * hot_ref[4 + t : 5 + t, :]
                )
            t = j // 2
            c = j % 2
            rsbuf[j, 96:112, :] = (
                qown[0, :, c * 128 : (c + 1) * 128] * hot_ref[t : t + 1, :]
                + qown[1, :, c * 128 : (c + 1) * 128] * hot_ref[4 + t : 5 + t, :]
            )
            rsbuf[j, 112:128, :] = (
                kvpeer[0, c * 16 : (c + 1) * 16, :] * hot_ref[t : t + 1, :]
                + kvpeer[1, c * 16 : (c + 1) * 16, :] * hot_ref[4 + t : 5 + t, :]
            )
        rs_start()
        rsall[me_dp] = rsbuf[me_dp]

    def step_reduce():
        rs_recv()
        total = rsall[0]
        for b in range(1, 8):
            total = total + rsall[b]
        agbuf[me_dp] = total
        ag_start()

    def parts_of(t):
        for n in range(3):
            lo = (t % 2) * 48 + n * 16
            yield [(t // 2) * 4 + cb for cb in range(4)], slice(lo, lo + 16)
        yield [2 * t, 2 * t + 1], slice(96, 112)
        yield [2 * t], slice(112, 128)
        yield [2 * t + 1], slice(112, 128)

    def step_squares():
        ag_recv()
        row = lax.broadcasted_iota(jnp.int32, (8, 128), 0)
        lane = lax.broadcasted_iota(jnp.int32, (8, 128), 1)
        tile = jnp.zeros((8, 128), F32)
        for t in range(TEN):
            for n, (pieces, rows) in enumerate(parts_of(t)):
                total = None
                for j in pieces:
                    v = agbuf[j, rows, :]
                    total = v * v if total is None else total + v * v
                value = jnp.sum(
                    jnp.sum(total, axis=0, keepdims=True), axis=1, keepdims=True
                )
                tile = jnp.where((row == t) & (lane == n), value, tile)
        sqall[me_t] = tile
        sq_start()

    def step_update():
        sq_recv()
        total = sqall[0]
        for b in range(1, 16):
            total = total + sqall[b]
        for t in range(TEN):
            for n, (pieces, rows) in enumerate(parts_of(t)):
                count = RANK * (8192 if n < 3 else 4096 if n == 3 else 2048)
                factor = 1.0 / jnp.sqrt(total[t : t + 1, n : n + 1] * (1.0 / count) + NORM_EPS)
                for i, j in enumerate(pieces):
                    value = agbuf[j, rows, :] * factor
                    if n < 3:
                        ud_ref[t, n * 16 : (n + 1) * 16, i * 128 : (i + 1) * 128] = value
                    elif n == 3:
                        uq_ref[t, :, i * 128 : (i + 1) * 128] = value
                    else:
                        ukv_ref[t, (n - 4) * 16 : (n - 3) * 16, :] = value

    def product(c, write, added):
        rows = pl.ds(first_row(c), CHUNK)
        for b in range(4):
            a_ref[b] = gall[b, rows, 0:256]
        for b in range(2):
            a_ref[4 + b] = (
                gall[2 * b, rows, 256:512].astype(F32) + gall[2 * b + 1, rows, 256:512].astype(F32)
            ).astype(BF16)

        def tile(n, carry):
            cols = pl.ds(pl.multiple_of(n * 512, 512), 512)
            acc = lax.dot_general(a_ref[0], wx[0, cols, :], NT, preferred_element_type=F32)
            for b in range(1, 6):
                acc = acc + lax.dot_general(
                    a_ref[b], wx[b, cols, :], NT, preferred_element_type=F32
                )
            for ref in added:
                acc = acc + ref[:, cols].astype(F32)
            write(cols, acc)
            return carry

        lax.fori_loop(0, 4, tile, 0)

    def z_copy(i):
        to = z_right if i % 2 == 0 else z_left
        return remote(part.at[i], zbuf.at[i], zsend.at[i], zrecv.at[i], me_dp, to)

    def to_part(i):
        def write(cols, acc):
            part[i, :, cols] = acc.astype(BF16)

        return write

    def to_final(half):
        def write(cols, acc):
            fbuf[2 * half, :, cols] = acc[:128].astype(BF16)
            fbuf[2 * half + 1, :, cols] = acc[128:].astype(BF16)

        return write

    def final_copy(o):
        return remote(fbuf.at[o], fin.at[x], fsend.at[o], frecv.at[x], me_dp, z * 4 + o)

    steps = (step_dlow, step_low, step_down, step_reduce, step_squares, step_update)
    arrive(0)
    for copy in w_copies:
        copy.wait()
    for c in range(8):
        if c + 1 < 8:
            arrive(c + 1)
        if c + 3 < 8:
            start(gather_out(c + 3))
        for copy in forward_in(c):
            copy.wait_recv()
        if c < 6:
            added = []
            if c in (2, 3):
                z_copy(c - 2).wait_recv()
                added = [zbuf.at[c - 2]]
            product(c, to_part(c), added)
            z_copy(c).start()
            steps[c]()
        else:
            half = ORDER[c][1]
            sources = (4, 3) if half == 1 else (2, 5)
            for i in sources:
                z_copy(i).wait_recv()
            product(c, to_final(half), [zbuf.at[i] for i in sources])
            for o in (2 * half, 2 * half + 1):

                @pl.when(x != o)
                def _(o=o):
                    final_copy(o).start()

    fin[x] = fbuf[x]
    for o in range(1, 4):
        xs = (x + o) % 4
        remote(fin.at[xs], fin.at[xs], fsend.at[xs], frecv.at[xs], me_dp, z * 4 + xs).wait_recv()
    for b in range(4):
        for n in range(4):
            cols = slice(b * BLOCK_D + n * 512, b * BLOCK_D + (n + 1) * 512)
            low_rank = lax.dot_general(
                dlw_ref[...], dsel_ref[:, cols], TN, preferred_element_type=F32
            )
            out_ref[:, cols] = (
                fin[b, :, n * 512 : (n + 1) * 512].astype(F32) + low_rank
            ).astype(BF16)

    for c in range(8):
        for copy in gather_out(c) + forward_out(c):
            copy.wait_send()
    for sent in (dl_sent, low_sent, dn_sent, sq_sent, rs_sent, ag_sent):
        sent()
    kv_copy.wait_send()
    for i in range(6):
        z_copy(i).wait_send()
    for o in range(4):

        @pl.when(x != o)
        def _(o=o):
            final_copy(o).wait_send()


def exchange_call(grad, dlow, low, hot, x, dsel, wq, wk, wv, pieces):
    vmem = pl.BlockSpec(memory_space=pltpu.VMEM)
    hbm = pl.BlockSpec(memory_space=pl.ANY)
    dma = pltpu.SemaphoreType.DMA
    tokens = grad.shape[0]
    return pl.pallas_call(
        exchange_kernel,
        in_specs=[vmem] * 6 + [hbm] * 9,
        out_specs=[vmem] * 4,
        out_shape=[
            jax.ShapeDtypeStruct(x.shape, BF16),
            jax.ShapeDtypeStruct((TEN, 48, 512), F32),
            jax.ShapeDtypeStruct((TEN, RANK, 256), F32),
            jax.ShapeDtypeStruct((TEN, 2 * RANK, 128), F32),
        ],
        scratch_shapes=[
            pltpu.VMEM((4, tokens, 512), BF16),
            pltpu.VMEM((6, CHUNK, 256), BF16),
            pltpu.VMEM((6, BLOCK_D, 256), BF16),
            pltpu.VMEM((6, CHUNK, BLOCK_D), BF16),
            pltpu.VMEM((6, CHUNK, BLOCK_D), BF16),
            pltpu.VMEM((4, 128, BLOCK_D), BF16),
            pltpu.VMEM((4, 128, BLOCK_D), BF16),
            pltpu.VMEM((16, 48, 128), F32),
            pltpu.VMEM((16, 48, 128), BF16),
            pltpu.VMEM((48, tokens), BF16),
            pltpu.VMEM((48, 128), BF16),
            pltpu.VMEM((2, 32, 128), F32),
            pltpu.VMEM((2, 32, 128), F32),
            pltpu.VMEM((2, 16, 256), F32),
            pltpu.VMEM((16, 48, 512), BF16),
            pltpu.VMEM((16, 48, 512), BF16),
            pltpu.VMEM((2, 48, 512), F32),
            pltpu.VMEM((8, 128, 128), F32),
            pltpu.VMEM((8, 128, 128), F32),
            pltpu.VMEM((8, 128, 128), F32),
            pltpu.VMEM((16, 8, 128), F32),
            dma((13,)), dma((4, 8)), dma((4, 8)), dma((16,)), dma((16,)), dma((16,)), dma((16,)),
            dma((2,)), dma((16,)), dma((16,)), dma((8,)), dma((8,)), dma((8,)), dma((8,)),
            dma((16,)), dma((16,)), dma((6,)), dma((6,)), dma((4,)), dma((4,)),
        ],
        compiler_params=pltpu.CompilerParams(
            collective_id=0, has_side_effects=True, vmem_limit_bytes=60 * 1024 * 1024
        ),
        cost_estimate=pl.CostEstimate(
            flops=13_000_000_000, bytes_accessed=30_000_000, transcendentals=0
        ),
        name="exchange",
    )(grad, dlow, low, hot, x, dsel, wq, wk, wv, *pieces)


def weight_pieces(w_query, w_key, w_value):
    x = lax.axis_index("tensor") % 4
    core = lax.axis_index("dp") % 2
    w_kv = jnp.concatenate([w_key, w_value], axis=1)

    def rows(w, block, skip, count):
        return lax.dynamic_slice_in_dim(w, block * BLOCK_D + core * 1024 + skip, count, 0)

    def swap(value, axis, mask):
        pairs = [(i, i ^ mask) for i in range(lax.axis_size(axis))]
        return lax.ppermute(value, axis, pairs)

    two, three = (x + 2) % 4, 3 - x
    sent = [
        rows(w_query, x + 1 - 2 * (x % 2), 0, 1024),
        jnp.concatenate([rows(w_query, two, 0, 1024), rows(w_kv, two, 0, 512)], axis=0),
        jnp.concatenate([rows(w_query, three, 0, 1024), rows(w_kv, three, 512, 512)], axis=0),
    ]
    got = [swap(value, "tensor", mask) for value, mask in zip(sent, (1, 2, 3))]
    return got + [swap(value, "dp", 1) for value in got]


def per_device(
    x_rows, d_attn, q_saved, k_saved, v_saved, w_query, w_key, w_value, down_all, up_query, up_kv,
    tenant, doc_starts,
):
    pieces = weight_pieces(w_query, w_key, w_value)
    grad, dlow, low, hot, dsel = attention_call(
        tenant, doc_starts, q_saved, k_saved, v_saved, d_attn, x_rows, down_all, up_query, up_kv
    )
    return tuple(
        exchange_call(grad, dlow, low, hot, x_rows, dsel, w_query, w_key, w_value, pieces)
    )


def solution(mesh):
    in_specs = (
        P(("dp", "tensor"), None),
        P("dp", "tensor"),
        P("dp", "tensor"),
        P("dp", "tensor"),
        P("dp", "tensor"),
        P(None, "tensor"),
        P(None, "tensor"),
        P(None, "tensor"),
        P(),
        P(None, None, "tensor"),
        P(None, None, "tensor"),
        P("dp"),
        P("dp", None),
    )
    out_specs = (
        P(("dp", "tensor"), None),
        P(None, None, "tensor"),
        P(None, None, "tensor"),
        P(None, None, "tensor"),
    )
    return jax.shard_map(
        per_device, mesh=mesh, in_specs=in_specs, out_specs=out_specs, check_vma=False
    )
```

```python
import functools
import math
import numpy as np
import jax
import jax.numpy as jnp
from jax import lax
from jax.experimental import pallas as pl
from jax.experimental.pallas import tpu as pltpu
from jax.sharding import PartitionSpec as P

HD = 128
RANK = 16
TEN = 4
SEQ = 1024
ROPE_BASE = 500000.0
NORM_EPS = 1e-06
MASKED = -1e30
NT = (((1,), (1,)), ((), ()))
TN = (((0,), (0,)), ((), ()))
F32 = jnp.float32
BF16 = jnp.bfloat16
ROWS = 256


def rope_constants():
    half = HD // 2
    freq = ROPE_BASE ** (-(2.0 * np.arange(half)) / HD)
    angle = np.arange(SEQ)[:, None] * freq[None, :]
    cosine = np.concatenate([np.cos(angle), np.cos(angle)], axis=1)
    sine = np.concatenate([np.sin(angle), -np.sin(angle)], axis=1)
    return cosine.astype(np.float32), sine.astype(np.float32)


MESH_ID = pl.DeviceIdType.MESH
CHUNK = 256
SUB = 128
QUARTER = 512
BLOCK_D = 2048
ORDER = ((2, 0), (1, 0), (3, 0), (0, 0), (2, 1), (1, 1), (3, 1), (0, 1))


def fused_kernel(
    tenant_ref, doc_ref, q_ref, k_ref, v_ref, g_ref, x_ref, down_ref, upq_ref, upkv_ref,
    cos_ref, sin_ref, wq_ref, wk_ref, wv_ref,
    out_ref, ud_ref, uq_ref, ukv_ref,
    grad_ref, dlow_ref, low_ref, hot_ref, kt_ref, vt_ref, dk_ref, dv_ref, c_ref, s_ref,
    gall, a_ref, wx, part, zbuf, fbuf, fin,
    dlall, lowall, lowcat, dlw_ref, kvown, kvpeer, qown, gdown, gdall, dsum,
    rsbuf, rsall, agbuf, sqall,
    wsem, wxsend, wxrecv, wysend, wyrecv, wcsend, wcrecv,
    gsend, grecv, dlsend, dlrecv, lowsend, lowrecv, kvsem, dnsend, dnrecv,
    rssend, rsrecv, agsend, agrecv, sqsend, sqrecv, zsend, zrecv, fsend, frecv,
):
    me_dp = lax.axis_index("dp")
    me_t = lax.axis_index("tensor")
    z = me_t // 4
    x = me_t % 4
    core = me_dp % 2
    xr, xl, xo = (x + 1) % 4, (x + 3) % 4, (x + 2) % 4
    pair = x + 1 - 2 * (x % 2)
    mirror = 3 - x
    z_right = ((z + 1) % 4) * 4 + x
    z_left = ((z + 3) % 4) * 4 + x

    def remote(src, dst, ssem, rsem, dp, t):
        return pltpu.make_async_remote_copy(
            src_ref=src, dst_ref=dst, send_sem=ssem, recv_sem=rsem,
            device_id=(dp, t), device_id_type=MESH_ID,
        )

    barrier = pltpu.get_barrier_semaphore()

    def greet_tensor(o, c):
        pl.semaphore_signal(
            barrier, inc=1, device_id=(me_dp, (me_t + o) % 16), device_id_type=MESH_ID
        )
        return c

    def greet_dp(o, c):
        pl.semaphore_signal(
            barrier, inc=1, device_id=((me_dp + o) % 8, me_t), device_id_type=MESH_ID
        )
        return c

    lax.fori_loop(1, 16, greet_tensor, 0)
    lax.fori_loop(1, 8, greet_dp, 0)

    y = me_dp // 2
    kv_here = 4 + x // 2
    kv_there = 5 - x // 2
    blocks = (pair, xo, mirror, kv_there)
    my_part = core * 1024 + y * 256
    d0 = pl.multiple_of(x * BLOCK_D, BLOCK_D)

    def rows_at(start, count):
        return pl.ds(pl.multiple_of(start, count), count)

    w_own = [
        pltpu.make_async_copy(src, dst, wsem.at[i])
        for i, (src, dst) in enumerate((
            (wq_ref.at[pl.ds(d0, BLOCK_D), :], wx.at[x]),
            (wk_ref.at[pl.ds(d0, BLOCK_D), :], wx.at[kv_here, :, pl.ds(0, 128)]),
            (wv_ref.at[pl.ds(d0, BLOCK_D), :], wx.at[kv_here, :, pl.ds(128, 128)]),
        ))
    ]

    def weights_x(sending):
        copies = []
        for i, xs in enumerate((pair, xo, mirror)):
            if sending:
                src = wq_ref.at[rows_at(xs * BLOCK_D + my_part, 256), :]
                dst = wx.at[x, rows_at(my_part, 256), :]
            else:
                src = dst = wx.at[xs, rows_at(my_part, 256), :]
            copies.append(remote(src, dst, wxsend.at[i], wxrecv.at[i], me_dp, z * 4 + xs))
        for i, xs in enumerate((xo, mirror)):
            for n, w in enumerate((wk_ref, wv_ref)):
                lanes = pl.ds(128 * n, 128)
                if sending:
                    row = my_part + (x % 2) * 128
                    src = w.at[rows_at(xs * BLOCK_D + row, 128), :]
                    dst = wx.at[kv_here, rows_at(row, 128), lanes]
                else:
                    row = my_part + (xs % 2) * 128
                    src = dst = wx.at[kv_there, rows_at(row, 128), lanes]
                k = 3 + 2 * i + n
                copies.append(remote(src, dst, wxsend.at[k], wxrecv.at[k], me_dp, z * 4 + xs))
        return copies

    def weights_y(sending):
        copies = []
        for i, b in enumerate(blocks):
            for o in range(1, 4):
                at_y = y if sending else (y + 4 - o) % 4
                ref = wx.at[b, rows_at(core * 1024 + at_y * 256, 256), :]
                to = ((y + o) % 4) * 2 + core
                copies.append(
                    remote(ref, ref, wysend.at[i, o - 1], wyrecv.at[i, o - 1], to, me_t)
                )
        return copies

    def weights_core(sending):
        copies = []
        for i, b in enumerate(blocks):
            at_core = core if sending else 1 - core
            ref = wx.at[b, rows_at(at_core * 1024, 1024), :]
            to = me_dp + 1 - 2 * core
            copies.append(remote(ref, ref, wcsend.at[i], wcrecv.at[i], to, me_t))
        return copies

    pl.semaphore_wait(barrier, 22)
    for copy in weights_x(True) + w_own:
        copy.start()

    def first_row(c):
        off, half = ORDER[c]
        return pl.multiple_of(((z + off) % 4) * QUARTER + half * CHUNK, CHUNK)

    def gather_out(c):
        rows = pl.ds(first_row(c), CHUNK)
        src = grad_ref.at[rows, :]
        dst = gall.at[x, rows, :]
        return (
            remote(src, dst, gsend.at[0, c], grecv.at[0, c], me_dp, z * 4 + xr),
            remote(src, dst, gsend.at[1, c], grecv.at[1, c], me_dp, z * 4 + xl),
        )

    def gather_in(c):
        rows = pl.ds(first_row(c), CHUNK)
        from_l = gall.at[xl, rows, :]
        from_r = gall.at[xr, rows, :]
        return (
            remote(from_l, from_l, gsend.at[0, c], grecv.at[0, c], me_dp, z * 4 + xr),
            remote(from_r, from_r, gsend.at[1, c], grecv.at[1, c], me_dp, z * 4 + xl),
        )

    def forward_out(c):
        r0 = first_row(c)
        to_r = gall.at[xl, pl.ds(r0, CHUNK // 2), :]
        to_l = gall.at[xr, pl.ds(pl.multiple_of(r0 + CHUNK // 2, CHUNK // 2), CHUNK // 2), :]
        return (
            remote(to_r, to_r, gsend.at[2, c], grecv.at[2, c], me_dp, z * 4 + xr),
            remote(to_l, to_l, gsend.at[3, c], grecv.at[3, c], me_dp, z * 4 + xl),
        )

    def forward_in(c):
        r0 = first_row(c)
        from_l = gall.at[xo, pl.ds(r0, CHUNK // 2), :]
        from_r = gall.at[xo, pl.ds(pl.multiple_of(r0 + CHUNK // 2, CHUNK // 2), CHUNK // 2), :]
        return (
            remote(from_l, from_l, gsend.at[2, c], grecv.at[2, c], me_dp, z * 4 + xr),
            remote(from_r, from_r, gsend.at[3, c], grecv.at[3, c], me_dp, z * 4 + xl),
        )

    def start(copies):
        for copy in copies:
            copy.start()

    def arrive(c):
        for copy in gather_in(c):
            copy.wait_recv()
        start(forward_out(c))

    def to_tensor(src, buf, ssem, rsem, picked):
        def descriptor(t):
            return remote(
                src.at[t] if picked else src, buf.at[me_t], ssem.at[t], rsem.at[me_t], me_dp, t
            )

        def begin(o, c):
            descriptor((me_t + o) % 16).start()
            return c

        def receive(o, c):
            t = (me_t + o) % 16
            remote(buf.at[t], buf.at[t], ssem.at[t], rsem.at[t], me_dp, t).wait_recv()
            return c

        def sent(o, c):
            descriptor((me_t + o) % 16).wait_send()
            return c

        return (
            lambda: lax.fori_loop(1, 16, begin, 0),
            lambda: lax.fori_loop(1, 16, receive, 0),
            lambda: lax.fori_loop(1, 16, sent, 0),
        )

    def to_dp(src_at, buf, ssem, rsem):
        def descriptor(d):
            return remote(src_at(d), buf.at[me_dp], ssem.at[d], rsem.at[me_dp], d, me_t)

        def begin(o, c):
            descriptor((me_dp + o) % 8).start()
            return c

        def receive(o, c):
            d = (me_dp + o) % 8
            remote(buf.at[d], buf.at[d], ssem.at[d], rsem.at[d], d, me_t).wait_recv()
            return c

        def sent(o, c):
            descriptor((me_dp + o) % 8).wait_send()
            return c

        return (
            lambda: lax.fori_loop(1, 8, begin, 0),
            lambda: lax.fori_loop(1, 8, receive, 0),
            lambda: lax.fori_loop(1, 8, sent, 0),
        )

    dl_start, dl_recv, dl_sent = to_tensor(dlow_ref, dlall, dlsend, dlrecv, True)
    low_start, low_recv, low_sent = to_tensor(low_ref, lowall, lowsend, lowrecv, False)
    dn_start, dn_recv, dn_sent = to_tensor(gdown, gdall, dnsend, dnrecv, True)
    sq_start, sq_recv, sq_sent = to_tensor(sqall.at[me_t], sqall, sqsend, sqrecv, False)
    rs_start, rs_recv, rs_sent = to_dp(lambda d: rsbuf.at[d], rsall, rssend, rsrecv)
    ag_start, ag_recv, ag_sent = to_dp(lambda d: agbuf.at[me_dp], agbuf, agsend, agrecv)
    kv_copy = remote(kvown, kvpeer, kvsem.at[0], kvsem.at[1], me_dp, z * 4 + pair)

    for s in range(2):
        for t in range(TEN):
            hot_ref[4 * s + t : 4 * s + t + 1, :] = jnp.where(
                jnp.full((1, 128), tenant_ref[s]) == t, 1.0, 0.0
            )
    own = tenant_ref[me_t // 8]
    low_ref[...] = lax.dot_general(
        down_ref[own], x_ref[...], NT, preferred_element_type=F32
    ).astype(BF16)
    low_start()

    scale = HD ** (-0.5)
    scale2 = scale * math.log2(math.e)

    def sequence(turn, carry):
        s = (1 - z // 2 + turn) % 2
        base = pl.multiple_of(s * SEQ, SEQ)
        starts = [doc_ref[s, j] for j in range(4)]
        pos = lax.broadcasted_iota(jnp.int32, (SEQ, HD), 0)
        cb = jnp.broadcast_to(cos_ref[pl.ds(starts[0], 1), :], (SEQ, HD))
        sb = jnp.broadcast_to(sin_ref[pl.ds(starts[0], 1), :], (SEQ, HD))
        for j in range(1, 4):
            inside = pos >= starts[j]
            cb = jnp.where(inside, cos_ref[pl.ds(starts[j], 1), :], cb)
            sb = jnp.where(inside, sin_ref[pl.ds(starts[j], 1), :], sb)
        cp = cos_ref[...]
        sp = sin_ref[...]
        c_ref[...] = cp * cb + sp * sb
        s_ref[...] = sp * cb - cp * sb
        kt_ref[...] = k_ref[pl.ds(base, SEQ), :].T
        vt_ref[...] = v_ref[pl.ds(base, SEQ), :].T
        dk_ref[...] = jnp.zeros_like(dk_ref)
        dv_ref[...] = jnp.zeros_like(dv_ref)
        for h in range(2):
            cols = slice(h * HD, (h + 1) * HD)
            for i in range(SEQ // ROWS):
                width = (i + 1) * ROWS
                rows = pl.ds(base + i * ROWS, ROWS)
                keys = pl.ds(base, width)
                q = q_ref[rows, cols]
                g = g_ref[rows, cols]
                p_row = lax.broadcasted_iota(jnp.int32, (1, ROWS), 1) + i * ROWS
                begin = jnp.zeros((1, ROWS), jnp.int32)
                for j in range(1, 4):
                    begin = jnp.where(p_row >= starts[j], starts[j], begin)
                k_idx = lax.broadcasted_iota(jnp.int32, (width, ROWS), 0)
                allowed = (k_idx >= begin) & (k_idx <= p_row)
                st = lax.dot_general(k_ref[keys, :], q, NT, preferred_element_type=F32)
                st = jnp.where(allowed, st * scale2, MASKED)
                top = jnp.max(st, axis=0, keepdims=True)
                e = jnp.exp2(st - top)
                inv = 1.0 / jnp.sum(e, axis=0, keepdims=True)
                p = e * inv
                p_low = p.astype(BF16)
                ot = jnp.dot(vt_ref[:, :width], p_low, preferred_element_type=F32)
                delta = jnp.sum(g.astype(F32).T * ot, axis=0, keepdims=True)
                dpt = lax.dot_general(v_ref[keys, :], g, NT, preferred_element_type=F32)
                ds_low = (p * (dpt - delta)).astype(BF16)
                dqt = jnp.dot(kt_ref[:, :width], ds_low, preferred_element_type=F32)
                dk_ref[:width, :] += jnp.dot(ds_low, q, preferred_element_type=F32)
                dv_ref[:width, :] += jnp.dot(p_low, g, preferred_element_type=F32)
                dq = dqt.T * scale
                dq = dq * c_ref[i * ROWS : (i + 1) * ROWS, :] + pltpu.roll(
                    dq, HD // 2, 1
                ) * s_ref[i * ROWS : (i + 1) * ROWS, :]
                grad_ref[rows, cols] = dq.astype(BF16)
            if h == 0:

                @pl.when(turn == 0)
                def _():
                    incoming = weights_x(False)
                    outgoing = weights_y(True)
                    for n in range(4):
                        for copy in [incoming[n]] if n < 3 else incoming[3:]:
                            copy.wait_recv()
                        start(outgoing[3 * n : 3 * n + 3])

        dk = dk_ref[...] * scale
        dk = dk * c_ref[...] + pltpu.roll(dk, HD // 2, 1) * s_ref[...]
        grad_ref[pl.ds(base, SEQ), 2 * HD : 3 * HD] = dk.astype(BF16)
        grad_ref[pl.ds(base, SEQ), 3 * HD : 4 * HD] = dv_ref[...].astype(BF16)
        t = tenant_ref[s]
        seq_rows = pl.ds(base, SEQ)
        parts = [
            (upq_ref[t], slice(0, 2 * HD)),
            (upkv_ref[t, :RANK, :], slice(2 * HD, 3 * HD)),
            (upkv_ref[t, RANK:, :], slice(3 * HD, 4 * HD)),
        ]
        for n, (up, c) in enumerate(parts):
            back = 2.0 * lax.dot_general(
                up, grad_ref[seq_rows, c], NT, preferred_element_type=F32
            )
            for b in range(8):
                dlow_ref[s * 8 + b, n * RANK : (n + 1) * RANK, :] = back[:, b * 128 : (b + 1) * 128]

        @pl.when(turn == 0)
        def _():
            start(gather_out(0))

        return carry

    lax.fori_loop(0, 2, sequence, 0)

    dl_start()
    start(gather_out(1))
    start(gather_out(2))
    dlall[me_t] = dlow_ref[me_t]
    lowall[me_t] = low_ref[...]
    gall[x] = grad_ref[...]

    def step_low():
        low_recv()
        for b in range(16):
            lowcat[:, b * 128 : (b + 1) * 128] = lowall[b]
        for s in range(2):
            rows = slice(s * SEQ, (s + 1) * SEQ)
            qown[s] = 2.0 * jnp.dot(
                lowcat[:RANK, rows], grad_ref[rows, 0:256], preferred_element_type=F32
            )
            kvown[s, :RANK, :] = 2.0 * jnp.dot(
                lowcat[RANK : 2 * RANK, rows], grad_ref[rows, 256:384], preferred_element_type=F32
            )
            kvown[s, RANK:, :] = 2.0 * jnp.dot(
                lowcat[2 * RANK :, rows], grad_ref[rows, 384:512], preferred_element_type=F32
            )
        kv_copy.start()

    def step_dlow():
        dl_recv()
        total = dlall[0]
        for b in range(1, 16):
            total = total + dlall[b]
        dlw_ref[...] = total.astype(BF16)

        def column(t, c):
            gdown[t] = jnp.dot(
                dlw_ref[...], x_ref[:, pl.ds(pl.multiple_of(t * 512, 512), 512)],
                preferred_element_type=F32,
            ).astype(BF16)
            return c

        lax.fori_loop(0, 16, column, 0)
        dn_start()
        gdall[me_t] = gdown[me_t]

    def step_down():
        dn_recv()
        kv_copy.wait_recv()
        for s in range(2):
            total = gdall[8 * s].astype(F32)
            for b in range(1, 8):
                total = total + gdall[8 * s + b].astype(F32)
            dsum[s] = total
            kvown_sum = kvown[s] + kvpeer[s]
            kvpeer[s] = kvown_sum
        for j in range(8):
            cb = j % 4
            for i in range(2):
                t = 2 * (j // 4) + i
                rsbuf[j, 48 * i : 48 * (i + 1), :] = (
                    dsum[0, :, cb * 128 : (cb + 1) * 128] * hot_ref[t : t + 1, :]
                    + dsum[1, :, cb * 128 : (cb + 1) * 128] * hot_ref[4 + t : 5 + t, :]
                )
            t = j // 2
            c = j % 2
            rsbuf[j, 96:112, :] = (
                qown[0, :, c * 128 : (c + 1) * 128] * hot_ref[t : t + 1, :]
                + qown[1, :, c * 128 : (c + 1) * 128] * hot_ref[4 + t : 5 + t, :]
            )
            rsbuf[j, 112:128, :] = (
                kvpeer[0, c * 16 : (c + 1) * 16, :] * hot_ref[t : t + 1, :]
                + kvpeer[1, c * 16 : (c + 1) * 16, :] * hot_ref[4 + t : 5 + t, :]
            )
        rs_start()
        rsall[me_dp] = rsbuf[me_dp]

    def step_reduce():
        rs_recv()
        total = rsall[0]
        for b in range(1, 8):
            total = total + rsall[b]
        agbuf[me_dp] = total
        ag_start()

    def parts_of(t):
        for n in range(3):
            lo = (t % 2) * 48 + n * 16
            yield [(t // 2) * 4 + cb for cb in range(4)], slice(lo, lo + 16)
        yield [2 * t, 2 * t + 1], slice(96, 112)
        yield [2 * t], slice(112, 128)
        yield [2 * t + 1], slice(112, 128)

    def step_squares():
        ag_recv()
        row = lax.broadcasted_iota(jnp.int32, (8, 128), 0)
        lane = lax.broadcasted_iota(jnp.int32, (8, 128), 1)
        tile = jnp.zeros((8, 128), F32)
        for t in range(TEN):
            for n, (pieces, rows) in enumerate(parts_of(t)):
                total = None
                for j in pieces:
                    v = agbuf[j, rows, :]
                    total = v * v if total is None else total + v * v
                value = jnp.sum(
                    jnp.sum(total, axis=0, keepdims=True), axis=1, keepdims=True
                )
                tile = jnp.where((row == t) & (lane == n), value, tile)
        sqall[me_t] = tile
        sq_start()

    def step_update():
        sq_recv()
        total = sqall[0]
        for b in range(1, 16):
            total = total + sqall[b]
        for t in range(TEN):
            for n, (pieces, rows) in enumerate(parts_of(t)):
                count = RANK * (8192 if n < 3 else 4096 if n == 3 else 2048)
                factor = 1.0 / jnp.sqrt(total[t : t + 1, n : n + 1] * (1.0 / count) + NORM_EPS)
                for i, j in enumerate(pieces):
                    value = agbuf[j, rows, :] * factor
                    if n < 3:
                        ud_ref[t, n * 16 : (n + 1) * 16, i * 128 : (i + 1) * 128] = value
                    elif n == 3:
                        uq_ref[t, :, i * 128 : (i + 1) * 128] = value
                    else:
                        ukv_ref[t, (n - 4) * 16 : (n - 3) * 16, :] = value

    def product(c, write, added):
        rows = pl.ds(first_row(c), CHUNK)
        for b in range(4):
            a_ref[b] = gall[b, rows, 0:256]
        for b in range(2):
            a_ref[4 + b] = (
                gall[2 * b, rows, 256:512].astype(F32) + gall[2 * b + 1, rows, 256:512].astype(F32)
            ).astype(BF16)

        def tile(n, carry):
            cols = pl.ds(pl.multiple_of(n * 512, 512), 512)
            acc = lax.dot_general(a_ref[0], wx[0, cols, :], NT, preferred_element_type=F32)
            for b in range(1, 6):
                acc = acc + lax.dot_general(
                    a_ref[b], wx[b, cols, :], NT, preferred_element_type=F32
                )
            write(cols, acc, added)
            return carry

        lax.fori_loop(0, 4, tile, 0)

    def z_copy(h, side, n):
        return remote(
            part.at[h, side, n], zbuf.at[h, side, n], zsend.at[h, side, n], zrecv.at[h, side, n],
            me_dp, z_left if side else z_right,
        )

    def to_far(h):
        def write(cols, acc, added):
            part[h, 0, 0, :, cols] = acc[:SUB].astype(BF16)
            part[h, 1, 0, :, cols] = acc[SUB:].astype(BF16)

        return write

    def to_near(h, side):
        def write(cols, acc, added):
            part[h, side, 2 - side, :, cols] = acc[:SUB].astype(BF16)
            part[h, side, 1 + side, :, cols] = acc[SUB:].astype(BF16)

        return write

    def to_final(h):
        def write(cols, acc, added):
            for i in range(2):
                total = acc[i * SUB : (i + 1) * SUB]
                for ref in added[i]:
                    total = total + ref[:, cols].astype(F32)
                fbuf[2 * h + i, :, cols] = total.astype(BF16)

        return write

    def add_far(h, side):
        z_copy(h, side, 0).wait_recv()
        for n in range(4):
            cols = slice(n * 512, (n + 1) * 512)
            part[h, side, 2, :, cols] = (
                part[h, side, 2, :, cols].astype(F32) + zbuf[h, side, 0, :, cols].astype(F32)
            ).astype(BF16)
        z_copy(h, side, 2).start()

    def final_copy(o):
        return remote(fbuf.at[o], fin.at[x], fsend.at[o], frecv.at[x], me_dp, z * 4 + o)

    def finish(c):
        h = ORDER[c][1]
        for side in range(2):
            for n in (1, 2):
                z_copy(h, side, n).wait_recv()
        product(
            c, to_final(h),
            ((zbuf.at[h, 0, 2], zbuf.at[h, 1, 1]), (zbuf.at[h, 0, 1], zbuf.at[h, 1, 2])),
        )
        for o in (2 * h, 2 * h + 1):

            @pl.when(x != o)
            def _(o=o):
                final_copy(o).start()

    def step_output():
        for n in range(16):
            cols = slice(n * 512, (n + 1) * 512)
            out_ref[:, cols] = lax.dot_general(
                dlw_ref[...], down_ref[own, :, cols], TN, preferred_element_type=F32
            ).astype(BF16)

    def ready(c):
        for copy in forward_in(c):
            copy.wait_recv()

    arrive(0)
    start(gather_out(3))
    step_dlow()
    incoming = weights_y(False)
    outgoing = weights_core(True)
    for n in range(4):
        for copy in incoming[3 * n : 3 * n + 3]:
            copy.wait_recv()
        outgoing[n].start()
    arrive(1)
    start(gather_out(4))
    for copy in w_own:
        copy.wait()
    for copy in weights_core(False):
        copy.wait_recv()
    for h in range(2):
        c = 4 * h
        ready(c)
        product(c, to_far(h), None)
        z_copy(h, 0, 0).start()
        z_copy(h, 1, 0).start()
        for side in range(2):
            arrive(c + 2 + side)
            if c + 5 + side < 8:
                start(gather_out(c + 5 + side))
            ready(c + 1 + side)
            product(c + 1 + side, to_near(h, side), None)
            z_copy(h, side, 1).start()
        (step_low, step_reduce)[h]()
        add_far(h, 0)
        add_far(h, 1)
        if h == 0:
            arrive(4)
            start(gather_out(7))
            step_down()
            arrive(5)
            step_output()
        else:
            step_squares()
        ready(c + 3)
        finish(c + 3)

    step_update()
    fin[x] = fbuf[x]
    for o in range(1, 4):
        xs = (x + o) % 4
        remote(fin.at[xs], fin.at[xs], fsend.at[xs], frecv.at[xs], me_dp, z * 4 + xs).wait_recv()
    for b in range(4):
        cols = slice(b * BLOCK_D, (b + 1) * BLOCK_D)
        out_ref[:, cols] = (fin[b].astype(F32) + out_ref[:, cols].astype(F32)).astype(BF16)

    for c in range(8):
        for copy in gather_out(c) + forward_out(c):
            copy.wait_send()
    for copy in weights_x(True) + weights_y(True) + weights_core(True):
        copy.wait_send()
    for sent in (dl_sent, low_sent, dn_sent, sq_sent, rs_sent, ag_sent):
        sent()
    kv_copy.wait_send()
    for h in range(2):
        for side in range(2):
            for n in range(3):
                z_copy(h, side, n).wait_send()
    for o in range(4):

        @pl.when(x != o)
        def _(o=o):
            final_copy(o).wait_send()


def fused_call(tenant, docs, q, k, v, g, x, down, upq, upkv, wq, wk, wv):
    vmem = pl.BlockSpec(memory_space=pltpu.VMEM)
    smem = pl.BlockSpec(memory_space=pltpu.SMEM)
    hbm = pl.BlockSpec(memory_space=pl.ANY)
    dma = pltpu.SemaphoreType.DMA
    tokens = q.shape[0]
    cosine, sine = rope_constants()
    return pl.pallas_call(
        fused_kernel,
        in_specs=[smem] * 2 + [vmem] * 10 + [hbm] * 3,
        out_specs=[vmem] * 4,
        out_shape=[
            jax.ShapeDtypeStruct(x.shape, BF16),
            jax.ShapeDtypeStruct((TEN, 48, 512), F32),
            jax.ShapeDtypeStruct((TEN, RANK, 256), F32),
            jax.ShapeDtypeStruct((TEN, 2 * RANK, 128), F32),
        ],
        scratch_shapes=[
            pltpu.VMEM((tokens, 512), BF16),
            pltpu.VMEM((16, 48, 128), F32),
            pltpu.VMEM((48, 128), BF16),
            pltpu.VMEM((8, 128), F32),
            pltpu.VMEM((HD, SEQ), BF16), pltpu.VMEM((HD, SEQ), BF16),
            pltpu.VMEM((SEQ, HD), F32), pltpu.VMEM((SEQ, HD), F32),
            pltpu.VMEM((SEQ, HD), F32), pltpu.VMEM((SEQ, HD), F32),
            pltpu.VMEM((4, tokens, 512), BF16),
            pltpu.VMEM((6, CHUNK, 256), BF16),
            pltpu.VMEM((6, BLOCK_D, 256), BF16),
            pltpu.VMEM((2, 2, 3, SUB, BLOCK_D), BF16),
            pltpu.VMEM((2, 2, 3, SUB, BLOCK_D), BF16),
            pltpu.VMEM((4, SUB, BLOCK_D), BF16),
            pltpu.VMEM((4, SUB, BLOCK_D), BF16),
            pltpu.VMEM((16, 48, 128), F32),
            pltpu.VMEM((16, 48, 128), BF16),
            pltpu.VMEM((48, tokens), BF16),
            pltpu.VMEM((48, 128), BF16),
            pltpu.VMEM((2, 32, 128), F32),
            pltpu.VMEM((2, 32, 128), F32),
            pltpu.VMEM((2, 16, 256), F32),
            pltpu.VMEM((16, 48, 512), BF16),
            pltpu.VMEM((16, 48, 512), BF16),
            pltpu.VMEM((2, 48, 512), F32),
            pltpu.VMEM((8, 128, 128), F32),
            pltpu.VMEM((8, 128, 128), F32),
            pltpu.VMEM((8, 128, 128), F32),
            pltpu.VMEM((16, 8, 128), F32),
            dma((3,)), dma((7,)), dma((7,)), dma((4, 3)), dma((4, 3)), dma((4,)), dma((4,)),
            dma((4, 8)), dma((4, 8)), dma((16,)), dma((16,)), dma((16,)), dma((16,)),
            dma((2,)), dma((16,)), dma((16,)), dma((8,)), dma((8,)), dma((8,)), dma((8,)),
            dma((16,)), dma((16,)), dma((2, 2, 3)), dma((2, 2, 3)), dma((4,)), dma((4,)),
        ],
        compiler_params=pltpu.CompilerParams(
            collective_id=0, has_side_effects=True, vmem_limit_bytes=63 * 1024 * 1024
        ),
        cost_estimate=pl.CostEstimate(
            flops=20_000_000_000, bytes_accessed=40_000_000, transcendentals=4_000_000
        ),
        name="exchange",
    )(tenant, docs, q, k, v, g, x, down, upq, upkv, cosine, sine, wq, wk, wv)


def per_device(
    x_rows, d_attn, q_saved, k_saved, v_saved, w_query, w_key, w_value, down_all, up_query, up_kv,
    tenant, doc_starts,
):
    return tuple(
        fused_call(
            tenant, doc_starts, q_saved, k_saved, v_saved, d_attn, x_rows, down_all, up_query,
            up_kv, w_query, w_key, w_value,
        )
    )


def solution(mesh):
    in_specs = (
        P(("dp", "tensor"), None),
        P("dp", "tensor"),
        P("dp", "tensor"),
        P("dp", "tensor"),
        P("dp", "tensor"),
        P(None, "tensor"),
        P(None, "tensor"),
        P(None, "tensor"),
        P(),
        P(None, None, "tensor"),
        P(None, None, "tensor"),
        P("dp"),
        P("dp", None),
    )
    out_specs = (
        P(("dp", "tensor"), None),
        P(None, None, "tensor"),
        P(None, None, "tensor"),
        P(None, None, "tensor"),
    )
    return jax.shard_map(
        per_device, mesh=mesh, in_specs=in_specs, out_specs=out_specs, check_vma=False
    )
```

```python
import functools
import math
import numpy as np
import jax
import jax.numpy as jnp
from jax import lax
from jax.experimental import pallas as pl
from jax.experimental.pallas import tpu as pltpu
from jax.sharding import PartitionSpec as P

HD = 128
RANK = 16
TEN = 4
SEQ = 1024
ROPE_BASE = 500000.0
NORM_EPS = 1e-06
MASKED = -1e30
NT = (((1,), (1,)), ((), ()))
TN = (((0,), (0,)), ((), ()))
F32 = jnp.float32
BF16 = jnp.bfloat16
ROWS = 256


def rope_constants():
    half = HD // 2
    freq = ROPE_BASE ** (-(2.0 * np.arange(half)) / HD)
    angle = np.arange(SEQ)[:, None] * freq[None, :]
    cosine = np.concatenate([np.cos(angle), np.cos(angle)], axis=1)
    sine = np.concatenate([np.sin(angle), -np.sin(angle)], axis=1)
    return cosine.astype(np.float32), sine.astype(np.float32)


MESH_ID = pl.DeviceIdType.MESH
CHUNK = 256
SUB = 128
QUARTER = 512
BLOCK_D = 2048
ORDER = ((2, 0), (1, 0), (3, 0), (2, 1), (1, 1), (3, 1), (0, 0), (0, 1))


def fused_kernel(
    tenant_ref, doc_ref, q_ref, k_ref, v_ref, g_ref, x_hbm, down_hbm, upq_ref, upkv_ref,
    cos_ref, sin_ref, wq_ref, wk_ref, wv_ref,
    out_ref, ud_ref, uq_ref, ukv_ref,
    grad_ref, dlow_ref, low_ref, hot_ref, kt_ref, vt_ref, dk_ref, dv_ref, c_ref, s_ref,
    qall, kvs, kvp, kvm, wx, part, zbuf, own_ref, fbuf, fin,
    dlall, lowall, lowcat, dlw_ref, kvown, kvpeer, qown, gdown, gdall, dsum,
    rsbuf, rsall, agbuf, sqall, x_ref, down_ref,
    wsem, wxsend, wxrecv, wysend, wyrecv, wcsend, wcrecv,
    gsend, grecv, dlsend, dlrecv, lowsend, lowrecv, kvsem, dnsend, dnrecv,
    rssend, rsrecv, agsend, agrecv, sqsend, sqrecv, zsend, zrecv, fsend, frecv,
):
    me_dp = lax.axis_index("dp")
    me_t = lax.axis_index("tensor")
    z = me_t // 4
    x = me_t % 4
    core = me_dp % 2
    xo = (x + 2) % 4
    pair = x + 1 - 2 * (x % 2)
    mirror = 3 - x
    z_right = ((z + 1) % 4) * 4 + x
    z_left = ((z + 3) % 4) * 4 + x

    def remote(src, dst, ssem, rsem, dp, t):
        return pltpu.make_async_remote_copy(
            src_ref=src, dst_ref=dst, send_sem=ssem, recv_sem=rsem,
            device_id=(dp, t), device_id_type=MESH_ID,
        )

    barrier = pltpu.get_barrier_semaphore()

    def greet_tensor(o, c):
        pl.semaphore_signal(
            barrier, inc=1, device_id=(me_dp, (me_t + o) % 16), device_id_type=MESH_ID
        )
        return c

    def greet_dp(o, c):
        pl.semaphore_signal(
            barrier, inc=1, device_id=((me_dp + o) % 8, me_t), device_id_type=MESH_ID
        )
        return c

    lax.fori_loop(1, 16, greet_tensor, 0)
    lax.fori_loop(1, 8, greet_dp, 0)

    y = me_dp // 2
    kv_here = 4 + x // 2
    kv_there = 5 - x // 2
    blocks = (pair, xo, mirror, kv_there)
    my_part = core * 1024 + y * 256
    d0 = pl.multiple_of(x * BLOCK_D, BLOCK_D)

    def rows_at(start, count):
        return pl.ds(pl.multiple_of(start, count), count)

    w_own = [
        pltpu.make_async_copy(src, dst, wsem.at[i])
        for i, (src, dst) in enumerate((
            (wq_ref.at[pl.ds(d0, BLOCK_D), :], wx.at[x]),
            (wk_ref.at[pl.ds(d0, BLOCK_D), :], wx.at[kv_here, :, pl.ds(0, 128)]),
            (wv_ref.at[pl.ds(d0, BLOCK_D), :], wx.at[kv_here, :, pl.ds(128, 128)]),
            (x_hbm, x_ref),
            (down_hbm, down_ref),
        ))
    ]

    def weights_x(sending):
        copies = []
        for i, xs in enumerate((pair, xo, mirror)):
            if sending:
                src = wq_ref.at[rows_at(xs * BLOCK_D + my_part, 256), :]
                dst = wx.at[x, rows_at(my_part, 256), :]
            else:
                src = dst = wx.at[xs, rows_at(my_part, 256), :]
            copies.append(remote(src, dst, wxsend.at[i], wxrecv.at[i], me_dp, z * 4 + xs))
        for i, xs in enumerate((xo, mirror)):
            for n, w in enumerate((wk_ref, wv_ref)):
                lanes = pl.ds(128 * n, 128)
                if sending:
                    row = my_part + (x % 2) * 128
                    src = w.at[rows_at(xs * BLOCK_D + row, 128), :]
                    dst = wx.at[kv_here, rows_at(row, 128), lanes]
                else:
                    row = my_part + (xs % 2) * 128
                    src = dst = wx.at[kv_there, rows_at(row, 128), lanes]
                k = 3 + 2 * i + n
                copies.append(remote(src, dst, wxsend.at[k], wxrecv.at[k], me_dp, z * 4 + xs))
        return copies

    def weights_y(sending):
        copies = []
        for i, b in enumerate(blocks):
            for o in range(1, 4):
                at_y = y if sending else (y + 4 - o) % 4
                ref = wx.at[b, rows_at(core * 1024 + at_y * 256, 256), :]
                to = ((y + o) % 4) * 2 + core
                copies.append(
                    remote(ref, ref, wysend.at[i, o - 1], wyrecv.at[i, o - 1], to, me_t)
                )
        return copies

    def weights_core(sending):
        copies = []
        for i, b in enumerate(blocks):
            for o in range(4):
                at_y = (y + 4 - o) % 4
                at_core = core if sending else 1 - core
                ref = wx.at[b, rows_at(at_core * 1024 + at_y * 256, 256), :]
                to = me_dp + 1 - 2 * core
                copies.append(remote(ref, ref, wcsend.at[i, o], wcrecv.at[i, o], to, me_t))
        return copies

    pl.semaphore_wait(barrier, 22)
    for copy in weights_x(True) + w_own:
        copy.start()

    def first_row(c):
        off, half = ORDER[c]
        return pl.multiple_of(((z + off) % 4) * QUARTER + half * CHUNK, CHUNK)

    def gather(c, n, src, dst, to):
        return remote(src, dst, gsend.at[n, c], grecv.at[n, c], me_dp, z * 4 + to)

    def gather_out(c):
        rows = pl.ds(first_row(c), CHUNK)
        mine = qall.at[x, rows, :]
        return (
            gather(c, 0, mine, mine, pair),
            gather(c, 2, mine, mine, mirror),
            gather(c, 1, kvs.at[rows, :], kvp.at[rows, :], pair),
        )

    def gather_in(c):
        rows = pl.ds(first_row(c), CHUNK)
        refs = (qall.at[pair, rows, :], qall.at[mirror, rows, :], kvp.at[rows, :])
        return [gather(c, n, ref, ref, to) for n, ref, to in zip((0, 2, 1), refs, (pair, mirror, pair))]

    def half_rows(c, n):
        return pl.ds(pl.multiple_of(first_row(c) + n * SUB, SUB), SUB)

    def forward_out(c):
        to_pair = qall.at[mirror, half_rows(c, 0), :]
        to_mirror = qall.at[pair, half_rows(c, 1), :]
        summed = kvm.at[x // 2, pl.ds(first_row(c), CHUNK), :]
        return (
            gather(c, 3, to_pair, to_pair, pair),
            gather(c, 4, to_mirror, to_mirror, mirror),
            gather(c, 5, summed, summed, mirror),
        )

    def forward_in(c):
        refs = (
            qall.at[xo, half_rows(c, 0), :], qall.at[xo, half_rows(c, 1), :],
            kvm.at[1 - x // 2, pl.ds(first_row(c), CHUNK), :],
        )
        return [gather(c, 3 + n, ref, ref, to) for n, (ref, to) in enumerate(zip(refs, (pair, mirror, mirror)))]

    def start(copies):
        for copy in copies:
            copy.start()

    def arrive(c):
        for copy in gather_in(c):
            copy.wait_recv()
        rows = pl.ds(first_row(c), CHUNK)
        outgoing = forward_out(c)
        outgoing[0].start()
        outgoing[1].start()
        kvm[x // 2, rows, :] = (kvs[rows, :].astype(F32) + kvp[rows, :].astype(F32)).astype(BF16)
        outgoing[2].start()

    def to_tensor(src, buf, ssem, rsem, picked):
        def descriptor(t):
            return remote(
                src.at[t] if picked else src, buf.at[me_t], ssem.at[t], rsem.at[me_t], me_dp, t
            )

        def begin(o, c):
            descriptor((me_t + o) % 16).start()
            return c

        def receive(o, c):
            t = (me_t + o) % 16
            remote(buf.at[t], buf.at[t], ssem.at[t], rsem.at[t], me_dp, t).wait_recv()
            return c

        def sent(o, c):
            descriptor((me_t + o) % 16).wait_send()
            return c

        return (
            lambda: lax.fori_loop(1, 16, begin, 0),
            lambda: lax.fori_loop(1, 16, receive, 0),
            lambda: lax.fori_loop(1, 16, sent, 0),
        )

    def to_dp(src_at, buf, ssem, rsem):
        def descriptor(d):
            return remote(src_at(d), buf.at[me_dp], ssem.at[d], rsem.at[me_dp], d, me_t)

        def begin(o, c):
            descriptor((me_dp + o) % 8).start()
            return c

        def receive(o, c):
            d = (me_dp + o) % 8
            remote(buf.at[d], buf.at[d], ssem.at[d], rsem.at[d], d, me_t).wait_recv()
            return c

        def sent(o, c):
            descriptor((me_dp + o) % 8).wait_send()
            return c

        return (
            lambda: lax.fori_loop(1, 8, begin, 0),
            lambda: lax.fori_loop(1, 8, receive, 0),
            lambda: lax.fori_loop(1, 8, sent, 0),
        )

    dl_start, dl_recv, dl_sent = to_tensor(dlow_ref, dlall, dlsend, dlrecv, True)
    low_start, low_recv, low_sent = to_tensor(low_ref, lowall, lowsend, lowrecv, False)
    dn_start, dn_recv, dn_sent = to_tensor(gdown, gdall, dnsend, dnrecv, True)
    sq_start, sq_recv, sq_sent = to_tensor(sqall.at[me_t], sqall, sqsend, sqrecv, False)
    rs_start, rs_recv, rs_sent = to_dp(lambda d: rsbuf.at[d], rsall, rssend, rsrecv)
    ag_start, ag_recv, ag_sent = to_dp(lambda d: agbuf.at[me_dp], agbuf, agsend, agrecv)
    kv_copy = remote(kvown, kvpeer, kvsem.at[0], kvsem.at[1], me_dp, z * 4 + pair)

    for s in range(2):
        for t in range(TEN):
            hot_ref[4 * s + t : 4 * s + t + 1, :] = jnp.where(
                jnp.full((1, 128), tenant_ref[s]) == t, 1.0, 0.0
            )
    own = tenant_ref[me_t // 8]

    scale = HD ** (-0.5)
    scale2 = scale * math.log2(math.e)

    def sequence(turn, carry):
        s = (1 - z // 2 + turn) % 2
        base = pl.multiple_of(s * SEQ, SEQ)
        starts = [doc_ref[s, j] for j in range(4)]
        pos = lax.broadcasted_iota(jnp.int32, (SEQ, HD), 0)
        cb = jnp.broadcast_to(cos_ref[pl.ds(starts[0], 1), :], (SEQ, HD))
        sb = jnp.broadcast_to(sin_ref[pl.ds(starts[0], 1), :], (SEQ, HD))
        for j in range(1, 4):
            inside = pos >= starts[j]
            cb = jnp.where(inside, cos_ref[pl.ds(starts[j], 1), :], cb)
            sb = jnp.where(inside, sin_ref[pl.ds(starts[j], 1), :], sb)
        cp = cos_ref[...]
        sp = sin_ref[...]
        c_ref[...] = cp * cb + sp * sb
        s_ref[...] = sp * cb - cp * sb
        kt_ref[...] = k_ref[pl.ds(base, SEQ), :].T
        vt_ref[...] = v_ref[pl.ds(base, SEQ), :].T
        dk_ref[...] = jnp.zeros_like(dk_ref)
        dv_ref[...] = jnp.zeros_like(dv_ref)
        for h in range(2):
            cols = slice(h * HD, (h + 1) * HD)
            for i in range(SEQ // ROWS):
                width = (i + 1) * ROWS
                rows = pl.ds(base + i * ROWS, ROWS)
                keys = pl.ds(base, width)
                q = q_ref[rows, cols]
                g = g_ref[rows, cols]
                p_row = lax.broadcasted_iota(jnp.int32, (1, ROWS), 1) + i * ROWS
                begin = jnp.zeros((1, ROWS), jnp.int32)
                for j in range(1, 4):
                    begin = jnp.where(p_row >= starts[j], starts[j], begin)
                k_idx = lax.broadcasted_iota(jnp.int32, (width, ROWS), 0)
                allowed = (k_idx >= begin) & (k_idx <= p_row)
                st = lax.dot_general(k_ref[keys, :], q, NT, preferred_element_type=F32)
                st = jnp.where(allowed, st * scale2, MASKED)
                top = jnp.max(st, axis=0, keepdims=True)
                e = jnp.exp2(st - top)
                inv = 1.0 / jnp.sum(e, axis=0, keepdims=True)
                p = e * inv
                p_low = p.astype(BF16)
                ot = jnp.dot(vt_ref[:, :width], p_low, preferred_element_type=F32)
                delta = jnp.sum(g.astype(F32).T * ot, axis=0, keepdims=True)
                dpt = lax.dot_general(v_ref[keys, :], g, NT, preferred_element_type=F32)
                ds_low = (p * (dpt - delta)).astype(BF16)
                dqt = jnp.dot(kt_ref[:, :width], ds_low, preferred_element_type=F32)
                dk_ref[:width, :] += jnp.dot(ds_low, q, preferred_element_type=F32)
                dv_ref[:width, :] += jnp.dot(p_low, g, preferred_element_type=F32)
                dq = dqt.T * scale
                dq = dq * c_ref[i * ROWS : (i + 1) * ROWS, :] + pltpu.roll(
                    dq, HD // 2, 1
                ) * s_ref[i * ROWS : (i + 1) * ROWS, :]
                dq = dq.astype(BF16)
                grad_ref[rows, cols] = dq
                for n in range(4):
                    at = (i // 2) * QUARTER + (n % 2) * CHUNK + (2 * (i % 2) + n // 2) * 64
                    qall[x, pl.ds(base + at, 64), cols] = dq[n * 64 : (n + 1) * 64]
            if h == 0:

                @pl.when(turn == 0)
                def _():
                    incoming = weights_x(False)
                    outgoing = weights_y(True)
                    relayed = weights_core(True)
                    for n in range(4):
                        for copy in [incoming[n]] if n < 3 else incoming[3:]:
                            copy.wait_recv()
                        start(outgoing[3 * n : 3 * n + 3])
                        relayed[4 * n].start()

        dk = dk_ref[...] * scale
        dk = dk * c_ref[...] + pltpu.roll(dk, HD // 2, 1) * s_ref[...]
        for n, value in enumerate((dk.astype(BF16), dv_ref[...].astype(BF16))):
            grad_ref[pl.ds(base, SEQ), (2 + n) * HD : (3 + n) * HD] = value
            for b in range(16):
                at = (b // 8) * QUARTER + (b % 2) * CHUNK + (b % 8) // 2 * 64
                kvs[pl.ds(base + at, 64), n * HD : (n + 1) * HD] = value[b * 64 : (b + 1) * 64]
        t = tenant_ref[s]
        seq_rows = pl.ds(base, SEQ)
        parts = [
            (upq_ref[t], slice(0, 2 * HD)),
            (upkv_ref[t, :RANK, :], slice(2 * HD, 3 * HD)),
            (upkv_ref[t, RANK:, :], slice(3 * HD, 4 * HD)),
        ]
        for n, (up, c) in enumerate(parts):
            back = 2.0 * lax.dot_general(
                up, grad_ref[seq_rows, c], NT, preferred_element_type=F32
            )
            for b in range(8):
                dlow_ref[s * 8 + b, n * RANK : (n + 1) * RANK, :] = back[:, b * 128 : (b + 1) * 128]

        @pl.when(turn == 0)
        def _():
            start(gather_out(0))

        return carry

    lax.fori_loop(0, 2, sequence, 0)

    start(gather_out(1))
    start(gather_out(2))
    dl_start()
    dlall[me_t] = dlow_ref[me_t]
    w_own[3].wait()
    w_own[4].wait()
    low_ref[...] = lax.dot_general(
        down_ref[own], x_ref[...], NT, preferred_element_type=F32
    ).astype(BF16)
    low_start()
    lowall[me_t] = low_ref[...]

    def step_low():
        low_recv()
        for b in range(16):
            lowcat[:, b * 128 : (b + 1) * 128] = lowall[b]
        for s in range(2):
            rows = slice(s * SEQ, (s + 1) * SEQ)
            qown[s] = 2.0 * jnp.dot(
                lowcat[:RANK, rows], grad_ref[rows, 0:256], preferred_element_type=F32
            )
            kvown[s, :RANK, :] = 2.0 * jnp.dot(
                lowcat[RANK : 2 * RANK, rows], grad_ref[rows, 256:384], preferred_element_type=F32
            )
            kvown[s, RANK:, :] = 2.0 * jnp.dot(
                lowcat[2 * RANK :, rows], grad_ref[rows, 384:512], preferred_element_type=F32
            )
        kv_copy.start()

    def step_dlow():
        dl_recv()
        total = dlall[0]
        for b in range(1, 16):
            total = total + dlall[b]
        dlw_ref[...] = total.astype(BF16)

        def column(t, c):
            gdown[t] = jnp.dot(
                dlw_ref[...], x_ref[:, pl.ds(pl.multiple_of(t * 512, 512), 512)],
                preferred_element_type=F32,
            ).astype(BF16)
            return c

        lax.fori_loop(0, 16, column, 0)
        dn_start()
        gdall[me_t] = gdown[me_t]

    def step_down():
        dn_recv()
        kv_copy.wait_recv()
        for s in range(2):
            total = gdall[8 * s].astype(F32)
            for b in range(1, 8):
                total = total + gdall[8 * s + b].astype(F32)
            dsum[s] = total
            kvown_sum = kvown[s] + kvpeer[s]
            kvpeer[s] = kvown_sum
        for j in range(8):
            cb = j % 4
            for i in range(2):
                t = 2 * (j // 4) + i
                rsbuf[j, 48 * i : 48 * (i + 1), :] = (
                    dsum[0, :, cb * 128 : (cb + 1) * 128] * hot_ref[t : t + 1, :]
                    + dsum[1, :, cb * 128 : (cb + 1) * 128] * hot_ref[4 + t : 5 + t, :]
                )
            t = j // 2
            c = j % 2
            rsbuf[j, 96:112, :] = (
                qown[0, :, c * 128 : (c + 1) * 128] * hot_ref[t : t + 1, :]
                + qown[1, :, c * 128 : (c + 1) * 128] * hot_ref[4 + t : 5 + t, :]
            )
            rsbuf[j, 112:128, :] = (
                kvpeer[0, c * 16 : (c + 1) * 16, :] * hot_ref[t : t + 1, :]
                + kvpeer[1, c * 16 : (c + 1) * 16, :] * hot_ref[4 + t : 5 + t, :]
            )
        rs_start()
        rsall[me_dp] = rsbuf[me_dp]

    def step_reduce():
        rs_recv()
        total = rsall[0]
        for b in range(1, 8):
            total = total + rsall[b]
        agbuf[me_dp] = total
        ag_start()

    def parts_of(t):
        for n in range(3):
            lo = (t % 2) * 48 + n * 16
            yield [(t // 2) * 4 + cb for cb in range(4)], slice(lo, lo + 16)
        yield [2 * t, 2 * t + 1], slice(96, 112)
        yield [2 * t], slice(112, 128)
        yield [2 * t + 1], slice(112, 128)

    def step_squares():
        ag_recv()
        row = lax.broadcasted_iota(jnp.int32, (8, 128), 0)
        lane = lax.broadcasted_iota(jnp.int32, (8, 128), 1)
        tile = jnp.zeros((8, 128), F32)
        for t in range(TEN):
            for n, (pieces, rows) in enumerate(parts_of(t)):
                total = None
                for j in pieces:
                    v = agbuf[j, rows, :]
                    total = v * v if total is None else total + v * v
                value = jnp.sum(
                    jnp.sum(total, axis=0, keepdims=True), axis=1, keepdims=True
                )
                tile = jnp.where((row == t) & (lane == n), value, tile)
        sqall[me_t] = tile
        sq_start()

    def step_update():
        sq_recv()
        total = sqall[0]
        for b in range(1, 16):
            total = total + sqall[b]
        for t in range(TEN):
            for n, (pieces, rows) in enumerate(parts_of(t)):
                count = RANK * (8192 if n < 3 else 4096 if n == 3 else 2048)
                factor = 1.0 / jnp.sqrt(total[t : t + 1, n : n + 1] * (1.0 / count) + NORM_EPS)
                for i, j in enumerate(pieces):
                    value = agbuf[j, rows, :] * factor
                    if n < 3:
                        ud_ref[t, n * 16 : (n + 1) * 16, i * 128 : (i + 1) * 128] = value
                    elif n == 3:
                        uq_ref[t, :, i * 128 : (i + 1) * 128] = value
                    else:
                        ukv_ref[t, (n - 4) * 16 : (n - 3) * 16, :] = value

    def product(c, write):
        rows = pl.ds(first_row(c), CHUNK)
        def tile(n, carry):
            cols = pl.ds(pl.multiple_of(n * 512, 512), 512)
            acc = None
            for b in range(6):
                left = qall[b, rows, :] if b < 4 else kvm[b - 4, rows, :]
                term = lax.dot_general(left, wx[b, cols, :], NT, preferred_element_type=F32)
                acc = term if acc is None else acc + term
            write(cols, acc)
            return carry

        lax.fori_loop(0, 4, tile, 0)

    def z_copy(h, side, n):
        if n < 2:
            src, dst = part.at[h, side, n], zbuf.at[h, side, n]
        else:
            cols = pl.ds((n - 2) * 1024, 1024)
            src, dst = part.at[h, side, 2, :, cols], zbuf.at[h, side, 2, :, cols]
        return remote(
            src, dst, zsend.at[h, side, n], zrecv.at[h, side, n],
            me_dp, z_left if side else z_right,
        )

    def to_far(h):
        def write(cols, acc):
            part[h, 0, 0, :, cols] = acc[:SUB].astype(BF16)
            part[h, 1, 0, :, cols] = acc[SUB:].astype(BF16)

        return write

    def to_near(h, side):
        def write(cols, acc):
            part[h, side, 2 - side, :, cols] = acc[:SUB].astype(BF16)
            part[h, side, 1 + side, :, cols] = acc[SUB:].astype(BF16)

        return write

    def write_own(cols, acc):
        own_ref[0, :, cols] = acc[:SUB].astype(BF16)
        own_ref[1, :, cols] = acc[SUB:].astype(BF16)

    def far(h):
        product(3 * h, to_far(h))
        z_copy(h, 0, 0).start()
        z_copy(h, 1, 0).start()

    def near(h, side):
        product(3 * h + 1 + side, to_near(h, side))
        z_copy(h, side, 1).start()

    def add_far(h, side):
        z_copy(h, side, 0).wait_recv()
        for m in range(2):
            for n in range(2):
                cols = slice(m * 1024 + n * 512, m * 1024 + (n + 1) * 512)
                part[h, side, 2, :, cols] = (
                    part[h, side, 2, :, cols].astype(F32) + zbuf[h, side, 0, :, cols].astype(F32)
                ).astype(BF16)
            z_copy(h, side, 2 + m).start()

    def final_copy(o, h, m):
        rows, cols = pl.ds(h * 64, 64), pl.ds(m * 1024, 1024)
        return remote(
            fbuf.at[o, rows, cols], fin.at[x, rows, cols], fsend.at[o, h, m], frecv.at[x, h, m],
            me_dp, z * 4 + o,
        )

    def finish(h):
        for m in range(2):
            for side in range(2):
                if m == 0:
                    z_copy(h, side, 1).wait_recv()
                z_copy(h, side, 2 + m).wait_recv()
            for i in range(2):
                for n in range(2):
                    cols = slice(m * 1024 + n * 512, m * 1024 + (n + 1) * 512)
                    total = (
                        own_ref[i, :, cols].astype(F32)
                        + zbuf[h, 0, 2 - i, :, cols].astype(F32)
                        + zbuf[h, 1, 1 + i, :, cols].astype(F32)
                    ).astype(BF16)
                    fbuf[2 * i, h * 64 : (h + 1) * 64, cols] = total[:64]
                    fbuf[2 * i + 1, h * 64 : (h + 1) * 64, cols] = total[64:]
                for o in (2 * i, 2 * i + 1):

                    @pl.when(x != o)
                    def _(o=o, m=m):
                        final_copy(o, h, m).start()

    def deliver(h):
        rows = slice(h * 64, (h + 1) * 64)
        fin[x, rows, :] = fbuf[x, rows, :]
        for m in range(2):
            for o in range(1, 4):
                xs = (x + o) % 4
                block = fin.at[xs, pl.ds(h * 64, 64), pl.ds(m * 1024, 1024)]
                remote(
                    block, block, fsend.at[xs, h, m], frecv.at[xs, h, m], me_dp, z * 4 + xs
                ).wait_recv()
            for b in range(4):
                cols = slice(b * BLOCK_D + m * 1024, b * BLOCK_D + (m + 1) * 1024)
                out_ref[rows, cols] = (
                    fin[b, rows, m * 1024 : (m + 1) * 1024].astype(F32)
                    + out_ref[rows, cols].astype(F32)
                ).astype(BF16)

    def all_sent(h):
        for side in range(2):
            for n in range(4):
                z_copy(h, side, n).wait_send()
        for o in range(4):

            @pl.when(x != o)
            def _(o=o):
                final_copy(o, h, 0).wait_send()
                final_copy(o, h, 1).wait_send()

    def step_output():
        for n in range(16):
            cols = slice(n * 512, (n + 1) * 512)
            out_ref[:, cols] = lax.dot_general(
                dlw_ref[...], down_ref[own, :, cols], TN, preferred_element_type=F32
            ).astype(BF16)

    def ready(c):
        for copy in forward_in(c):
            copy.wait_recv()

    arrive(0)
    start(gather_out(3))
    incoming = weights_y(False)
    relayed = weights_core(True)
    for n in range(4):
        for o in range(3):
            incoming[3 * n + o].wait_recv()
            relayed[4 * n + o + 1].start()
    arrive(1)
    start(gather_out(4))
    for copy in w_own[:3]:
        copy.wait()
    for copy in weights_core(False):
        copy.wait_recv()
    ready(0)
    far(0)
    arrive(2)
    start(gather_out(5))
    ready(1)
    near(0, 0)
    ready(2)
    near(0, 1)
    arrive(3)
    start(gather_out(6))
    step_dlow()
    add_far(0, 0)
    add_far(0, 1)
    arrive(4)
    start(gather_out(7))
    ready(3)
    far(1)
    arrive(5)
    step_low()
    ready(4)
    near(1, 0)
    ready(5)
    near(1, 1)
    arrive(6)
    step_down()
    ready(6)
    product(6, write_own)
    finish(0)
    arrive(7)
    add_far(1, 0)
    add_far(1, 1)
    step_reduce()
    ready(7)
    product(7, write_own)
    step_output()
    deliver(0)
    step_squares()
    for c in range(8):
        for copy in gather_out(c) + forward_out(c):
            copy.wait_send()
    for copy in weights_x(True) + weights_y(True) + weights_core(True):
        copy.wait_send()
    for sent in (dl_sent, low_sent, dn_sent, rs_sent, ag_sent):
        sent()
    kv_copy.wait_send()
    all_sent(0)
    step_update()
    sq_sent()
    finish(1)
    deliver(1)
    all_sent(1)


def fused_call(tenant, docs, q, k, v, g, x, down, upq, upkv, wq, wk, wv):
    vmem = pl.BlockSpec(memory_space=pltpu.VMEM)
    smem = pl.BlockSpec(memory_space=pltpu.SMEM)
    hbm = pl.BlockSpec(memory_space=pl.ANY)
    dma = pltpu.SemaphoreType.DMA
    tokens = q.shape[0]
    cosine, sine = rope_constants()
    return pl.pallas_call(
        fused_kernel,
        in_specs=[smem] * 2 + [vmem] * 4 + [hbm] * 2 + [vmem] * 4 + [hbm] * 3,
        out_specs=[vmem] * 4,
        out_shape=[
            jax.ShapeDtypeStruct(x.shape, BF16),
            jax.ShapeDtypeStruct((TEN, 48, 512), F32),
            jax.ShapeDtypeStruct((TEN, RANK, 256), F32),
            jax.ShapeDtypeStruct((TEN, 2 * RANK, 128), F32),
        ],
        scratch_shapes=[
            pltpu.VMEM((tokens, 512), BF16),
            pltpu.VMEM((16, 48, 128), F32),
            pltpu.VMEM((48, 128), BF16),
            pltpu.VMEM((8, 128), F32),
            pltpu.VMEM((HD, SEQ), BF16), pltpu.VMEM((HD, SEQ), BF16),
            pltpu.VMEM((SEQ, HD), F32), pltpu.VMEM((SEQ, HD), F32),
            pltpu.VMEM((SEQ, HD), F32), pltpu.VMEM((SEQ, HD), F32),
            pltpu.VMEM((4, tokens, 256), BF16),
            pltpu.VMEM((tokens, 256), BF16), pltpu.VMEM((tokens, 256), BF16),
            pltpu.VMEM((2, tokens, 256), BF16),
            pltpu.VMEM((6, BLOCK_D, 256), BF16),
            pltpu.VMEM((2, 2, 3, SUB, BLOCK_D), BF16),
            pltpu.VMEM((2, 2, 3, SUB, BLOCK_D), BF16),
            pltpu.VMEM((2, SUB, BLOCK_D), BF16),
            pltpu.VMEM((4, SUB, BLOCK_D), BF16),
            pltpu.VMEM((4, SUB, BLOCK_D), BF16),
            pltpu.VMEM((16, 48, 128), F32),
            pltpu.VMEM((16, 48, 128), BF16),
            pltpu.VMEM((48, tokens), BF16),
            pltpu.VMEM((48, 128), BF16),
            pltpu.VMEM((2, 32, 128), F32),
            pltpu.VMEM((2, 32, 128), F32),
            pltpu.VMEM((2, 16, 256), F32),
            pltpu.VMEM((16, 48, 512), BF16),
            pltpu.VMEM((16, 48, 512), BF16),
            pltpu.VMEM((2, 48, 512), F32),
            pltpu.VMEM((8, 128, 128), F32),
            pltpu.VMEM((8, 128, 128), F32),
            pltpu.VMEM((8, 128, 128), F32),
            pltpu.VMEM((16, 8, 128), F32),
            pltpu.VMEM(x.shape, BF16),
            pltpu.VMEM(down.shape, BF16),
            dma((5,)), dma((7,)), dma((7,)), dma((4, 3)), dma((4, 3)), dma((4, 4)), dma((4, 4)),
            dma((6, 8)), dma((6, 8)), dma((16,)), dma((16,)), dma((16,)), dma((16,)),
            dma((2,)), dma((16,)), dma((16,)), dma((8,)), dma((8,)), dma((8,)), dma((8,)),
            dma((16,)), dma((16,)), dma((2, 2, 4)), dma((2, 2, 4)), dma((4, 2, 2)), dma((4, 2, 2)),
        ],
        compiler_params=pltpu.CompilerParams(
            collective_id=0, has_side_effects=True, vmem_limit_bytes=63 * 1024 * 1024
        ),
        cost_estimate=pl.CostEstimate(
            flops=20_000_000_000, bytes_accessed=40_000_000, transcendentals=4_000_000
        ),
        name="exchange",
    )(tenant, docs, q, k, v, g, x, down, upq, upkv, cosine, sine, wq, wk, wv)


def per_device(
    x_rows, d_attn, q_saved, k_saved, v_saved, w_query, w_key, w_value, down_all, up_query, up_kv,
    tenant, doc_starts,
):
    return tuple(
        fused_call(
            tenant, doc_starts, q_saved, k_saved, v_saved, d_attn, x_rows, down_all, up_query,
            up_kv, w_query, w_key, w_value,
        )
    )


def solution(mesh):
    in_specs = (
        P(("dp", "tensor"), None),
        P("dp", "tensor"),
        P("dp", "tensor"),
        P("dp", "tensor"),
        P("dp", "tensor"),
        P(None, "tensor"),
        P(None, "tensor"),
        P(None, "tensor"),
        P(),
        P(None, None, "tensor"),
        P(None, None, "tensor"),
        P("dp"),
        P("dp", None),
    )
    out_specs = (
        P(("dp", "tensor"), None),
        P(None, None, "tensor"),
        P(None, None, "tensor"),
        P(None, None, "tensor"),
    )
    return jax.shard_map(
        per_device, mesh=mesh, in_specs=in_specs, out_specs=out_specs, check_vma=False
    )
```

```python
import functools
import math
import numpy as np
import jax
import jax.numpy as jnp
from jax import lax
from jax.experimental import pallas as pl
from jax.experimental.pallas import tpu as pltpu
from jax.sharding import PartitionSpec as P

HD = 128
RANK = 16
TEN = 4
SEQ = 1024
ROPE_BASE = 500000.0
NORM_EPS = 1e-06
MASKED = -1e30
NT = (((1,), (1,)), ((), ()))
TN = (((0,), (0,)), ((), ()))
F32 = jnp.float32
BF16 = jnp.bfloat16
ROWS = 256


def rope_constants():
    half = HD // 2
    freq = ROPE_BASE ** (-(2.0 * np.arange(half)) / HD)
    angle = np.arange(SEQ)[:, None] * freq[None, :]
    cosine = np.concatenate([np.cos(angle), np.cos(angle)], axis=1)
    sine = np.concatenate([np.sin(angle), -np.sin(angle)], axis=1)
    return cosine.astype(np.float32), sine.astype(np.float32)


MESH_ID = pl.DeviceIdType.MESH
CHUNK = 256
SUB = 128
QUARTER = 512
BLOCK_D = 2048
ORDER = ((2, 0), (1, 0), (3, 0), (2, 1), (1, 1), (3, 1), (0, 0), (0, 1))


def fused_kernel(
    tenant_ref, doc_ref, q_ref, k_ref, v_ref, g_ref, x_hbm, down_hbm, upq_ref, upkv_ref,
    cos_ref, sin_ref, wq_ref, wk_ref, wv_ref,
    out_ref, ud_ref, uq_ref, ukv_ref,
    grad_ref, dlow_ref, low_ref, hot_ref, kt_ref, vt_ref, dk_ref, dv_ref, c_ref, s_ref,
    qall, kvs, kvp, kvm, wx, part, zbuf, own_ref, fbuf, fin,
    dlx_in, dlz_out, dlz_in, lowx, lowall, lowcat, dlw_ref, kvown, kvpeer, qown,
    gdown, dnz, dnx_out, dnx_in, dsum,
    rsbuf, rsall, agbuf, sqall, x_ref, down_ref,
    wsem, wxsend, wxrecv, wysend, wyrecv, wcsend, wcrecv,
    gsend, grecv, dlsend, dlrecv, esend, erecv, kvsem,
    rssend, rsrecv, agsend, agrecv, sqsend, sqrecv, zsend, zrecv, fsend, frecv,
):
    me_dp = lax.axis_index("dp")
    me_t = lax.axis_index("tensor")
    z = me_t // 4
    x = me_t % 4
    core = me_dp % 2
    xo = (x + 2) % 4
    pair = x + 1 - 2 * (x % 2)
    mirror = 3 - x
    z_right = ((z + 1) % 4) * 4 + x
    z_left = ((z + 3) % 4) * 4 + x

    def remote(src, dst, ssem, rsem, dp, t):
        return pltpu.make_async_remote_copy(
            src_ref=src, dst_ref=dst, send_sem=ssem, recv_sem=rsem,
            device_id=(dp, t), device_id_type=MESH_ID,
        )

    barrier = pltpu.get_barrier_semaphore()

    def greet_tensor(o, c):
        pl.semaphore_signal(
            barrier, inc=1, device_id=(me_dp, (me_t + o) % 16), device_id_type=MESH_ID
        )
        return c

    def greet_dp(o, c):
        pl.semaphore_signal(
            barrier, inc=1, device_id=((me_dp + o) % 8, me_t), device_id_type=MESH_ID
        )
        return c

    lax.fori_loop(1, 16, greet_tensor, 0)
    lax.fori_loop(1, 8, greet_dp, 0)

    y = me_dp // 2
    kv_here = 4 + x // 2
    kv_there = 5 - x // 2
    blocks = (pair, xo, mirror, kv_there)
    my_part = core * 1024 + y * 256
    d0 = pl.multiple_of(x * BLOCK_D, BLOCK_D)

    def rows_at(start, count):
        return pl.ds(pl.multiple_of(start, count), count)

    w_own = [
        pltpu.make_async_copy(src, dst, wsem.at[i])
        for i, (src, dst) in enumerate((
            (wq_ref.at[pl.ds(d0, BLOCK_D), :], wx.at[x]),
            (wk_ref.at[pl.ds(d0, BLOCK_D), :], wx.at[kv_here, :, pl.ds(0, 128)]),
            (wv_ref.at[pl.ds(d0, BLOCK_D), :], wx.at[kv_here, :, pl.ds(128, 128)]),
            (x_hbm, x_ref),
            (down_hbm, down_ref),
        ))
    ]

    def weights_x(sending):
        copies = []
        for i, xs in enumerate((pair, xo, mirror)):
            if sending:
                src = wq_ref.at[rows_at(xs * BLOCK_D + my_part, 256), :]
                dst = wx.at[x, rows_at(my_part, 256), :]
            else:
                src = dst = wx.at[xs, rows_at(my_part, 256), :]
            copies.append(remote(src, dst, wxsend.at[i], wxrecv.at[i], me_dp, z * 4 + xs))
        for i, xs in enumerate((xo, mirror)):
            for n, w in enumerate((wk_ref, wv_ref)):
                lanes = pl.ds(128 * n, 128)
                if sending:
                    row = my_part + (x % 2) * 128
                    src = w.at[rows_at(xs * BLOCK_D + row, 128), :]
                    dst = wx.at[kv_here, rows_at(row, 128), lanes]
                else:
                    row = my_part + (xs % 2) * 128
                    src = dst = wx.at[kv_there, rows_at(row, 128), lanes]
                k = 3 + 2 * i + n
                copies.append(remote(src, dst, wxsend.at[k], wxrecv.at[k], me_dp, z * 4 + xs))
        return copies

    def weights_y(sending):
        copies = []
        for i, b in enumerate(blocks):
            for o in range(1, 4):
                at_y = y if sending else (y + 4 - o) % 4
                ref = wx.at[b, rows_at(core * 1024 + at_y * 256, 256), :]
                to = ((y + o) % 4) * 2 + core
                copies.append(
                    remote(ref, ref, wysend.at[i, o - 1], wyrecv.at[i, o - 1], to, me_t)
                )
        return copies

    def weights_core(sending):
        copies = []
        for i, b in enumerate(blocks):
            for o in range(4):
                at_y = (y + 4 - o) % 4
                at_core = core if sending else 1 - core
                ref = wx.at[b, rows_at(at_core * 1024 + at_y * 256, 256), :]
                to = me_dp + 1 - 2 * core
                copies.append(remote(ref, ref, wcsend.at[i, o], wcrecv.at[i, o], to, me_t))
        return copies

    pl.semaphore_wait(barrier, 22)
    for copy in weights_x(True) + w_own:
        copy.start()

    def first_row(c):
        off, half = ORDER[c]
        return pl.multiple_of(((z + off) % 4) * QUARTER + half * CHUNK, CHUNK)

    def gather(c, n, src, dst, to):
        return remote(src, dst, gsend.at[n, c], grecv.at[n, c], me_dp, z * 4 + to)

    def gather_out(c):
        rows = pl.ds(first_row(c), CHUNK)
        mine = qall.at[x, rows, :]
        return (
            gather(c, 0, mine, mine, pair),
            gather(c, 2, mine, mine, mirror),
            gather(c, 1, kvs.at[rows, :], kvp.at[rows, :], pair),
        )

    def gather_in(c):
        rows = pl.ds(first_row(c), CHUNK)
        refs = (qall.at[pair, rows, :], qall.at[mirror, rows, :], kvp.at[rows, :])
        return [gather(c, n, ref, ref, to) for n, ref, to in zip((0, 2, 1), refs, (pair, mirror, pair))]

    def half_rows(c, n):
        return pl.ds(pl.multiple_of(first_row(c) + n * SUB, SUB), SUB)

    def forward_out(c):
        to_pair = qall.at[mirror, half_rows(c, 0), :]
        to_mirror = qall.at[pair, half_rows(c, 1), :]
        summed = kvm.at[x // 2, pl.ds(first_row(c), CHUNK), :]
        return (
            gather(c, 3, to_pair, to_pair, pair),
            gather(c, 4, to_mirror, to_mirror, mirror),
            gather(c, 5, summed, summed, mirror),
        )

    def forward_in(c):
        refs = (
            qall.at[xo, half_rows(c, 0), :], qall.at[xo, half_rows(c, 1), :],
            kvm.at[1 - x // 2, pl.ds(first_row(c), CHUNK), :],
        )
        return [gather(c, 3 + n, ref, ref, to) for n, (ref, to) in enumerate(zip(refs, (pair, mirror, mirror)))]

    def start(copies):
        for copy in copies:
            copy.start()

    def arrive(c):
        for copy in gather_in(c):
            copy.wait_recv()
        rows = pl.ds(first_row(c), CHUNK)
        outgoing = forward_out(c)
        outgoing[0].start()
        outgoing[1].start()
        kvm[x // 2, rows, :] = (kvs[rows, :].astype(F32) + kvp[rows, :].astype(F32)).astype(BF16)
        outgoing[2].start()

    def to_tensor(src, buf, ssem, rsem, picked):
        def descriptor(t):
            return remote(
                src.at[t] if picked else src, buf.at[me_t], ssem.at[t], rsem.at[me_t], me_dp, t
            )

        def begin(o, c):
            descriptor((me_t + o) % 16).start()
            return c

        def receive(o, c):
            t = (me_t + o) % 16
            remote(buf.at[t], buf.at[t], ssem.at[t], rsem.at[t], me_dp, t).wait_recv()
            return c

        def sent(o, c):
            descriptor((me_t + o) % 16).wait_send()
            return c

        return (
            lambda: lax.fori_loop(1, 16, begin, 0),
            lambda: lax.fori_loop(1, 16, receive, 0),
            lambda: lax.fori_loop(1, 16, sent, 0),
        )

    def to_dp(src_at, buf, ssem, rsem):
        def descriptor(d):
            return remote(src_at(d), buf.at[me_dp], ssem.at[d], rsem.at[me_dp], d, me_t)

        def begin(o, c):
            descriptor((me_dp + o) % 8).start()
            return c

        def receive(o, c):
            d = (me_dp + o) % 8
            remote(buf.at[d], buf.at[d], ssem.at[d], rsem.at[d], d, me_t).wait_recv()
            return c

        def sent(o, c):
            descriptor((me_dp + o) % 8).wait_send()
            return c

        return (
            lambda: lax.fori_loop(1, 8, begin, 0),
            lambda: lax.fori_loop(1, 8, receive, 0),
            lambda: lax.fori_loop(1, 8, sent, 0),
        )

    def to_line(along, i, src_at, buf):
        at = x if along == "x" else z
        peers = []
        for o in range(1, 4):
            p = (at + o) % 4
            peers.append((p, z * 4 + p if along == "x" else p * 4 + x))

        def out():
            return [
                remote(src_at(p), buf.at[at], esend.at[i, p], erecv.at[i, at], me_dp, t)
                for p, t in peers
            ]

        def begin():
            start(out())

        def receive():
            for p, t in peers:
                remote(
                    buf.at[p], buf.at[p], esend.at[i, p], erecv.at[i, p], me_dp, t
                ).wait_recv()

        def sent():
            for copy in out():
                copy.wait_send()

        return begin, receive, sent

    def dl_parts(turn, sending):
        s = (1 - z // 2 + turn) % 2
        copies = []
        for o in range(1, 4):
            p = (x + o) % 4
            if sending:
                src, dst = dlow_ref.at[p, pl.ds(2 * s, 2)], dlx_in.at[x, pl.ds(2 * s, 2)]
                sems = (dlsend.at[turn, p], dlrecv.at[turn, x])
            else:
                src = dst = dlx_in.at[p, pl.ds(2 * s, 2)]
                sems = (dlsend.at[turn, p], dlrecv.at[turn, p])
            copies.append(remote(src, dst, *sems, me_dp, z * 4 + p))
        return copies

    dlz_start, dlz_recv, dlz_sent = to_line("z", 0, lambda p: dlz_out.at[p], dlz_in)
    lowx_start, lowx_recv, lowx_sent = to_line("x", 1, lambda p: lowx.at[x], lowx)
    lowz_start, lowz_recv, lowz_sent = to_line("z", 2, lambda p: lowx, lowall)
    dnz_start, dnz_recv, dnz_sent = to_line("z", 3, lambda p: gdown.at[p], dnz)
    dnx_start, dnx_recv, dnx_sent = to_line("x", 4, lambda p: dnx_out.at[p], dnx_in)
    sq_start, sq_recv, sq_sent = to_tensor(sqall.at[me_t], sqall, sqsend, sqrecv, False)
    rs_start, rs_recv, rs_sent = to_dp(lambda d: rsbuf.at[d], rsall, rssend, rsrecv)
    ag_start, ag_recv, ag_sent = to_dp(lambda d: agbuf.at[me_dp], agbuf, agsend, agrecv)
    kv_copy = remote(kvown, kvpeer, kvsem.at[0], kvsem.at[1], me_dp, z * 4 + pair)

    for s in range(2):
        for t in range(TEN):
            hot_ref[4 * s + t : 4 * s + t + 1, :] = jnp.where(
                jnp.full((1, 128), tenant_ref[s]) == t, 1.0, 0.0
            )
    own = tenant_ref[me_t // 8]

    scale = HD ** (-0.5)
    scale2 = scale * math.log2(math.e)

    def sequence(turn, carry):
        s = (1 - z // 2 + turn) % 2
        base = pl.multiple_of(s * SEQ, SEQ)
        starts = [doc_ref[s, j] for j in range(4)]
        pos = lax.broadcasted_iota(jnp.int32, (SEQ, HD), 0)
        cb = jnp.broadcast_to(cos_ref[pl.ds(starts[0], 1), :], (SEQ, HD))
        sb = jnp.broadcast_to(sin_ref[pl.ds(starts[0], 1), :], (SEQ, HD))
        for j in range(1, 4):
            inside = pos >= starts[j]
            cb = jnp.where(inside, cos_ref[pl.ds(starts[j], 1), :], cb)
            sb = jnp.where(inside, sin_ref[pl.ds(starts[j], 1), :], sb)
        cp = cos_ref[...]
        sp = sin_ref[...]
        c_ref[...] = cp * cb + sp * sb
        s_ref[...] = sp * cb - cp * sb
        kt_ref[...] = k_ref[pl.ds(base, SEQ), :].T
        vt_ref[...] = v_ref[pl.ds(base, SEQ), :].T
        dk_ref[...] = jnp.zeros_like(dk_ref)
        dv_ref[...] = jnp.zeros_like(dv_ref)
        for h in range(2):
            cols = slice(h * HD, (h + 1) * HD)
            for i in range(SEQ // ROWS):
                width = (i + 1) * ROWS
                rows = pl.ds(base + i * ROWS, ROWS)
                keys = pl.ds(base, width)
                q = q_ref[rows, cols]
                g = g_ref[rows, cols]
                p_row = lax.broadcasted_iota(jnp.int32, (1, ROWS), 1) + i * ROWS
                begin = jnp.zeros((1, ROWS), jnp.int32)
                for j in range(1, 4):
                    begin = jnp.where(p_row >= starts[j], starts[j], begin)
                k_idx = lax.broadcasted_iota(jnp.int32, (width, ROWS), 0)
                allowed = (k_idx >= begin) & (k_idx <= p_row)
                st = lax.dot_general(k_ref[keys, :], q, NT, preferred_element_type=F32)
                st = jnp.where(allowed, st * scale2, MASKED)
                top = jnp.max(st, axis=0, keepdims=True)
                e = jnp.exp2(st - top)
                inv = 1.0 / jnp.sum(e, axis=0, keepdims=True)
                p = e * inv
                p_low = p.astype(BF16)
                ot = jnp.dot(vt_ref[:, :width], p_low, preferred_element_type=F32)
                delta = jnp.sum(g.astype(F32).T * ot, axis=0, keepdims=True)
                dpt = lax.dot_general(v_ref[keys, :], g, NT, preferred_element_type=F32)
                ds_low = (p * (dpt - delta)).astype(BF16)
                dqt = jnp.dot(kt_ref[:, :width], ds_low, preferred_element_type=F32)
                dk_ref[:width, :] += jnp.dot(ds_low, q, preferred_element_type=F32)
                dv_ref[:width, :] += jnp.dot(p_low, g, preferred_element_type=F32)
                dq = dqt.T * scale
                dq = dq * c_ref[i * ROWS : (i + 1) * ROWS, :] + pltpu.roll(
                    dq, HD // 2, 1
                ) * s_ref[i * ROWS : (i + 1) * ROWS, :]
                dq = dq.astype(BF16)
                grad_ref[rows, cols] = dq
                for n in range(4):
                    at = (i // 2) * QUARTER + (n % 2) * CHUNK + (2 * (i % 2) + n // 2) * 64
                    qall[x, pl.ds(base + at, 64), cols] = dq[n * 64 : (n + 1) * 64]
            if h == 0:

                @pl.when(turn == 0)
                def _():
                    incoming = weights_x(False)
                    outgoing = weights_y(True)
                    relayed = weights_core(True)
                    for n in range(4):
                        for copy in [incoming[n]] if n < 3 else incoming[3:]:
                            copy.wait_recv()
                        start(outgoing[3 * n : 3 * n + 3])
                        relayed[4 * n].start()

        dk = dk_ref[...] * scale
        dk = dk * c_ref[...] + pltpu.roll(dk, HD // 2, 1) * s_ref[...]
        for n, value in enumerate((dk.astype(BF16), dv_ref[...].astype(BF16))):
            grad_ref[pl.ds(base, SEQ), (2 + n) * HD : (3 + n) * HD] = value
            for b in range(16):
                at = (b // 8) * QUARTER + (b % 2) * CHUNK + (b % 8) // 2 * 64
                kvs[pl.ds(base + at, 64), n * HD : (n + 1) * HD] = value[b * 64 : (b + 1) * 64]
        t = tenant_ref[s]
        seq_rows = pl.ds(base, SEQ)
        parts = [
            (upq_ref[t], slice(0, 2 * HD)),
            (upkv_ref[t, :RANK, :], slice(2 * HD, 3 * HD)),
            (upkv_ref[t, RANK:, :], slice(3 * HD, 4 * HD)),
        ]
        for n, (up, c) in enumerate(parts):
            back = 2.0 * lax.dot_general(
                up, grad_ref[seq_rows, c], NT, preferred_element_type=F32
            )
            for b in range(8):
                dlow_ref[b % 4, 2 * s + b // 4, n * RANK : (n + 1) * RANK, :] = back[
                    :, b * 128 : (b + 1) * 128
                ].astype(BF16)

        start(dl_parts(turn, True))

        @pl.when(turn == 0)
        def _():
            start(gather_out(0))
            w_own[3].wait()
            w_own[4].wait()
            lowx[x] = lax.dot_general(
                down_ref[own], x_ref[...], NT, preferred_element_type=F32
            ).astype(BF16)
            lowx_start()

        return carry

    lax.fori_loop(0, 2, sequence, 0)

    start(gather_out(1))
    start(gather_out(2))
    lowx_recv()
    lowz_start()
    lowall[z] = lowx[...]
    dlx_in[x] = dlow_ref[x]
    for turn in range(2):
        for copy in dl_parts(turn, False):
            copy.wait_recv()
    dlz_out[...] = (
        (dlx_in[0].astype(F32) + dlx_in[1].astype(F32))
        + (dlx_in[2].astype(F32) + dlx_in[3].astype(F32))
    ).astype(BF16)
    dlz_start()
    dlz_in[z] = dlz_out[z]

    def step_low():
        lowz_recv()
        for b in range(16):
            lowcat[:, b * 128 : (b + 1) * 128] = lowall[b // 4, b % 4]
        for s in range(2):
            rows = slice(s * SEQ, (s + 1) * SEQ)
            qown[s] = 2.0 * jnp.dot(
                lowcat[:RANK, rows], grad_ref[rows, 0:256], preferred_element_type=F32
            )
            kvown[s, :RANK, :] = 2.0 * jnp.dot(
                lowcat[RANK : 2 * RANK, rows], grad_ref[rows, 256:384], preferred_element_type=F32
            )
            kvown[s, RANK:, :] = 2.0 * jnp.dot(
                lowcat[2 * RANK :, rows], grad_ref[rows, 384:512], preferred_element_type=F32
            )
        kv_copy.start()

    def step_dlow():
        dlz_recv()
        dlw_ref[...] = (
            (dlz_in[0].astype(F32) + dlz_in[1].astype(F32))
            + (dlz_in[2].astype(F32) + dlz_in[3].astype(F32))
        ).astype(BF16)

        def column(t, c):
            gdown[t // 4, t % 4] = jnp.dot(
                dlw_ref[...], x_ref[:, pl.ds(pl.multiple_of(t * 512, 512), 512)],
                preferred_element_type=F32,
            ).astype(BF16)
            return c

        lax.fori_loop(0, 16, column, 0)
        dnz_start()
        dnz[z] = gdown[z]

    def step_down_x():
        dnz_recv()
        for s in range(2):
            for b in range(4):
                dnx_out[b, s] = (
                    dnz[2 * s, b].astype(F32) + dnz[2 * s + 1, b].astype(F32)
                ).astype(BF16)
        dnx_start()
        dnx_in[x] = dnx_out[x]

    def step_down():
        dnx_recv()
        kv_copy.wait_recv()
        for s in range(2):
            total = dnx_in[0, s].astype(F32)
            for b in range(1, 4):
                total = total + dnx_in[b, s].astype(F32)
            dsum[s] = total
            kvown_sum = kvown[s] + kvpeer[s]
            kvpeer[s] = kvown_sum
        for j in range(8):
            cb = j % 4
            for i in range(2):
                t = 2 * (j // 4) + i
                rsbuf[j, 48 * i : 48 * (i + 1), :] = (
                    dsum[0, :, cb * 128 : (cb + 1) * 128] * hot_ref[t : t + 1, :]
                    + dsum[1, :, cb * 128 : (cb + 1) * 128] * hot_ref[4 + t : 5 + t, :]
                )
            t = j // 2
            c = j % 2
            rsbuf[j, 96:112, :] = (
                qown[0, :, c * 128 : (c + 1) * 128] * hot_ref[t : t + 1, :]
                + qown[1, :, c * 128 : (c + 1) * 128] * hot_ref[4 + t : 5 + t, :]
            )
            rsbuf[j, 112:128, :] = (
                kvpeer[0, c * 16 : (c + 1) * 16, :] * hot_ref[t : t + 1, :]
                + kvpeer[1, c * 16 : (c + 1) * 16, :] * hot_ref[4 + t : 5 + t, :]
            )
        rs_start()
        rsall[me_dp] = rsbuf[me_dp]

    def step_reduce():
        rs_recv()
        total = rsall[0]
        for b in range(1, 8):
            total = total + rsall[b]
        agbuf[me_dp] = total
        ag_start()

    def parts_of(t):
        for n in range(3):
            lo = (t % 2) * 48 + n * 16
            yield [(t // 2) * 4 + cb for cb in range(4)], slice(lo, lo + 16)
        yield [2 * t, 2 * t + 1], slice(96, 112)
        yield [2 * t], slice(112, 128)
        yield [2 * t + 1], slice(112, 128)

    def step_squares():
        ag_recv()
        row = lax.broadcasted_iota(jnp.int32, (8, 128), 0)
        lane = lax.broadcasted_iota(jnp.int32, (8, 128), 1)
        tile = jnp.zeros((8, 128), F32)
        for t in range(TEN):
            for n, (pieces, rows) in enumerate(parts_of(t)):
                total = None
                for j in pieces:
                    v = agbuf[j, rows, :]
                    total = v * v if total is None else total + v * v
                value = jnp.sum(
                    jnp.sum(total, axis=0, keepdims=True), axis=1, keepdims=True
                )
                tile = jnp.where((row == t) & (lane == n), value, tile)
        sqall[me_t] = tile
        sq_start()

    def step_update():
        sq_recv()
        total = sqall[0]
        for b in range(1, 16):
            total = total + sqall[b]
        for t in range(TEN):
            for n, (pieces, rows) in enumerate(parts_of(t)):
                count = RANK * (8192 if n < 3 else 4096 if n == 3 else 2048)
                factor = 1.0 / jnp.sqrt(total[t : t + 1, n : n + 1] * (1.0 / count) + NORM_EPS)
                for i, j in enumerate(pieces):
                    value = agbuf[j, rows, :] * factor
                    if n < 3:
                        ud_ref[t, n * 16 : (n + 1) * 16, i * 128 : (i + 1) * 128] = value
                    elif n == 3:
                        uq_ref[t, :, i * 128 : (i + 1) * 128] = value
                    else:
                        ukv_ref[t, (n - 4) * 16 : (n - 3) * 16, :] = value

    def product(c, write):
        rows = pl.ds(first_row(c), CHUNK)
        def tile(n, carry):
            cols = pl.ds(pl.multiple_of(n * 512, 512), 512)
            acc = None
            for b in range(6):
                left = qall[b, rows, :] if b < 4 else kvm[b - 4, rows, :]
                term = lax.dot_general(left, wx[b, cols, :], NT, preferred_element_type=F32)
                acc = term if acc is None else acc + term
            write(cols, acc)
            return carry

        lax.fori_loop(0, 4, tile, 0)

    def z_copy(h, side, n):
        if n < 2:
            src, dst = part.at[h, side, n], zbuf.at[h, side, n]
        else:
            cols = pl.ds((n - 2) * 1024, 1024)
            src, dst = part.at[h, side, 2, :, cols], zbuf.at[h, side, 2, :, cols]
        return remote(
            src, dst, zsend.at[h, side, n], zrecv.at[h, side, n],
            me_dp, z_left if side else z_right,
        )

    def to_far(h):
        def write(cols, acc):
            part[h, 0, 0, :, cols] = acc[:SUB].astype(BF16)
            part[h, 1, 0, :, cols] = acc[SUB:].astype(BF16)

        return write

    def to_near(h, side):
        def write(cols, acc):
            part[h, side, 2 - side, :, cols] = acc[:SUB].astype(BF16)
            part[h, side, 1 + side, :, cols] = acc[SUB:].astype(BF16)

        return write

    def write_own(cols, acc):
        own_ref[0, :, cols] = acc[:SUB].astype(BF16)
        own_ref[1, :, cols] = acc[SUB:].astype(BF16)

    def far(h):
        product(3 * h, to_far(h))
        z_copy(h, 0, 0).start()
        z_copy(h, 1, 0).start()

    def near(h, side):
        product(3 * h + 1 + side, to_near(h, side))
        z_copy(h, side, 1).start()

    def add_far(h, side):
        z_copy(h, side, 0).wait_recv()
        for m in range(2):
            for n in range(2):
                cols = slice(m * 1024 + n * 512, m * 1024 + (n + 1) * 512)
                part[h, side, 2, :, cols] = (
                    part[h, side, 2, :, cols].astype(F32) + zbuf[h, side, 0, :, cols].astype(F32)
                ).astype(BF16)
            z_copy(h, side, 2 + m).start()

    def final_copy(o, h, m):
        rows, cols = pl.ds(h * 64, 64), pl.ds(m * 1024, 1024)
        return remote(
            fbuf.at[o, rows, cols], fin.at[x, rows, cols], fsend.at[o, h, m], frecv.at[x, h, m],
            me_dp, z * 4 + o,
        )

    def finish(h):
        for m in range(2):
            for side in range(2):
                if m == 0:
                    z_copy(h, side, 1).wait_recv()
                z_copy(h, side, 2 + m).wait_recv()
            for i in range(2):
                for n in range(2):
                    cols = slice(m * 1024 + n * 512, m * 1024 + (n + 1) * 512)
                    total = (
                        own_ref[i, :, cols].astype(F32)
                        + zbuf[h, 0, 2 - i, :, cols].astype(F32)
                        + zbuf[h, 1, 1 + i, :, cols].astype(F32)
                    ).astype(BF16)
                    fbuf[2 * i, h * 64 : (h + 1) * 64, cols] = total[:64]
                    fbuf[2 * i + 1, h * 64 : (h + 1) * 64, cols] = total[64:]
                for o in (2 * i, 2 * i + 1):

                    @pl.when(x != o)
                    def _(o=o, m=m):
                        final_copy(o, h, m).start()

    def deliver(h):
        rows = slice(h * 64, (h + 1) * 64)
        fin[x, rows, :] = fbuf[x, rows, :]
        for m in range(2):
            for o in range(1, 4):
                xs = (x + o) % 4
                block = fin.at[xs, pl.ds(h * 64, 64), pl.ds(m * 1024, 1024)]
                remote(
                    block, block, fsend.at[xs, h, m], frecv.at[xs, h, m], me_dp, z * 4 + xs
                ).wait_recv()
            for b in range(4):
                cols = slice(b * BLOCK_D + m * 1024, b * BLOCK_D + (m + 1) * 1024)
                out_ref[rows, cols] = (
                    fin[b, rows, m * 1024 : (m + 1) * 1024].astype(F32)
                    + out_ref[rows, cols].astype(F32)
                ).astype(BF16)

    def all_sent(h):
        for side in range(2):
            for n in range(4):
                z_copy(h, side, n).wait_send()
        for o in range(4):

            @pl.when(x != o)
            def _(o=o):
                final_copy(o, h, 0).wait_send()
                final_copy(o, h, 1).wait_send()

    def step_output():
        for n in range(16):
            cols = slice(n * 512, (n + 1) * 512)
            out_ref[:, cols] = lax.dot_general(
                dlw_ref[...], down_ref[own, :, cols], TN, preferred_element_type=F32
            ).astype(BF16)

    def ready(c):
        for copy in forward_in(c):
            copy.wait_recv()

    arrive(0)
    start(gather_out(3))
    incoming = weights_y(False)
    relayed = weights_core(True)
    for n in range(4):
        for o in range(3):
            incoming[3 * n + o].wait_recv()
            relayed[4 * n + o + 1].start()
    step_dlow()
    arrive(1)
    start(gather_out(4))
    for copy in w_own[:3]:
        copy.wait()
    for copy in weights_core(False):
        copy.wait_recv()
    ready(0)
    far(0)
    arrive(2)
    start(gather_out(5))
    ready(1)
    near(0, 0)
    ready(2)
    near(0, 1)
    arrive(3)
    start(gather_out(6))
    add_far(0, 0)
    add_far(0, 1)
    step_low()
    arrive(4)
    start(gather_out(7))
    step_down_x()
    ready(3)
    far(1)
    arrive(5)
    ready(4)
    near(1, 0)
    ready(5)
    near(1, 1)
    arrive(6)
    step_down()
    ready(6)
    product(6, write_own)
    finish(0)
    arrive(7)
    add_far(1, 0)
    add_far(1, 1)
    step_reduce()
    ready(7)
    product(7, write_own)
    step_output()
    deliver(0)
    step_squares()
    for c in range(8):
        for copy in gather_out(c) + forward_out(c):
            copy.wait_send()
    for copy in weights_x(True) + weights_y(True) + weights_core(True):
        copy.wait_send()
    for sent in (dlz_sent, lowx_sent, lowz_sent, dnz_sent, dnx_sent, rs_sent, ag_sent):
        sent()
    for turn in range(2):
        for copy in dl_parts(turn, True):
            copy.wait_send()
    kv_copy.wait_send()
    all_sent(0)
    step_update()
    sq_sent()
    finish(1)
    deliver(1)
    all_sent(1)


def fused_call(tenant, docs, q, k, v, g, x, down, upq, upkv, wq, wk, wv):
    vmem = pl.BlockSpec(memory_space=pltpu.VMEM)
    smem = pl.BlockSpec(memory_space=pltpu.SMEM)
    hbm = pl.BlockSpec(memory_space=pl.ANY)
    dma = pltpu.SemaphoreType.DMA
    tokens = q.shape[0]
    cosine, sine = rope_constants()
    return pl.pallas_call(
        fused_kernel,
        in_specs=[smem] * 2 + [vmem] * 4 + [hbm] * 2 + [vmem] * 4 + [hbm] * 3,
        out_specs=[vmem] * 4,
        out_shape=[
            jax.ShapeDtypeStruct(x.shape, BF16),
            jax.ShapeDtypeStruct((TEN, 48, 512), F32),
            jax.ShapeDtypeStruct((TEN, RANK, 256), F32),
            jax.ShapeDtypeStruct((TEN, 2 * RANK, 128), F32),
        ],
        scratch_shapes=[
            pltpu.VMEM((tokens, 512), BF16),
            pltpu.VMEM((4, 4, 48, 128), BF16),
            pltpu.VMEM((48, 128), BF16),
            pltpu.VMEM((8, 128), F32),
            pltpu.VMEM((HD, SEQ), BF16), pltpu.VMEM((HD, SEQ), BF16),
            pltpu.VMEM((SEQ, HD), F32), pltpu.VMEM((SEQ, HD), F32),
            pltpu.VMEM((SEQ, HD), F32), pltpu.VMEM((SEQ, HD), F32),
            pltpu.VMEM((4, tokens, 256), BF16),
            pltpu.VMEM((tokens, 256), BF16), pltpu.VMEM((tokens, 256), BF16),
            pltpu.VMEM((2, tokens, 256), BF16),
            pltpu.VMEM((6, BLOCK_D, 256), BF16),
            pltpu.VMEM((2, 2, 3, SUB, BLOCK_D), BF16),
            pltpu.VMEM((2, 2, 3, SUB, BLOCK_D), BF16),
            pltpu.VMEM((2, SUB, BLOCK_D), BF16),
            pltpu.VMEM((4, SUB, BLOCK_D), BF16),
            pltpu.VMEM((4, SUB, BLOCK_D), BF16),
            pltpu.VMEM((4, 4, 48, 128), BF16),
            pltpu.VMEM((4, 48, 128), BF16), pltpu.VMEM((4, 48, 128), BF16),
            pltpu.VMEM((4, 48, 128), BF16),
            pltpu.VMEM((4, 4, 48, 128), BF16),
            pltpu.VMEM((48, tokens), BF16),
            pltpu.VMEM((48, 128), BF16),
            pltpu.VMEM((2, 32, 128), F32),
            pltpu.VMEM((2, 32, 128), F32),
            pltpu.VMEM((2, 16, 256), F32),
            pltpu.VMEM((4, 4, 48, 512), BF16),
            pltpu.VMEM((4, 4, 48, 512), BF16),
            pltpu.VMEM((4, 2, 48, 512), BF16), pltpu.VMEM((4, 2, 48, 512), BF16),
            pltpu.VMEM((2, 48, 512), F32),
            pltpu.VMEM((8, 128, 128), F32),
            pltpu.VMEM((8, 128, 128), F32),
            pltpu.VMEM((8, 128, 128), F32),
            pltpu.VMEM((16, 8, 128), F32),
            pltpu.VMEM(x.shape, BF16),
            pltpu.VMEM(down.shape, BF16),
            dma((5,)), dma((7,)), dma((7,)), dma((4, 3)), dma((4, 3)), dma((4, 4)), dma((4, 4)),
            dma((6, 8)), dma((6, 8)), dma((2, 4)), dma((2, 4)), dma((5, 4)), dma((5, 4)),
            dma((2,)), dma((8,)), dma((8,)), dma((8,)), dma((8,)),
            dma((16,)), dma((16,)), dma((2, 2, 4)), dma((2, 2, 4)), dma((4, 2, 2)), dma((4, 2, 2)),
        ],
        compiler_params=pltpu.CompilerParams(
            collective_id=0, has_side_effects=True, vmem_limit_bytes=63 * 1024 * 1024
        ),
        cost_estimate=pl.CostEstimate(
            flops=20_000_000_000, bytes_accessed=40_000_000, transcendentals=4_000_000
        ),
        name="exchange",
    )(tenant, docs, q, k, v, g, x, down, upq, upkv, cosine, sine, wq, wk, wv)


def per_device(
    x_rows, d_attn, q_saved, k_saved, v_saved, w_query, w_key, w_value, down_all, up_query, up_kv,
    tenant, doc_starts,
):
    return tuple(
        fused_call(
            tenant, doc_starts, q_saved, k_saved, v_saved, d_attn, x_rows, down_all, up_query,
            up_kv, w_query, w_key, w_value,
        )
    )


def solution(mesh):
    in_specs = (
        P(("dp", "tensor"), None),
        P("dp", "tensor"),
        P("dp", "tensor"),
        P("dp", "tensor"),
        P("dp", "tensor"),
        P(None, "tensor"),
        P(None, "tensor"),
        P(None, "tensor"),
        P(),
        P(None, None, "tensor"),
        P(None, None, "tensor"),
        P("dp"),
        P("dp", None),
    )
    out_specs = (
        P(("dp", "tensor"), None),
        P(None, None, "tensor"),
        P(None, None, "tensor"),
        P(None, None, "tensor"),
    )
    return jax.shard_map(
        per_device, mesh=mesh, in_specs=in_specs, out_specs=out_specs, check_vma=False
    )
```

```python
import functools
import math
import numpy as np
import jax
import jax.numpy as jnp
from jax import lax
from jax.experimental import pallas as pl
from jax.experimental.pallas import tpu as pltpu
from jax.sharding import PartitionSpec as P

HD = 128
RANK = 16
TEN = 4
SEQ = 1024
ROPE_BASE = 500000.0
NORM_EPS = 1e-06
MASKED = -1e30
NT = (((1,), (1,)), ((), ()))
TN = (((0,), (0,)), ((), ()))
F32 = jnp.float32
BF16 = jnp.bfloat16
ROWS = 256


def rope_constants():
    half = HD // 2
    freq = ROPE_BASE ** (-(2.0 * np.arange(half)) / HD)
    angle = np.arange(SEQ)[:, None] * freq[None, :]
    cosine = np.concatenate([np.cos(angle), np.cos(angle)], axis=1)
    sine = np.concatenate([np.sin(angle), -np.sin(angle)], axis=1)
    return cosine.astype(np.float32), sine.astype(np.float32)


MESH_ID = pl.DeviceIdType.MESH
CHUNK = 256
SUB = 128
QUARTER = 512
BLOCK_D = 2048
ORDER = ((2, 0), (1, 0), (3, 0), (2, 1), (1, 1), (3, 1), (0, 0), (0, 1))


def fused_kernel(
    tenant_ref, doc_ref, q_ref, k_ref, v_ref, g_ref, x_hbm, down_hbm, upq_ref, upkv_ref,
    cos_ref, sin_ref, wq_ref, wk_ref, wv_ref,
    out_ref, ud_ref, uq_ref, ukv_ref,
    grad_ref, dlow_ref, low_ref, hot_ref, kt_ref, vt_ref, dk_ref, dv_ref, c_ref, s_ref,
    qall, kvs, kvp, kvm, wx, part, zbuf, own_ref, fbuf, fin,
    dlx_in, dlz_out, dlz_in, lowx, lowall, lowcat, dlw_ref, kvown, kvpeer, qown,
    gdown, dnz, dnx_out, dnx_in, dsum,
    rsbuf, rsall, agbuf, sqall, x_ref, down_ref,
    wsem, wxsend, wxrecv, wysend, wyrecv, wcsend, wcrecv,
    gsend, grecv, dlsend, dlrecv, esend, erecv, kvsem,
    rssend, rsrecv, agsend, agrecv, sqsend, sqrecv, zsend, zrecv, fsend, frecv,
):
    me_dp = lax.axis_index("dp")
    me_t = lax.axis_index("tensor")
    z = me_t // 4
    x = me_t % 4
    core = me_dp % 2
    xo = (x + 2) % 4
    pair = x + 1 - 2 * (x % 2)
    mirror = 3 - x
    z_right = ((z + 1) % 4) * 4 + x
    z_left = ((z + 3) % 4) * 4 + x

    def remote(src, dst, ssem, rsem, dp, t):
        return pltpu.make_async_remote_copy(
            src_ref=src, dst_ref=dst, send_sem=ssem, recv_sem=rsem,
            device_id=(dp, t), device_id_type=MESH_ID,
        )

    barrier = pltpu.get_barrier_semaphore()

    def greet_tensor(o, c):
        pl.semaphore_signal(
            barrier, inc=1, device_id=(me_dp, (me_t + o) % 16), device_id_type=MESH_ID
        )
        return c

    def greet_dp(o, c):
        pl.semaphore_signal(
            barrier, inc=1, device_id=((me_dp + o) % 8, me_t), device_id_type=MESH_ID
        )
        return c

    lax.fori_loop(1, 16, greet_tensor, 0)
    lax.fori_loop(1, 8, greet_dp, 0)

    y = me_dp // 2
    kv_here = 4 + x // 2
    kv_there = 5 - x // 2
    blocks = (pair, xo, mirror, kv_there)
    my_part = core * 1024 + y * 256
    d0 = pl.multiple_of(x * BLOCK_D, BLOCK_D)

    def rows_at(start, count):
        return pl.ds(pl.multiple_of(start, count), count)

    w_own = [
        pltpu.make_async_copy(src, dst, wsem.at[i])
        for i, (src, dst) in enumerate((
            (wq_ref.at[pl.ds(d0, BLOCK_D), :], wx.at[x]),
            (wk_ref.at[pl.ds(d0, BLOCK_D), :], wx.at[kv_here, :, pl.ds(0, 128)]),
            (wv_ref.at[pl.ds(d0, BLOCK_D), :], wx.at[kv_here, :, pl.ds(128, 128)]),
            (x_hbm, x_ref),
            (down_hbm, down_ref),
        ))
    ]

    def weights_x(sending):
        copies = []
        for i, xs in enumerate((pair, xo, mirror)):
            if sending:
                src = wq_ref.at[rows_at(xs * BLOCK_D + my_part, 256), :]
                dst = wx.at[x, rows_at(my_part, 256), :]
            else:
                src = dst = wx.at[xs, rows_at(my_part, 256), :]
            copies.append(remote(src, dst, wxsend.at[i], wxrecv.at[i], me_dp, z * 4 + xs))
        for i, xs in enumerate((xo, mirror)):
            for n, w in enumerate((wk_ref, wv_ref)):
                lanes = pl.ds(128 * n, 128)
                if sending:
                    row = my_part + (x % 2) * 128
                    src = w.at[rows_at(xs * BLOCK_D + row, 128), :]
                    dst = wx.at[kv_here, rows_at(row, 128), lanes]
                else:
                    row = my_part + (xs % 2) * 128
                    src = dst = wx.at[kv_there, rows_at(row, 128), lanes]
                k = 3 + 2 * i + n
                copies.append(remote(src, dst, wxsend.at[k], wxrecv.at[k], me_dp, z * 4 + xs))
        return copies

    def weights_y(sending):
        copies = []
        for i, b in enumerate(blocks):
            for o in range(1, 4):
                at_y = y if sending else (y + 4 - o) % 4
                ref = wx.at[b, rows_at(core * 1024 + at_y * 256, 256), :]
                to = ((y + o) % 4) * 2 + core
                copies.append(
                    remote(ref, ref, wysend.at[i, o - 1], wyrecv.at[i, o - 1], to, me_t)
                )
        return copies

    def weights_core(sending):
        copies = []
        for i, b in enumerate(blocks):
            for o in range(4):
                at_y = (y + 4 - o) % 4
                at_core = core if sending else 1 - core
                ref = wx.at[b, rows_at(at_core * 1024 + at_y * 256, 256), :]
                to = me_dp + 1 - 2 * core
                copies.append(remote(ref, ref, wcsend.at[i, o], wcrecv.at[i, o], to, me_t))
        return copies

    pl.semaphore_wait(barrier, 22)
    for copy in weights_x(True) + w_own:
        copy.start()

    def first_row(c):
        off, half = ORDER[c]
        return pl.multiple_of(((z + off) % 4) * QUARTER + half * CHUNK, CHUNK)

    def gather(c, n, src, dst, to):
        return remote(src, dst, gsend.at[n, c], grecv.at[n, c], me_dp, z * 4 + to)

    def gather_out(c):
        rows = pl.ds(first_row(c), CHUNK)
        mine = qall.at[x, rows, :]
        return (
            gather(c, 0, mine, mine, pair),
            gather(c, 2, mine, mine, mirror),
            gather(c, 1, kvs.at[rows, :], kvp.at[rows, :], pair),
        )

    def gather_in(c):
        rows = pl.ds(first_row(c), CHUNK)
        refs = (qall.at[pair, rows, :], qall.at[mirror, rows, :], kvp.at[rows, :])
        return [gather(c, n, ref, ref, to) for n, ref, to in zip((0, 2, 1), refs, (pair, mirror, pair))]

    def half_rows(c, n):
        return pl.ds(pl.multiple_of(first_row(c) + n * SUB, SUB), SUB)

    def forward_out(c):
        to_pair = qall.at[mirror, half_rows(c, 0), :]
        to_mirror = qall.at[pair, half_rows(c, 1), :]
        summed = kvm.at[x // 2, pl.ds(first_row(c), CHUNK), :]
        return (
            gather(c, 3, to_pair, to_pair, pair),
            gather(c, 4, to_mirror, to_mirror, mirror),
            gather(c, 5, summed, summed, mirror),
        )

    def forward_in(c):
        refs = (
            qall.at[xo, half_rows(c, 0), :], qall.at[xo, half_rows(c, 1), :],
            kvm.at[1 - x // 2, pl.ds(first_row(c), CHUNK), :],
        )
        return [gather(c, 3 + n, ref, ref, to) for n, (ref, to) in enumerate(zip(refs, (pair, mirror, mirror)))]

    def start(copies):
        for copy in copies:
            copy.start()

    def arrive(c):
        for copy in gather_in(c):
            copy.wait_recv()
        rows = pl.ds(first_row(c), CHUNK)
        outgoing = forward_out(c)
        outgoing[0].start()
        outgoing[1].start()
        kvm[x // 2, rows, :] = (kvs[rows, :].astype(F32) + kvp[rows, :].astype(F32)).astype(BF16)
        outgoing[2].start()

    def to_tensor(src, buf, ssem, rsem, picked):
        def descriptor(t):
            return remote(
                src.at[t] if picked else src, buf.at[me_t], ssem.at[t], rsem.at[me_t], me_dp, t
            )

        def begin(o, c):
            descriptor((me_t + o) % 16).start()
            return c

        def receive(o, c):
            t = (me_t + o) % 16
            remote(buf.at[t], buf.at[t], ssem.at[t], rsem.at[t], me_dp, t).wait_recv()
            return c

        def sent(o, c):
            descriptor((me_t + o) % 16).wait_send()
            return c

        return (
            lambda: lax.fori_loop(1, 16, begin, 0),
            lambda: lax.fori_loop(1, 16, receive, 0),
            lambda: lax.fori_loop(1, 16, sent, 0),
        )

    def to_dp(src_at, buf, ssem, rsem):
        def descriptor(d):
            return remote(src_at(d), buf.at[me_dp], ssem.at[d], rsem.at[me_dp], d, me_t)

        def begin(o, c):
            descriptor((me_dp + o) % 8).start()
            return c

        def receive(o, c):
            d = (me_dp + o) % 8
            remote(buf.at[d], buf.at[d], ssem.at[d], rsem.at[d], d, me_t).wait_recv()
            return c

        def sent(o, c):
            descriptor((me_dp + o) % 8).wait_send()
            return c

        return (
            lambda: lax.fori_loop(1, 8, begin, 0),
            lambda: lax.fori_loop(1, 8, receive, 0),
            lambda: lax.fori_loop(1, 8, sent, 0),
        )

    def to_line(along, i, src_at, buf):
        at = x if along == "x" else z
        peers = []
        for o in range(1, 4):
            p = (at + o) % 4
            peers.append((p, z * 4 + p if along == "x" else p * 4 + x))

        def out():
            return [
                remote(src_at(p), buf.at[at], esend.at[i, p], erecv.at[i, at], me_dp, t)
                for p, t in peers
            ]

        def begin():
            start(out())

        def receive():
            for p, t in peers:
                remote(
                    buf.at[p], buf.at[p], esend.at[i, p], erecv.at[i, p], me_dp, t
                ).wait_recv()

        def sent():
            for copy in out():
                copy.wait_send()

        return begin, receive, sent

    def dl_parts(turn, sending):
        s = (1 - z // 2 + turn) % 2
        copies = []
        for o in range(1, 4):
            p = (x + o) % 4
            if sending:
                src, dst = dlow_ref.at[p, pl.ds(2 * s, 2)], dlx_in.at[x, pl.ds(2 * s, 2)]
                sems = (dlsend.at[turn, p], dlrecv.at[turn, x])
            else:
                src = dst = dlx_in.at[p, pl.ds(2 * s, 2)]
                sems = (dlsend.at[turn, p], dlrecv.at[turn, p])
            copies.append(remote(src, dst, *sems, me_dp, z * 4 + p))
        return copies

    dlz_start, dlz_recv, dlz_sent = to_line("z", 0, lambda p: dlz_out.at[p], dlz_in)
    lowx_start, lowx_recv, lowx_sent = to_line("x", 1, lambda p: lowx.at[x], lowx)
    lowz_start, lowz_recv, lowz_sent = to_line("z", 2, lambda p: lowx, lowall)
    dnz_start, dnz_recv, dnz_sent = to_line("z", 3, lambda p: gdown.at[p], dnz)
    dnx_start, dnx_recv, dnx_sent = to_line("x", 4, lambda p: dnx_out.at[p], dnx_in)
    sq_start, sq_recv, sq_sent = to_tensor(sqall.at[me_t], sqall, sqsend, sqrecv, False)
    rs_start, rs_recv, rs_sent = to_dp(lambda d: rsbuf.at[d], rsall, rssend, rsrecv)
    ag_start, ag_recv, ag_sent = to_dp(lambda d: agbuf.at[me_dp], agbuf, agsend, agrecv)
    kv_copy = remote(kvown, kvpeer, kvsem.at[0], kvsem.at[1], me_dp, z * 4 + pair)

    for s in range(2):
        for t in range(TEN):
            hot_ref[4 * s + t : 4 * s + t + 1, :] = jnp.where(
                jnp.full((1, 128), tenant_ref[s]) == t, 1.0, 0.0
            )
    own = tenant_ref[me_t // 8]

    scale = HD ** (-0.5)
    scale2 = scale * math.log2(math.e)

    def sequence(turn, carry):
        s = (1 - z // 2 + turn) % 2
        base = pl.multiple_of(s * SEQ, SEQ)
        starts = [doc_ref[s, j] for j in range(4)]
        pos = lax.broadcasted_iota(jnp.int32, (SEQ, HD), 0)
        cb = jnp.broadcast_to(cos_ref[pl.ds(starts[0], 1), :], (SEQ, HD))
        sb = jnp.broadcast_to(sin_ref[pl.ds(starts[0], 1), :], (SEQ, HD))
        for j in range(1, 4):
            inside = pos >= starts[j]
            cb = jnp.where(inside, cos_ref[pl.ds(starts[j], 1), :], cb)
            sb = jnp.where(inside, sin_ref[pl.ds(starts[j], 1), :], sb)
        cp = cos_ref[...]
        sp = sin_ref[...]
        c_ref[...] = cp * cb + sp * sb
        s_ref[...] = sp * cb - cp * sb
        kt_ref[...] = k_ref[pl.ds(base, SEQ), :].T
        vt_ref[...] = v_ref[pl.ds(base, SEQ), :].T
        dk_ref[...] = jnp.zeros_like(dk_ref)
        dv_ref[...] = jnp.zeros_like(dv_ref)
        for h in range(2):
            cols = slice(h * HD, (h + 1) * HD)
            for i in range(SEQ // ROWS):
                width = (i + 1) * ROWS
                rows = pl.ds(base + i * ROWS, ROWS)
                keys = pl.ds(base, width)
                q = q_ref[rows, cols]
                g = g_ref[rows, cols]
                p_row = lax.broadcasted_iota(jnp.int32, (1, ROWS), 1) + i * ROWS
                begin = jnp.zeros((1, ROWS), jnp.int32)
                for j in range(1, 4):
                    begin = jnp.where(p_row >= starts[j], starts[j], begin)
                k_idx = lax.broadcasted_iota(jnp.int32, (width, ROWS), 0)
                st = lax.dot_general(k_ref[keys, :], q, NT, preferred_element_type=F32) * scale2
                far_keys = width - ROWS
                near_keys = k_idx[far_keys:]
                masked = jnp.where(
                    (near_keys >= begin) & (near_keys <= p_row), st[far_keys:], MASKED
                )
                if far_keys:
                    masked = jnp.concatenate(
                        [jnp.where(k_idx[:far_keys] >= begin, st[:far_keys], MASKED), masked], axis=0
                    )
                st = masked
                top = jnp.max(st, axis=0, keepdims=True)
                e = jnp.exp2(st - top)
                inv = 1.0 / jnp.sum(e, axis=0, keepdims=True)
                p = e * inv
                p_low = p.astype(BF16)
                ot = jnp.dot(vt_ref[:, :width], p_low, preferred_element_type=F32)
                delta = jnp.sum(g.astype(F32).T * ot, axis=0, keepdims=True)
                dpt = lax.dot_general(v_ref[keys, :], g, NT, preferred_element_type=F32)
                ds_low = (p * (dpt - delta)).astype(BF16)
                dqt = jnp.dot(kt_ref[:, :width], ds_low, preferred_element_type=F32)
                dk_ref[:width, :] += jnp.dot(ds_low, q, preferred_element_type=F32)
                dv_ref[:width, :] += jnp.dot(p_low, g, preferred_element_type=F32)
                dq = dqt.T * scale
                dq = dq * c_ref[i * ROWS : (i + 1) * ROWS, :] + pltpu.roll(
                    dq, HD // 2, 1
                ) * s_ref[i * ROWS : (i + 1) * ROWS, :]
                dq = dq.astype(BF16)
                grad_ref[rows, cols] = dq
                for n in range(4):
                    at = (i // 2) * QUARTER + (n % 2) * CHUNK + (2 * (i % 2) + n // 2) * 64
                    qall[x, pl.ds(base + at, 64), cols] = dq[n * 64 : (n + 1) * 64]
            if h == 0:

                @pl.when(turn == 0)
                def _():
                    incoming = weights_x(False)
                    outgoing = weights_y(True)
                    relayed = weights_core(True)
                    for n in range(4):
                        for copy in [incoming[n]] if n < 3 else incoming[3:]:
                            copy.wait_recv()
                        start(outgoing[3 * n : 3 * n + 3])
                        relayed[4 * n].start()

                @pl.when(turn == 1)
                def _():
                    arrive(0)

        dk = dk_ref[...] * scale
        dk = dk * c_ref[...] + pltpu.roll(dk, HD // 2, 1) * s_ref[...]
        for n, value in enumerate((dk.astype(BF16), dv_ref[...].astype(BF16))):
            grad_ref[pl.ds(base, SEQ), (2 + n) * HD : (3 + n) * HD] = value
            for b in range(16):
                at = (b // 8) * QUARTER + (b % 2) * CHUNK + (b % 8) // 2 * 64
                kvs[pl.ds(base + at, 64), n * HD : (n + 1) * HD] = value[b * 64 : (b + 1) * 64]
        t = tenant_ref[s]
        seq_rows = pl.ds(base, SEQ)
        parts = [
            (upq_ref[t], slice(0, 2 * HD)),
            (upkv_ref[t, :RANK, :], slice(2 * HD, 3 * HD)),
            (upkv_ref[t, RANK:, :], slice(3 * HD, 4 * HD)),
        ]
        for n, (up, c) in enumerate(parts):
            back = 2.0 * lax.dot_general(
                up, grad_ref[seq_rows, c], NT, preferred_element_type=F32
            )
            for b in range(8):
                dlow_ref[b % 4, 2 * s + b // 4, n * RANK : (n + 1) * RANK, :] = back[
                    :, b * 128 : (b + 1) * 128
                ].astype(BF16)

        start(dl_parts(turn, True))

        @pl.when(turn == 0)
        def _():
            start(gather_out(0))
            start(gather_out(3))
            w_own[3].wait()
            w_own[4].wait()
            lowx[x] = lax.dot_general(
                down_ref[own], x_ref[...], NT, preferred_element_type=F32
            ).astype(BF16)
            lowx_start()

        return carry

    lax.fori_loop(0, 2, sequence, 0)

    start(gather_out(1))
    start(gather_out(2))
    lowx_recv()
    lowz_start()
    lowall[z] = lowx[...]
    dlx_in[x] = dlow_ref[x]
    for turn in range(2):
        for copy in dl_parts(turn, False):
            copy.wait_recv()
    dlz_out[...] = (
        (dlx_in[0].astype(F32) + dlx_in[1].astype(F32))
        + (dlx_in[2].astype(F32) + dlx_in[3].astype(F32))
    ).astype(BF16)
    dlz_start()
    dlz_in[z] = dlz_out[z]

    def step_low():
        lowz_recv()
        for b in range(16):
            lowcat[:, b * 128 : (b + 1) * 128] = lowall[b // 4, b % 4]
        for s in range(2):
            rows = slice(s * SEQ, (s + 1) * SEQ)
            qown[s] = 2.0 * jnp.dot(
                lowcat[:RANK, rows], grad_ref[rows, 0:256], preferred_element_type=F32
            )
            kvown[s, :RANK, :] = 2.0 * jnp.dot(
                lowcat[RANK : 2 * RANK, rows], grad_ref[rows, 256:384], preferred_element_type=F32
            )
            kvown[s, RANK:, :] = 2.0 * jnp.dot(
                lowcat[2 * RANK :, rows], grad_ref[rows, 384:512], preferred_element_type=F32
            )
        kv_copy.start()

    def step_dlow():
        dlz_recv()
        dlw_ref[...] = (
            (dlz_in[0].astype(F32) + dlz_in[1].astype(F32))
            + (dlz_in[2].astype(F32) + dlz_in[3].astype(F32))
        ).astype(BF16)

        def column(t, c):
            gdown[t // 4, t % 4] = jnp.dot(
                dlw_ref[...], x_ref[:, pl.ds(pl.multiple_of(t * 512, 512), 512)],
                preferred_element_type=F32,
            ).astype(BF16)
            return c

        lax.fori_loop(0, 16, column, 0)
        dnz_start()
        dnz[z] = gdown[z]

    def step_down_x():
        dnz_recv()
        for s in range(2):
            for b in range(4):
                dnx_out[b, s] = (
                    dnz[2 * s, b].astype(F32) + dnz[2 * s + 1, b].astype(F32)
                ).astype(BF16)
        dnx_start()
        dnx_in[x] = dnx_out[x]

    def step_down():
        dnx_recv()
        kv_copy.wait_recv()
        for s in range(2):
            total = dnx_in[0, s].astype(F32)
            for b in range(1, 4):
                total = total + dnx_in[b, s].astype(F32)
            dsum[s] = total
            kvown_sum = kvown[s] + kvpeer[s]
            kvpeer[s] = kvown_sum
        for j in range(8):
            cb = j % 4
            for i in range(2):
                t = 2 * (j // 4) + i
                rsbuf[j, 48 * i : 48 * (i + 1), :] = (
                    dsum[0, :, cb * 128 : (cb + 1) * 128] * hot_ref[t : t + 1, :]
                    + dsum[1, :, cb * 128 : (cb + 1) * 128] * hot_ref[4 + t : 5 + t, :]
                )
            t = j // 2
            c = j % 2
            rsbuf[j, 96:112, :] = (
                qown[0, :, c * 128 : (c + 1) * 128] * hot_ref[t : t + 1, :]
                + qown[1, :, c * 128 : (c + 1) * 128] * hot_ref[4 + t : 5 + t, :]
            )
            rsbuf[j, 112:128, :] = (
                kvpeer[0, c * 16 : (c + 1) * 16, :] * hot_ref[t : t + 1, :]
                + kvpeer[1, c * 16 : (c + 1) * 16, :] * hot_ref[4 + t : 5 + t, :]
            )
        rs_start()
        rsall[me_dp] = rsbuf[me_dp]

    def step_reduce():
        rs_recv()
        total = rsall[0]
        for b in range(1, 8):
            total = total + rsall[b]
        agbuf[me_dp] = total
        ag_start()

    def parts_of(t):
        for n in range(3):
            lo = (t % 2) * 48 + n * 16
            yield [(t // 2) * 4 + cb for cb in range(4)], slice(lo, lo + 16)
        yield [2 * t, 2 * t + 1], slice(96, 112)
        yield [2 * t], slice(112, 128)
        yield [2 * t + 1], slice(112, 128)

    def step_squares():
        ag_recv()
        row = lax.broadcasted_iota(jnp.int32, (8, 128), 0)
        lane = lax.broadcasted_iota(jnp.int32, (8, 128), 1)
        tile = jnp.zeros((8, 128), F32)
        for t in range(TEN):
            for n, (pieces, rows) in enumerate(parts_of(t)):
                total = None
                for j in pieces:
                    v = agbuf[j, rows, :]
                    total = v * v if total is None else total + v * v
                value = jnp.sum(
                    jnp.sum(total, axis=0, keepdims=True), axis=1, keepdims=True
                )
                tile = jnp.where((row == t) & (lane == n), value, tile)
        sqall[me_t] = tile
        sq_start()

    def step_update():
        sq_recv()
        total = sqall[0]
        for b in range(1, 16):
            total = total + sqall[b]
        for t in range(TEN):
            for n, (pieces, rows) in enumerate(parts_of(t)):
                count = RANK * (8192 if n < 3 else 4096 if n == 3 else 2048)
                factor = 1.0 / jnp.sqrt(total[t : t + 1, n : n + 1] * (1.0 / count) + NORM_EPS)
                for i, j in enumerate(pieces):
                    value = agbuf[j, rows, :] * factor
                    if n < 3:
                        ud_ref[t, n * 16 : (n + 1) * 16, i * 128 : (i + 1) * 128] = value
                    elif n == 3:
                        uq_ref[t, :, i * 128 : (i + 1) * 128] = value
                    else:
                        ukv_ref[t, (n - 4) * 16 : (n - 3) * 16, :] = value

    def product(c, write):
        rows = pl.ds(first_row(c), CHUNK)
        def tile(n, carry):
            cols = pl.ds(pl.multiple_of(n * 512, 512), 512)
            acc = None
            for b in range(6):
                left = qall[b, rows, :] if b < 4 else kvm[b - 4, rows, :]
                term = lax.dot_general(left, wx[b, cols, :], NT, preferred_element_type=F32)
                acc = term if acc is None else acc + term
            write(cols, acc)
            return carry

        lax.fori_loop(0, 4, tile, 0)

    def z_copy(h, side, n):
        if n < 2:
            src, dst = part.at[h, side, n], zbuf.at[h, side, n]
        else:
            cols = pl.ds((n - 2) * 1024, 1024)
            src, dst = part.at[h, side, 2, :, cols], zbuf.at[h, side, 2, :, cols]
        return remote(
            src, dst, zsend.at[h, side, n], zrecv.at[h, side, n],
            me_dp, z_left if side else z_right,
        )

    def to_far(h):
        def write(cols, acc):
            part[h, 0, 0, :, cols] = acc[:SUB].astype(BF16)
            part[h, 1, 0, :, cols] = acc[SUB:].astype(BF16)

        return write

    def to_near(h, side):
        def write(cols, acc):
            part[h, side, 2 - side, :, cols] = acc[:SUB].astype(BF16)
            part[h, side, 1 + side, :, cols] = acc[SUB:].astype(BF16)

        return write

    def write_own(cols, acc):
        own_ref[0, :, cols] = acc[:SUB].astype(BF16)
        own_ref[1, :, cols] = acc[SUB:].astype(BF16)

    def far(h):
        product(3 * h, to_far(h))
        z_copy(h, 0, 0).start()
        z_copy(h, 1, 0).start()

    def near(h, side):
        product(3 * h + 1 + side, to_near(h, side))
        z_copy(h, side, 1).start()

    def add_far(h, side):
        z_copy(h, side, 0).wait_recv()
        for m in range(2):
            for n in range(2):
                cols = slice(m * 1024 + n * 512, m * 1024 + (n + 1) * 512)
                part[h, side, 2, :, cols] = (
                    part[h, side, 2, :, cols].astype(F32) + zbuf[h, side, 0, :, cols].astype(F32)
                ).astype(BF16)
            z_copy(h, side, 2 + m).start()

    def final_copy(o, h, m):
        rows, cols = pl.ds(h * 64, 64), pl.ds(m * 1024, 1024)
        return remote(
            fbuf.at[o, rows, cols], fin.at[x, rows, cols], fsend.at[o, h, m], frecv.at[x, h, m],
            me_dp, z * 4 + o,
        )

    def finish(h):
        for m in range(2):
            for side in range(2):
                if m == 0:
                    z_copy(h, side, 1).wait_recv()
                z_copy(h, side, 2 + m).wait_recv()
            for i in range(2):
                for n in range(2):
                    cols = slice(m * 1024 + n * 512, m * 1024 + (n + 1) * 512)
                    total = (
                        own_ref[i, :, cols].astype(F32)
                        + zbuf[h, 0, 2 - i, :, cols].astype(F32)
                        + zbuf[h, 1, 1 + i, :, cols].astype(F32)
                    ).astype(BF16)
                    fbuf[2 * i, h * 64 : (h + 1) * 64, cols] = total[:64]
                    fbuf[2 * i + 1, h * 64 : (h + 1) * 64, cols] = total[64:]
                for o in (2 * i, 2 * i + 1):

                    @pl.when(x != o)
                    def _(o=o, m=m):
                        final_copy(o, h, m).start()

    def deliver(h):
        rows = slice(h * 64, (h + 1) * 64)
        fin[x, rows, :] = fbuf[x, rows, :]
        for m in range(2):
            for o in range(1, 4):
                xs = (x + o) % 4
                block = fin.at[xs, pl.ds(h * 64, 64), pl.ds(m * 1024, 1024)]
                remote(
                    block, block, fsend.at[xs, h, m], frecv.at[xs, h, m], me_dp, z * 4 + xs
                ).wait_recv()
            for b in range(4):
                cols = slice(b * BLOCK_D + m * 1024, b * BLOCK_D + (m + 1) * 1024)
                out_ref[rows, cols] = (
                    fin[b, rows, m * 1024 : (m + 1) * 1024].astype(F32)
                    + out_ref[rows, cols].astype(F32)
                ).astype(BF16)

    def all_sent(h):
        for side in range(2):
            for n in range(4):
                z_copy(h, side, n).wait_send()
        for o in range(4):

            @pl.when(x != o)
            def _(o=o):
                final_copy(o, h, 0).wait_send()
                final_copy(o, h, 1).wait_send()

    def step_output():
        for n in range(16):
            cols = slice(n * 512, (n + 1) * 512)
            out_ref[:, cols] = lax.dot_general(
                dlw_ref[...], down_ref[own, :, cols], TN, preferred_element_type=F32
            ).astype(BF16)

    def ready(c):
        for copy in forward_in(c):
            copy.wait_recv()

    incoming = weights_y(False)
    relayed = weights_core(True)
    for n in range(4):
        for o in range(3):
            incoming[3 * n + o].wait_recv()
            relayed[4 * n + o + 1].start()
    step_dlow()
    arrive(1)
    start(gather_out(4))
    for copy in w_own[:3]:
        copy.wait()
    for copy in weights_core(False):
        copy.wait_recv()
    ready(0)
    far(0)
    arrive(2)
    start(gather_out(5))
    ready(1)
    near(0, 0)
    ready(2)
    near(0, 1)
    arrive(3)
    start(gather_out(6))
    add_far(0, 0)
    add_far(0, 1)
    step_low()
    arrive(4)
    start(gather_out(7))
    step_down_x()
    ready(3)
    far(1)
    arrive(5)
    ready(4)
    near(1, 0)
    ready(5)
    near(1, 1)
    arrive(6)
    step_down()
    ready(6)
    product(6, write_own)
    finish(0)
    arrive(7)
    add_far(1, 0)
    add_far(1, 1)
    step_reduce()
    ready(7)
    product(7, write_own)
    step_output()
    deliver(0)
    step_squares()
    finish(1)
    step_update()
    sq_sent()
    for c in range(8):
        for copy in gather_out(c) + forward_out(c):
            copy.wait_send()
    for copy in weights_x(True) + weights_y(True) + weights_core(True):
        copy.wait_send()
    for sent in (dlz_sent, lowx_sent, lowz_sent, dnz_sent, dnx_sent, rs_sent, ag_sent):
        sent()
    for turn in range(2):
        for copy in dl_parts(turn, True):
            copy.wait_send()
    kv_copy.wait_send()
    all_sent(0)
    deliver(1)
    all_sent(1)


def fused_call(tenant, docs, q, k, v, g, x, down, upq, upkv, wq, wk, wv):
    vmem = pl.BlockSpec(memory_space=pltpu.VMEM)
    smem = pl.BlockSpec(memory_space=pltpu.SMEM)
    hbm = pl.BlockSpec(memory_space=pl.ANY)
    dma = pltpu.SemaphoreType.DMA
    tokens = q.shape[0]
    cosine, sine = rope_constants()
    return pl.pallas_call(
        fused_kernel,
        in_specs=[smem] * 2 + [vmem] * 4 + [hbm] * 2 + [vmem] * 4 + [hbm] * 3,
        out_specs=[vmem] * 4,
        out_shape=[
            jax.ShapeDtypeStruct(x.shape, BF16),
            jax.ShapeDtypeStruct((TEN, 48, 512), F32),
            jax.ShapeDtypeStruct((TEN, RANK, 256), F32),
            jax.ShapeDtypeStruct((TEN, 2 * RANK, 128), F32),
        ],
        scratch_shapes=[
            pltpu.VMEM((tokens, 512), BF16),
            pltpu.VMEM((4, 4, 48, 128), BF16),
            pltpu.VMEM((48, 128), BF16),
            pltpu.VMEM((8, 128), F32),
            pltpu.VMEM((HD, SEQ), BF16), pltpu.VMEM((HD, SEQ), BF16),
            pltpu.VMEM((SEQ, HD), F32), pltpu.VMEM((SEQ, HD), F32),
            pltpu.VMEM((SEQ, HD), F32), pltpu.VMEM((SEQ, HD), F32),
            pltpu.VMEM((4, tokens, 256), BF16),
            pltpu.VMEM((tokens, 256), BF16), pltpu.VMEM((tokens, 256), BF16),
            pltpu.VMEM((2, tokens, 256), BF16),
            pltpu.VMEM((6, BLOCK_D, 256), BF16),
            pltpu.VMEM((2, 2, 3, SUB, BLOCK_D), BF16),
            pltpu.VMEM((2, 2, 3, SUB, BLOCK_D), BF16),
            pltpu.VMEM((2, SUB, BLOCK_D), BF16),
            pltpu.VMEM((4, SUB, BLOCK_D), BF16),
            pltpu.VMEM((4, SUB, BLOCK_D), BF16),
            pltpu.VMEM((4, 4, 48, 128), BF16),
            pltpu.VMEM((4, 48, 128), BF16), pltpu.VMEM((4, 48, 128), BF16),
            pltpu.VMEM((4, 48, 128), BF16),
            pltpu.VMEM((4, 4, 48, 128), BF16),
            pltpu.VMEM((48, tokens), BF16),
            pltpu.VMEM((48, 128), BF16),
            pltpu.VMEM((2, 32, 128), F32),
            pltpu.VMEM((2, 32, 128), F32),
            pltpu.VMEM((2, 16, 256), F32),
            pltpu.VMEM((4, 4, 48, 512), BF16),
            pltpu.VMEM((4, 4, 48, 512), BF16),
            pltpu.VMEM((4, 2, 48, 512), BF16), pltpu.VMEM((4, 2, 48, 512), BF16),
            pltpu.VMEM((2, 48, 512), F32),
            pltpu.VMEM((8, 128, 128), F32),
            pltpu.VMEM((8, 128, 128), F32),
            pltpu.VMEM((8, 128, 128), F32),
            pltpu.VMEM((16, 8, 128), F32),
            pltpu.VMEM(x.shape, BF16),
            pltpu.VMEM(down.shape, BF16),
            dma((5,)), dma((7,)), dma((7,)), dma((4, 3)), dma((4, 3)), dma((4, 4)), dma((4, 4)),
            dma((6, 8)), dma((6, 8)), dma((2, 4)), dma((2, 4)), dma((5, 4)), dma((5, 4)),
            dma((2,)), dma((8,)), dma((8,)), dma((8,)), dma((8,)),
            dma((16,)), dma((16,)), dma((2, 2, 4)), dma((2, 2, 4)), dma((4, 2, 2)), dma((4, 2, 2)),
        ],
        compiler_params=pltpu.CompilerParams(
            collective_id=0, has_side_effects=True, vmem_limit_bytes=63 * 1024 * 1024
        ),
        cost_estimate=pl.CostEstimate(
            flops=20_000_000_000, bytes_accessed=40_000_000, transcendentals=4_000_000
        ),
        name="exchange",
    )(tenant, docs, q, k, v, g, x, down, upq, upkv, cosine, sine, wq, wk, wv)


def per_device(
    x_rows, d_attn, q_saved, k_saved, v_saved, w_query, w_key, w_value, down_all, up_query, up_kv,
    tenant, doc_starts,
):
    return tuple(
        fused_call(
            tenant, doc_starts, q_saved, k_saved, v_saved, d_attn, x_rows, down_all, up_query,
            up_kv, w_query, w_key, w_value,
        )
    )


def solution(mesh):
    in_specs = (
        P(("dp", "tensor"), None),
        P("dp", "tensor"),
        P("dp", "tensor"),
        P("dp", "tensor"),
        P("dp", "tensor"),
        P(None, "tensor"),
        P(None, "tensor"),
        P(None, "tensor"),
        P(),
        P(None, None, "tensor"),
        P(None, None, "tensor"),
        P("dp"),
        P("dp", None),
    )
    out_specs = (
        P(("dp", "tensor"), None),
        P(None, None, "tensor"),
        P(None, None, "tensor"),
        P(None, None, "tensor"),
    )
    return jax.shard_map(
        per_device, mesh=mesh, in_specs=in_specs, out_specs=out_specs, check_vma=False
    )
```

```python
import functools
import math
import numpy as np
import jax
import jax.numpy as jnp
from jax import lax
from jax.experimental import pallas as pl
from jax.experimental.pallas import tpu as pltpu
from jax.sharding import PartitionSpec as P

HD = 128
RANK = 16
TEN = 4
SEQ = 1024
ROPE_BASE = 500000.0
NORM_EPS = 1e-06
MASKED = -1e30
NT = (((1,), (1,)), ((), ()))
TN = (((0,), (0,)), ((), ()))
F32 = jnp.float32
BF16 = jnp.bfloat16
ROWS = 256


def rope_constants():
    half = HD // 2
    freq = ROPE_BASE ** (-(2.0 * np.arange(half)) / HD)
    angle = np.arange(SEQ)[:, None] * freq[None, :]
    cosine = np.concatenate([np.cos(angle), np.cos(angle)], axis=1)
    sine = np.concatenate([np.sin(angle), -np.sin(angle)], axis=1)
    return cosine.astype(np.float32), sine.astype(np.float32)


MESH_ID = pl.DeviceIdType.MESH
CHUNK = 256
SUB = 128
QUARTER = 512
BLOCK_D = 2048
ORDER = ((2, 0), (1, 0), (3, 0), (2, 1), (1, 1), (3, 1), (0, 0), (0, 1))


def fused_kernel(
    tenant_ref, doc_ref, q_ref, k_ref, v_ref, g_ref, x_hbm, down_hbm, upq_ref, upkv_ref,
    cos_ref, sin_ref, wq_ref, wk_ref, wv_ref,
    out_ref, ud_ref, uq_ref, ukv_ref,
    grad_ref, dlow_ref, low_ref, hot_ref, kt_ref, vt_ref, dk_ref, dv_ref, c_ref, s_ref,
    qall, kvs, kvp, kvm, wx, part, zbuf, own_ref, fbuf, fin,
    dlx_in, dlz_out, dlz_in, lowx, lowall, lowcat, dlw_ref, kvown, kvpeer, qown,
    gdown, dnz, dnx_out, dnx_in, dsum,
    rsbuf, rsall, agbuf, sqall, x_ref, down_ref,
    wsem, wxsend, wxrecv, wysend, wyrecv, wcsend, wcrecv,
    gsend, grecv, dlsend, dlrecv, esend, erecv, kvsem,
    rssend, rsrecv, agsend, agrecv, sqsend, sqrecv, zsend, zrecv, fsend, frecv,
):
    me_dp = lax.axis_index("dp")
    me_t = lax.axis_index("tensor")
    z = me_t // 4
    x = me_t % 4
    core = me_dp % 2
    xo = (x + 2) % 4
    pair = x + 1 - 2 * (x % 2)
    mirror = 3 - x
    z_right = ((z + 1) % 4) * 4 + x
    z_left = ((z + 3) % 4) * 4 + x

    def remote(src, dst, ssem, rsem, dp, t):
        return pltpu.make_async_remote_copy(
            src_ref=src, dst_ref=dst, send_sem=ssem, recv_sem=rsem,
            device_id=(dp, t), device_id_type=MESH_ID,
        )

    barrier = pltpu.get_barrier_semaphore()

    def greet_tensor(o, c):
        pl.semaphore_signal(
            barrier, inc=1, device_id=(me_dp, (me_t + o) % 16), device_id_type=MESH_ID
        )
        return c

    def greet_dp(o, c):
        pl.semaphore_signal(
            barrier, inc=1, device_id=((me_dp + o) % 8, me_t), device_id_type=MESH_ID
        )
        return c

    lax.fori_loop(1, 16, greet_tensor, 0)
    lax.fori_loop(1, 8, greet_dp, 0)

    y = me_dp // 2
    kv_here = 4 + x // 2
    kv_there = 5 - x // 2
    blocks = (pair, xo, mirror, kv_there)
    my_part = core * 1024 + y * 256
    d0 = pl.multiple_of(x * BLOCK_D, BLOCK_D)

    def rows_at(start, count):
        return pl.ds(pl.multiple_of(start, count), count)

    w_own = [
        pltpu.make_async_copy(src, dst, wsem.at[i])
        for i, (src, dst) in enumerate((
            (wq_ref.at[pl.ds(d0, BLOCK_D), :], wx.at[x]),
            (wk_ref.at[pl.ds(d0, BLOCK_D), :], wx.at[kv_here, :, pl.ds(0, 128)]),
            (wv_ref.at[pl.ds(d0, BLOCK_D), :], wx.at[kv_here, :, pl.ds(128, 128)]),
            (x_hbm, x_ref),
            (down_hbm, down_ref),
        ))
    ]

    def weights_x(sending):
        copies = []
        for i, xs in enumerate((pair, xo, mirror)):
            if sending:
                src = wq_ref.at[rows_at(xs * BLOCK_D + my_part, 256), :]
                dst = wx.at[x, rows_at(my_part, 256), :]
            else:
                src = dst = wx.at[xs, rows_at(my_part, 256), :]
            copies.append(remote(src, dst, wxsend.at[i], wxrecv.at[i], me_dp, z * 4 + xs))
        for i, xs in enumerate((xo, mirror)):
            for n, w in enumerate((wk_ref, wv_ref)):
                lanes = pl.ds(128 * n, 128)
                if sending:
                    row = my_part + (x % 2) * 128
                    src = w.at[rows_at(xs * BLOCK_D + row, 128), :]
                    dst = wx.at[kv_here, rows_at(row, 128), lanes]
                else:
                    row = my_part + (xs % 2) * 128
                    src = dst = wx.at[kv_there, rows_at(row, 128), lanes]
                k = 3 + 2 * i + n
                copies.append(remote(src, dst, wxsend.at[k], wxrecv.at[k], me_dp, z * 4 + xs))
        return copies

    def weights_y(sending):
        copies = []
        for i, b in enumerate(blocks):
            for o in range(1, 4):
                at_y = y if sending else (y + 4 - o) % 4
                ref = wx.at[b, rows_at(core * 1024 + at_y * 256, 256), :]
                to = ((y + o) % 4) * 2 + core
                copies.append(
                    remote(ref, ref, wysend.at[i, o - 1], wyrecv.at[i, o - 1], to, me_t)
                )
        return copies

    def weights_core(sending):
        copies = []
        for i, b in enumerate(blocks):
            for o in range(4):
                at_y = (y + 4 - o) % 4
                at_core = core if sending else 1 - core
                ref = wx.at[b, rows_at(at_core * 1024 + at_y * 256, 256), :]
                to = me_dp + 1 - 2 * core
                copies.append(remote(ref, ref, wcsend.at[i, o], wcrecv.at[i, o], to, me_t))
        return copies

    pl.semaphore_wait(barrier, 22)
    for copy in weights_x(True) + w_own:
        copy.start()

    def first_row(c):
        off, half = ORDER[c]
        return pl.multiple_of(((z + off) % 4) * QUARTER + half * CHUNK, CHUNK)

    def gather(c, n, src, dst, to):
        return remote(src, dst, gsend.at[n, c], grecv.at[n, c], me_dp, z * 4 + to)

    def gather_out(c):
        rows = pl.ds(first_row(c), CHUNK)
        mine = qall.at[x, rows, :]
        return (
            gather(c, 0, mine, mine, pair),
            gather(c, 2, mine, mine, mirror),
            gather(c, 1, kvs.at[rows, :], kvp.at[rows, :], pair),
        )

    def gather_in(c):
        rows = pl.ds(first_row(c), CHUNK)
        refs = (qall.at[pair, rows, :], qall.at[mirror, rows, :], kvp.at[rows, :])
        return [gather(c, n, ref, ref, to) for n, ref, to in zip((0, 2, 1), refs, (pair, mirror, pair))]

    def half_rows(c, n):
        return pl.ds(pl.multiple_of(first_row(c) + n * SUB, SUB), SUB)

    def forward_out(c):
        to_pair = qall.at[mirror, half_rows(c, 0), :]
        to_mirror = qall.at[pair, half_rows(c, 1), :]
        summed = kvm.at[x // 2, pl.ds(first_row(c), CHUNK), :]
        return (
            gather(c, 3, to_pair, to_pair, pair),
            gather(c, 4, to_mirror, to_mirror, mirror),
            gather(c, 5, summed, summed, mirror),
        )

    def forward_in(c):
        refs = (
            qall.at[xo, half_rows(c, 0), :], qall.at[xo, half_rows(c, 1), :],
            kvm.at[1 - x // 2, pl.ds(first_row(c), CHUNK), :],
        )
        return [gather(c, 3 + n, ref, ref, to) for n, (ref, to) in enumerate(zip(refs, (pair, mirror, mirror)))]

    def start(copies):
        for copy in copies:
            copy.start()

    def beside(first):
        @pl.when(z % 2 == 0)
        def _():
            start(gather_out(2 if first else 1))

        @pl.when(z % 2 == 1)
        def _():
            start(gather_out(1 if first else 2))

    def arrive(c):
        for copy in gather_in(c):
            copy.wait_recv()
        rows = pl.ds(first_row(c), CHUNK)
        outgoing = forward_out(c)
        outgoing[0].start()
        outgoing[1].start()
        kvm[x // 2, rows, :] = (kvs[rows, :].astype(F32) + kvp[rows, :].astype(F32)).astype(BF16)
        outgoing[2].start()

    def to_tensor(src, buf, ssem, rsem, picked):
        def descriptor(t):
            return remote(
                src.at[t] if picked else src, buf.at[me_t], ssem.at[t], rsem.at[me_t], me_dp, t
            )

        def begin(o, c):
            descriptor((me_t + o) % 16).start()
            return c

        def receive(o, c):
            t = (me_t + o) % 16
            remote(buf.at[t], buf.at[t], ssem.at[t], rsem.at[t], me_dp, t).wait_recv()
            return c

        def sent(o, c):
            descriptor((me_t + o) % 16).wait_send()
            return c

        return (
            lambda: lax.fori_loop(1, 16, begin, 0),
            lambda: lax.fori_loop(1, 16, receive, 0),
            lambda: lax.fori_loop(1, 16, sent, 0),
        )

    def to_dp(src_at, buf, ssem, rsem):
        def descriptor(d):
            return remote(src_at(d), buf.at[me_dp], ssem.at[d], rsem.at[me_dp], d, me_t)

        def begin(o, c):
            descriptor((me_dp + o) % 8).start()
            return c

        def receive(o, c):
            d = (me_dp + o) % 8
            remote(buf.at[d], buf.at[d], ssem.at[d], rsem.at[d], d, me_t).wait_recv()
            return c

        def sent(o, c):
            descriptor((me_dp + o) % 8).wait_send()
            return c

        return (
            lambda: lax.fori_loop(1, 8, begin, 0),
            lambda: lax.fori_loop(1, 8, receive, 0),
            lambda: lax.fori_loop(1, 8, sent, 0),
        )

    def to_line(along, i, src_at, buf):
        at = x if along == "x" else z
        peers = []
        for o in range(1, 4):
            p = (at + o) % 4
            peers.append((p, z * 4 + p if along == "x" else p * 4 + x))

        def out():
            return [
                remote(src_at(p), buf.at[at], esend.at[i, p], erecv.at[i, at], me_dp, t)
                for p, t in peers
            ]

        def begin():
            start(out())

        def receive():
            for p, t in peers:
                remote(
                    buf.at[p], buf.at[p], esend.at[i, p], erecv.at[i, p], me_dp, t
                ).wait_recv()

        def sent():
            for copy in out():
                copy.wait_send()

        return begin, receive, sent

    def dl_parts(turn, sending):
        s = (1 - z // 2 + turn) % 2
        copies = []
        for o in range(1, 4):
            p = (x + o) % 4
            if sending:
                src, dst = dlow_ref.at[p, pl.ds(2 * s, 2)], dlx_in.at[x, pl.ds(2 * s, 2)]
                sems = (dlsend.at[turn, p], dlrecv.at[turn, x])
            else:
                src = dst = dlx_in.at[p, pl.ds(2 * s, 2)]
                sems = (dlsend.at[turn, p], dlrecv.at[turn, p])
            copies.append(remote(src, dst, *sems, me_dp, z * 4 + p))
        return copies

    dlz_start, dlz_recv, dlz_sent = to_line("z", 0, lambda p: dlz_out.at[p], dlz_in)
    lowx_start, lowx_recv, lowx_sent = to_line("x", 1, lambda p: lowx.at[x], lowx)
    lowz_start, lowz_recv, lowz_sent = to_line("z", 2, lambda p: lowx, lowall)
    dnz_start, dnz_recv, dnz_sent = to_line("z", 3, lambda p: gdown.at[p], dnz)
    dnx_start, dnx_recv, dnx_sent = to_line("x", 4, lambda p: dnx_out.at[p], dnx_in)
    sq_start, sq_recv, sq_sent = to_tensor(sqall.at[me_t], sqall, sqsend, sqrecv, False)
    rs_start, rs_recv, rs_sent = to_dp(lambda d: rsbuf.at[d], rsall, rssend, rsrecv)
    ag_start, ag_recv, ag_sent = to_dp(lambda d: agbuf.at[me_dp], agbuf, agsend, agrecv)
    kv_copy = remote(kvown, kvpeer, kvsem.at[0], kvsem.at[1], me_dp, z * 4 + pair)

    for s in range(2):
        for t in range(TEN):
            hot_ref[4 * s + t : 4 * s + t + 1, :] = jnp.where(
                jnp.full((1, 128), tenant_ref[s]) == t, 1.0, 0.0
            )
    own = tenant_ref[me_t // 8]

    scale = HD ** (-0.5)
    scale2 = scale * math.log2(math.e)

    def sequence(turn, carry):
        s = (1 - z // 2 + turn) % 2
        base = pl.multiple_of(s * SEQ, SEQ)
        starts = [doc_ref[s, j] for j in range(4)]
        pos = lax.broadcasted_iota(jnp.int32, (SEQ, HD), 0)
        cb = jnp.broadcast_to(cos_ref[pl.ds(starts[0], 1), :], (SEQ, HD))
        sb = jnp.broadcast_to(sin_ref[pl.ds(starts[0], 1), :], (SEQ, HD))
        for j in range(1, 4):
            inside = pos >= starts[j]
            cb = jnp.where(inside, cos_ref[pl.ds(starts[j], 1), :], cb)
            sb = jnp.where(inside, sin_ref[pl.ds(starts[j], 1), :], sb)
        cp = cos_ref[...]
        sp = sin_ref[...]
        c_ref[...] = cp * cb + sp * sb
        s_ref[...] = sp * cb - cp * sb
        kt_ref[...] = k_ref[pl.ds(base, SEQ), :].T
        vt_ref[...] = v_ref[pl.ds(base, SEQ), :].T
        dk_ref[...] = jnp.zeros_like(dk_ref)
        dv_ref[...] = jnp.zeros_like(dv_ref)
        for h in range(2):
            cols = slice(h * HD, (h + 1) * HD)
            for i in range(SEQ // ROWS):
                width = (i + 1) * ROWS
                rows = pl.ds(base + i * ROWS, ROWS)
                keys = pl.ds(base, width)
                q = q_ref[rows, cols]
                g = g_ref[rows, cols]
                p_row = lax.broadcasted_iota(jnp.int32, (1, ROWS), 1) + i * ROWS
                begin = jnp.zeros((1, ROWS), jnp.int32)
                for j in range(1, 4):
                    begin = jnp.where(p_row >= starts[j], starts[j], begin)
                k_idx = lax.broadcasted_iota(jnp.int32, (width, ROWS), 0)
                st = lax.dot_general(k_ref[keys, :], q, NT, preferred_element_type=F32) * scale2
                far_keys = width - ROWS
                near_keys = k_idx[far_keys:]
                masked = jnp.where(
                    (near_keys >= begin) & (near_keys <= p_row), st[far_keys:], MASKED
                )
                if far_keys:
                    masked = jnp.concatenate(
                        [jnp.where(k_idx[:far_keys] >= begin, st[:far_keys], MASKED), masked], axis=0
                    )
                st = masked
                top = jnp.max(st, axis=0, keepdims=True)
                e = jnp.exp2(st - top)
                inv = 1.0 / jnp.sum(e, axis=0, keepdims=True)
                p = e * inv
                p_low = p.astype(BF16)
                ot = jnp.dot(vt_ref[:, :width], p_low, preferred_element_type=F32)
                delta = jnp.sum(g.astype(F32).T * ot, axis=0, keepdims=True)
                dpt = lax.dot_general(v_ref[keys, :], g, NT, preferred_element_type=F32)
                ds_low = (p * (dpt - delta)).astype(BF16)
                dqt = jnp.dot(kt_ref[:, :width], ds_low, preferred_element_type=F32)
                dk_ref[:width, :] += jnp.dot(ds_low, q, preferred_element_type=F32)
                dv_ref[:width, :] += jnp.dot(p_low, g, preferred_element_type=F32)
                dq = dqt.T * scale
                dq = dq * c_ref[i * ROWS : (i + 1) * ROWS, :] + pltpu.roll(
                    dq, HD // 2, 1
                ) * s_ref[i * ROWS : (i + 1) * ROWS, :]
                dq = dq.astype(BF16)
                grad_ref[rows, cols] = dq
                for n in range(4):
                    at = (i // 2) * QUARTER + (n % 2) * CHUNK + (2 * (i % 2) + n // 2) * 64
                    qall[x, pl.ds(base + at, 64), cols] = dq[n * 64 : (n + 1) * 64]
            if h == 0:

                @pl.when(turn == 0)
                def _():
                    incoming = weights_x(False)
                    outgoing = weights_y(True)
                    relayed = weights_core(True)
                    for n in range(4):
                        for copy in [incoming[n]] if n < 3 else incoming[3:]:
                            copy.wait_recv()
                        start(outgoing[3 * n : 3 * n + 3])
                        relayed[4 * n].start()

                @pl.when(turn == 1)
                def _():
                    arrive(0)

        dk = dk_ref[...] * scale
        dk = dk * c_ref[...] + pltpu.roll(dk, HD // 2, 1) * s_ref[...]
        for n, value in enumerate((dk.astype(BF16), dv_ref[...].astype(BF16))):
            grad_ref[pl.ds(base, SEQ), (2 + n) * HD : (3 + n) * HD] = value
            for b in range(16):
                at = (b // 8) * QUARTER + (b % 2) * CHUNK + (b % 8) // 2 * 64
                kvs[pl.ds(base + at, 64), n * HD : (n + 1) * HD] = value[b * 64 : (b + 1) * 64]
        t = tenant_ref[s]
        seq_rows = pl.ds(base, SEQ)
        parts = [
            (upq_ref[t], slice(0, 2 * HD)),
            (upkv_ref[t, :RANK, :], slice(2 * HD, 3 * HD)),
            (upkv_ref[t, RANK:, :], slice(3 * HD, 4 * HD)),
        ]
        for n, (up, c) in enumerate(parts):
            back = 2.0 * lax.dot_general(
                up, grad_ref[seq_rows, c], NT, preferred_element_type=F32
            )
            for b in range(8):
                dlow_ref[b % 4, 2 * s + b // 4, n * RANK : (n + 1) * RANK, :] = back[
                    :, b * 128 : (b + 1) * 128
                ].astype(BF16)

        start(dl_parts(turn, True))

        @pl.when(turn == 0)
        def _():
            start(gather_out(0))
            beside(True)
            w_own[3].wait()
            w_own[4].wait()
            lowx[x] = lax.dot_general(
                down_ref[own], x_ref[...], NT, preferred_element_type=F32
            ).astype(BF16)
            lowx_start()

        return carry

    lax.fori_loop(0, 2, sequence, 0)

    beside(False)
    start(gather_out(3))
    lowx_recv()
    lowz_start()
    lowall[z] = lowx[...]
    dlx_in[x] = dlow_ref[x]
    for turn in range(2):
        for copy in dl_parts(turn, False):
            copy.wait_recv()
    dlz_out[...] = (
        (dlx_in[0].astype(F32) + dlx_in[1].astype(F32))
        + (dlx_in[2].astype(F32) + dlx_in[3].astype(F32))
    ).astype(BF16)
    dlz_start()
    dlz_in[z] = dlz_out[z]

    def step_low():
        lowz_recv()
        for b in range(16):
            lowcat[:, b * 128 : (b + 1) * 128] = lowall[b // 4, b % 4]
        for s in range(2):
            rows = slice(s * SEQ, (s + 1) * SEQ)
            qown[s] = 2.0 * jnp.dot(
                lowcat[:RANK, rows], grad_ref[rows, 0:256], preferred_element_type=F32
            )
            kvown[s, :RANK, :] = 2.0 * jnp.dot(
                lowcat[RANK : 2 * RANK, rows], grad_ref[rows, 256:384], preferred_element_type=F32
            )
            kvown[s, RANK:, :] = 2.0 * jnp.dot(
                lowcat[2 * RANK :, rows], grad_ref[rows, 384:512], preferred_element_type=F32
            )
        kv_copy.start()

    def step_dlow():
        dlz_recv()
        dlw_ref[...] = (
            (dlz_in[0].astype(F32) + dlz_in[1].astype(F32))
            + (dlz_in[2].astype(F32) + dlz_in[3].astype(F32))
        ).astype(BF16)

        def column(t, c):
            gdown[t // 4, t % 4] = jnp.dot(
                dlw_ref[...], x_ref[:, pl.ds(pl.multiple_of(t * 512, 512), 512)],
                preferred_element_type=F32,
            ).astype(BF16)
            return c

        lax.fori_loop(0, 16, column, 0)
        dnz_start()
        dnz[z] = gdown[z]

    def step_down_x():
        dnz_recv()
        for s in range(2):
            for b in range(4):
                dnx_out[b, s] = (
                    dnz[2 * s, b].astype(F32) + dnz[2 * s + 1, b].astype(F32)
                ).astype(BF16)
        dnx_start()
        dnx_in[x] = dnx_out[x]

    def step_down():
        dnx_recv()
        kv_copy.wait_recv()
        for s in range(2):
            total = dnx_in[0, s].astype(F32)
            for b in range(1, 4):
                total = total + dnx_in[b, s].astype(F32)
            dsum[s] = total
            kvown_sum = kvown[s] + kvpeer[s]
            kvpeer[s] = kvown_sum
        for j in range(8):
            cb = j % 4
            for i in range(2):
                t = 2 * (j // 4) + i
                rsbuf[j, 48 * i : 48 * (i + 1), :] = (
                    dsum[0, :, cb * 128 : (cb + 1) * 128] * hot_ref[t : t + 1, :]
                    + dsum[1, :, cb * 128 : (cb + 1) * 128] * hot_ref[4 + t : 5 + t, :]
                )
            t = j // 2
            c = j % 2
            rsbuf[j, 96:112, :] = (
                qown[0, :, c * 128 : (c + 1) * 128] * hot_ref[t : t + 1, :]
                + qown[1, :, c * 128 : (c + 1) * 128] * hot_ref[4 + t : 5 + t, :]
            )
            rsbuf[j, 112:128, :] = (
                kvpeer[0, c * 16 : (c + 1) * 16, :] * hot_ref[t : t + 1, :]
                + kvpeer[1, c * 16 : (c + 1) * 16, :] * hot_ref[4 + t : 5 + t, :]
            )
        rs_start()
        rsall[me_dp] = rsbuf[me_dp]

    def step_reduce():
        rs_recv()
        total = rsall[0]
        for b in range(1, 8):
            total = total + rsall[b]
        agbuf[me_dp] = total
        ag_start()

    def parts_of(t):
        for n in range(3):
            lo = (t % 2) * 48 + n * 16
            yield [(t // 2) * 4 + cb for cb in range(4)], slice(lo, lo + 16)
        yield [2 * t, 2 * t + 1], slice(96, 112)
        yield [2 * t], slice(112, 128)
        yield [2 * t + 1], slice(112, 128)

    def step_squares():
        ag_recv()
        row = lax.broadcasted_iota(jnp.int32, (8, 128), 0)
        lane = lax.broadcasted_iota(jnp.int32, (8, 128), 1)
        tile = jnp.zeros((8, 128), F32)
        for t in range(TEN):
            for n, (pieces, rows) in enumerate(parts_of(t)):
                total = None
                for j in pieces:
                    v = agbuf[j, rows, :]
                    total = v * v if total is None else total + v * v
                value = jnp.sum(
                    jnp.sum(total, axis=0, keepdims=True), axis=1, keepdims=True
                )
                tile = jnp.where((row == t) & (lane == n), value, tile)
        sqall[me_t] = tile
        sq_start()

    def step_update():
        sq_recv()
        total = sqall[0]
        for b in range(1, 16):
            total = total + sqall[b]
        for t in range(TEN):
            for n, (pieces, rows) in enumerate(parts_of(t)):
                count = RANK * (8192 if n < 3 else 4096 if n == 3 else 2048)
                factor = 1.0 / jnp.sqrt(total[t : t + 1, n : n + 1] * (1.0 / count) + NORM_EPS)
                for i, j in enumerate(pieces):
                    value = agbuf[j, rows, :] * factor
                    if n < 3:
                        ud_ref[t, n * 16 : (n + 1) * 16, i * 128 : (i + 1) * 128] = value
                    elif n == 3:
                        uq_ref[t, :, i * 128 : (i + 1) * 128] = value
                    else:
                        ukv_ref[t, (n - 4) * 16 : (n - 3) * 16, :] = value

    def product(c, write):
        rows = pl.ds(first_row(c), CHUNK)
        def tile(n, carry):
            cols = pl.ds(pl.multiple_of(n * 512, 512), 512)
            acc = None
            for b in range(6):
                left = qall[b, rows, :] if b < 4 else kvm[b - 4, rows, :]
                term = lax.dot_general(left, wx[b, cols, :], NT, preferred_element_type=F32)
                acc = term if acc is None else acc + term
            write(cols, acc)
            return carry

        lax.fori_loop(0, 4, tile, 0)

    def z_copy(h, side, n):
        if n < 2:
            src, dst = part.at[h, side, n], zbuf.at[h, side, n]
        else:
            cols = pl.ds((n - 2) * 1024, 1024)
            src, dst = part.at[h, side, 2, :, cols], zbuf.at[h, side, 2, :, cols]
        return remote(
            src, dst, zsend.at[h, side, n], zrecv.at[h, side, n],
            me_dp, z_left if side else z_right,
        )

    def to_far(h):
        def write(cols, acc):
            part[h, 0, 0, :, cols] = acc[:SUB].astype(BF16)
            part[h, 1, 0, :, cols] = acc[SUB:].astype(BF16)

        return write

    def to_near(h, side):
        def write(cols, acc):
            part[h, side, 2 - side, :, cols] = acc[:SUB].astype(BF16)
            part[h, side, 1 + side, :, cols] = acc[SUB:].astype(BF16)

        return write

    def write_own(cols, acc):
        own_ref[0, :, cols] = acc[:SUB].astype(BF16)
        own_ref[1, :, cols] = acc[SUB:].astype(BF16)

    def far(h):
        product(3 * h, to_far(h))
        z_copy(h, 0, 0).start()
        z_copy(h, 1, 0).start()

    def near(h, side):
        product(3 * h + 1 + side, to_near(h, side))
        z_copy(h, side, 1).start()

    def add_far(h, side):
        z_copy(h, side, 0).wait_recv()
        for m in range(2):
            for n in range(2):
                cols = slice(m * 1024 + n * 512, m * 1024 + (n + 1) * 512)
                part[h, side, 2, :, cols] = (
                    part[h, side, 2, :, cols].astype(F32) + zbuf[h, side, 0, :, cols].astype(F32)
                ).astype(BF16)
            z_copy(h, side, 2 + m).start()

    def final_copy(o, h, m):
        rows, cols = pl.ds(h * 64, 64), pl.ds(m * 1024, 1024)
        return remote(
            fbuf.at[o, rows, cols], fin.at[x, rows, cols], fsend.at[o, h, m], frecv.at[x, h, m],
            me_dp, z * 4 + o,
        )

    def finish(h):
        for m in range(2):
            for side in range(2):
                if m == 0:
                    z_copy(h, side, 1).wait_recv()
                z_copy(h, side, 2 + m).wait_recv()
            for i in range(2):
                for n in range(2):
                    cols = slice(m * 1024 + n * 512, m * 1024 + (n + 1) * 512)
                    total = (
                        own_ref[i, :, cols].astype(F32)
                        + zbuf[h, 0, 2 - i, :, cols].astype(F32)
                        + zbuf[h, 1, 1 + i, :, cols].astype(F32)
                    ).astype(BF16)
                    fbuf[2 * i, h * 64 : (h + 1) * 64, cols] = total[:64]
                    fbuf[2 * i + 1, h * 64 : (h + 1) * 64, cols] = total[64:]
                for o in (2 * i, 2 * i + 1):

                    @pl.when(x != o)
                    def _(o=o, m=m):
                        final_copy(o, h, m).start()

    def deliver(h):
        rows = slice(h * 64, (h + 1) * 64)
        fin[x, rows, :] = fbuf[x, rows, :]
        for m in range(2):
            for o in range(1, 4):
                xs = (x + o) % 4
                block = fin.at[xs, pl.ds(h * 64, 64), pl.ds(m * 1024, 1024)]
                remote(
                    block, block, fsend.at[xs, h, m], frecv.at[xs, h, m], me_dp, z * 4 + xs
                ).wait_recv()
            for b in range(4):
                cols = slice(b * BLOCK_D + m * 1024, b * BLOCK_D + (m + 1) * 1024)
                out_ref[rows, cols] = (
                    fin[b, rows, m * 1024 : (m + 1) * 1024].astype(F32)
                    + out_ref[rows, cols].astype(F32)
                ).astype(BF16)

    def all_sent(h):
        for side in range(2):
            for n in range(4):
                z_copy(h, side, n).wait_send()
        for o in range(4):

            @pl.when(x != o)
            def _(o=o):
                final_copy(o, h, 0).wait_send()
                final_copy(o, h, 1).wait_send()

    def step_output():
        for n in range(16):
            cols = slice(n * 512, (n + 1) * 512)
            out_ref[:, cols] = lax.dot_general(
                dlw_ref[...], down_ref[own, :, cols], TN, preferred_element_type=F32
            ).astype(BF16)

    def ready(c):
        for copy in forward_in(c):
            copy.wait_recv()

    incoming = weights_y(False)
    relayed = weights_core(True)
    for n in range(4):
        for o in range(3):
            incoming[3 * n + o].wait_recv()
            relayed[4 * n + o + 1].start()
    step_dlow()
    arrive(1)
    start(gather_out(4))
    for copy in w_own[:3]:
        copy.wait()
    for copy in weights_core(False):
        copy.wait_recv()
    ready(0)
    far(0)
    arrive(2)
    start(gather_out(5))
    ready(1)
    near(0, 0)
    ready(2)
    near(0, 1)
    arrive(3)
    start(gather_out(6))
    add_far(0, 0)
    add_far(0, 1)
    step_low()
    arrive(4)
    start(gather_out(7))
    step_down_x()
    ready(3)
    far(1)
    arrive(5)
    ready(4)
    near(1, 0)
    ready(5)
    near(1, 1)
    arrive(6)
    step_down()
    ready(6)
    product(6, write_own)
    finish(0)
    arrive(7)
    add_far(1, 0)
    add_far(1, 1)
    step_reduce()
    ready(7)
    product(7, write_own)
    step_output()
    deliver(0)
    step_squares()
    finish(1)
    step_update()
    sq_sent()
    for c in range(8):
        for copy in gather_out(c) + forward_out(c):
            copy.wait_send()
    for copy in weights_x(True) + weights_y(True) + weights_core(True):
        copy.wait_send()
    for sent in (dlz_sent, lowx_sent, lowz_sent, dnz_sent, dnx_sent, rs_sent, ag_sent):
        sent()
    for turn in range(2):
        for copy in dl_parts(turn, True):
            copy.wait_send()
    kv_copy.wait_send()
    all_sent(0)
    deliver(1)
    all_sent(1)


def fused_call(tenant, docs, q, k, v, g, x, down, upq, upkv, wq, wk, wv):
    vmem = pl.BlockSpec(memory_space=pltpu.VMEM)
    smem = pl.BlockSpec(memory_space=pltpu.SMEM)
    hbm = pl.BlockSpec(memory_space=pl.ANY)
    dma = pltpu.SemaphoreType.DMA
    tokens = q.shape[0]
    cosine, sine = rope_constants()
    return pl.pallas_call(
        fused_kernel,
        in_specs=[smem] * 2 + [vmem] * 4 + [hbm] * 2 + [vmem] * 4 + [hbm] * 3,
        out_specs=[vmem] * 4,
        out_shape=[
            jax.ShapeDtypeStruct(x.shape, BF16),
            jax.ShapeDtypeStruct((TEN, 48, 512), F32),
            jax.ShapeDtypeStruct((TEN, RANK, 256), F32),
            jax.ShapeDtypeStruct((TEN, 2 * RANK, 128), F32),
        ],
        scratch_shapes=[
            pltpu.VMEM((tokens, 512), BF16),
            pltpu.VMEM((4, 4, 48, 128), BF16),
            pltpu.VMEM((48, 128), BF16),
            pltpu.VMEM((8, 128), F32),
            pltpu.VMEM((HD, SEQ), BF16), pltpu.VMEM((HD, SEQ), BF16),
            pltpu.VMEM((SEQ, HD), F32), pltpu.VMEM((SEQ, HD), F32),
            pltpu.VMEM((SEQ, HD), F32), pltpu.VMEM((SEQ, HD), F32),
            pltpu.VMEM((4, tokens, 256), BF16),
            pltpu.VMEM((tokens, 256), BF16), pltpu.VMEM((tokens, 256), BF16),
            pltpu.VMEM((2, tokens, 256), BF16),
            pltpu.VMEM((6, BLOCK_D, 256), BF16),
            pltpu.VMEM((2, 2, 3, SUB, BLOCK_D), BF16),
            pltpu.VMEM((2, 2, 3, SUB, BLOCK_D), BF16),
            pltpu.VMEM((2, SUB, BLOCK_D), BF16),
            pltpu.VMEM((4, SUB, BLOCK_D), BF16),
            pltpu.VMEM((4, SUB, BLOCK_D), BF16),
            pltpu.VMEM((4, 4, 48, 128), BF16),
            pltpu.VMEM((4, 48, 128), BF16), pltpu.VMEM((4, 48, 128), BF16),
            pltpu.VMEM((4, 48, 128), BF16),
            pltpu.VMEM((4, 4, 48, 128), BF16),
            pltpu.VMEM((48, tokens), BF16),
            pltpu.VMEM((48, 128), BF16),
            pltpu.VMEM((2, 32, 128), F32),
            pltpu.VMEM((2, 32, 128), F32),
            pltpu.VMEM((2, 16, 256), F32),
            pltpu.VMEM((4, 4, 48, 512), BF16),
            pltpu.VMEM((4, 4, 48, 512), BF16),
            pltpu.VMEM((4, 2, 48, 512), BF16), pltpu.VMEM((4, 2, 48, 512), BF16),
            pltpu.VMEM((2, 48, 512), F32),
            pltpu.VMEM((8, 128, 128), F32),
            pltpu.VMEM((8, 128, 128), F32),
            pltpu.VMEM((8, 128, 128), F32),
            pltpu.VMEM((16, 8, 128), F32),
            pltpu.VMEM(x.shape, BF16),
            pltpu.VMEM(down.shape, BF16),
            dma((5,)), dma((7,)), dma((7,)), dma((4, 3)), dma((4, 3)), dma((4, 4)), dma((4, 4)),
            dma((6, 8)), dma((6, 8)), dma((2, 4)), dma((2, 4)), dma((5, 4)), dma((5, 4)),
            dma((2,)), dma((8,)), dma((8,)), dma((8,)), dma((8,)),
            dma((16,)), dma((16,)), dma((2, 2, 4)), dma((2, 2, 4)), dma((4, 2, 2)), dma((4, 2, 2)),
        ],
        compiler_params=pltpu.CompilerParams(
            collective_id=0, has_side_effects=True, vmem_limit_bytes=63 * 1024 * 1024
        ),
        cost_estimate=pl.CostEstimate(
            flops=20_000_000_000, bytes_accessed=40_000_000, transcendentals=4_000_000
        ),
        name="exchange",
    )(tenant, docs, q, k, v, g, x, down, upq, upkv, cosine, sine, wq, wk, wv)


def per_device(
    x_rows, d_attn, q_saved, k_saved, v_saved, w_query, w_key, w_value, down_all, up_query, up_kv,
    tenant, doc_starts,
):
    return tuple(
        fused_call(
            tenant, doc_starts, q_saved, k_saved, v_saved, d_attn, x_rows, down_all, up_query,
            up_kv, w_query, w_key, w_value,
        )
    )


def solution(mesh):
    in_specs = (
        P(("dp", "tensor"), None),
        P("dp", "tensor"),
        P("dp", "tensor"),
        P("dp", "tensor"),
        P("dp", "tensor"),
        P(None, "tensor"),
        P(None, "tensor"),
        P(None, "tensor"),
        P(),
        P(None, None, "tensor"),
        P(None, None, "tensor"),
        P("dp"),
        P("dp", None),
    )
    out_specs = (
        P(("dp", "tensor"), None),
        P(None, None, "tensor"),
        P(None, None, "tensor"),
        P(None, None, "tensor"),
    )
    return jax.shard_map(
        per_device, mesh=mesh, in_specs=in_specs, out_specs=out_specs, check_vma=False
    )
```
